32 devices in a mesh: sp: 4 (over y, x), dp: 8 (over z, core).
Axes of the slice: x: 2, y: 2, z: 4, core: 2. Of those that a mesh axis runs over, the one named last changes fastest.
Arguments:
- tokens: bfloat16 [16, 1024, 1024], P('dp', 'sp'), may hold values from -6 to 6
- cotangent: bfloat16 [16, 1024, 1024], P('dp', 'sp'), may hold values from -6 to 6
- layer_norm_gain: float32 [2, 2, 1024], replicated, may hold values from 0.5 to 1.5
- layer_norm_bias: float32 [2, 2, 1024], replicated, may hold values from -1 to 1
- query_key_value_weight: bfloat16 [2, 1024, 3072], P(None, ('sp', 'dp')), may hold values from -0.1875 to 0.1875
- query_value_bias: float32 [2, 2, 1024], replicated, may hold values from -1.5 to 1.5
- attention_out_weight: bfloat16 [2, 1024, 1024], P(None, ('sp', 'dp')), may hold values from -0.75 to 0.75
- output_projection_bias: float32 [2, 2, 1024], replicated, may hold values from -1.5 to 1.5
- feed_up_weight: bfloat16 [2, 1024, 4096], P(None, ('sp', 'dp')), may hold values from -0.1875 to 0.1875
- feed_up_bias: float32 [2, 4096], replicated, may hold values from -1.5 to 1.5
- feed_down_weight: bfloat16 [2, 4096, 1024], P(None, ('sp', 'dp')), may hold values from -0.09375 to 0.09375
- adapter_down_maps: bfloat16 [2, 2, 1024, 4], replicated, may hold values from -0.1875 to 0.1875
- adapter_up_weights: bfloat16 [2, 2, 4, 1024], replicated, may hold values from -0.23925781 to 0.23925781
Outputs:
- layer_outputs: float32 [2, 16, 1024, 1024], P(None, 'dp', 'sp')
- grad_tokens: float32 [16, 1024, 1024], P('dp', 'sp')
- grad_lora_a: float32 [2, 2, 1024, 4], replicated
- grad_lora_b: float32 [2, 2, 4, 1024], replicated
The draws below stay inside these ranges and needn't reach their ends.
All inputs are finite; a program needn't handle non-finite values.
Results may differ from the reference program's by a relative error of at most 0.014.
Values may be sent and summed in bfloat16 or wider, within the bound.
No kernel may reach another device: no remote copies, remote signals or barrier semaphores. Data moves between devices by JAX's collectives and lax.ppermute only.
A program may use at most 384 MiB of HBM per device.

```python
import math
import jax
import jax.numpy as jnp
from jax import lax

MODEL_WIDTH = 1024
FF = 4096
HEAD = 64
ADAPTER_RANK = 4
LAYER_COUNT = 2
LENGTH = 1024
DOCS = 16


def block_levels(stream_key, shape, shards, low, high):
    level, own = 1.0, jax.random.fold_in(stream_key, 6)
    for dim, shards_of in shards:
        steps = jnp.exp(jax.random.uniform(jax.random.fold_in(own, dim), (shards_of,), jnp.float32, low / len(shards), high / len(shards)))
        level = level * jnp.repeat(steps, shape[dim] // shards_of).reshape([-1 if axis == dim else 1 for axis in range(len(shape))])
    return level


def gaussian(rng, shape, deviation, limit, shards=(), held_as=jnp.bfloat16):
    entries = jax.random.normal(rng, shape, jnp.float32) * deviation
    if len(shards) > 0:
        entries = block_levels(rng, shape, shards, -0.22, 0.18) * entries
    return jnp.clip(entries, min=-limit, max=limit).astype(held_as)


def setup_inputs(seed: int = 0) -> dict:
    splits = jax.random.split(jax.random.key(seed), 14)
    tokens = gaussian(splits[0], (DOCS, LENGTH, MODEL_WIDTH), 1.0, 6.0, ((0, 8), (1, 4)))
    cotangent = gaussian(splits[1], (DOCS, LENGTH, MODEL_WIDTH), 1.0, 6.0, ((0, 8), (1, 4)))
    layer_norm_gain = jnp.clip(1.0 + 0.1 * jax.random.normal(splits[2], (LAYER_COUNT, 2, MODEL_WIDTH), jnp.float32), 0.5, 1.5)
    layer_norm_bias = gaussian(splits[3], (LAYER_COUNT, 2, MODEL_WIDTH), 0.2, 1.0, (), jnp.float32)
    query_key_value_weight = gaussian(splits[4], (LAYER_COUNT, MODEL_WIDTH, 3 * MODEL_WIDTH), MODEL_WIDTH ** -0.5, 0.1875, ((1, 32),))
    query_value_bias = gaussian(splits[5], (LAYER_COUNT, 2, MODEL_WIDTH), 0.3, 1.5, (), jnp.float32)
    attention_out_weight = gaussian(splits[6], (LAYER_COUNT, MODEL_WIDTH, MODEL_WIDTH), (MODEL_WIDTH // 16) ** -0.5, 0.75, ((1, 32),))
    output_projection_bias = gaussian(splits[7], (LAYER_COUNT, 2, MODEL_WIDTH), 0.3, 1.5, (), jnp.float32)
    feed_up_weight = gaussian(splits[8], (LAYER_COUNT, MODEL_WIDTH, FF), MODEL_WIDTH ** -0.5, 0.1875, ((1, 32),))
    feed_up_bias = gaussian(splits[9], (LAYER_COUNT, FF), 0.3, 1.5, (), jnp.float32)
    feed_down_weight = gaussian(splits[10], (LAYER_COUNT, FF, MODEL_WIDTH), FF ** -0.5, 0.09375, ((1, 32),))
    adapter_down_maps = gaussian(splits[11], (LAYER_COUNT, 2, MODEL_WIDTH, ADAPTER_RANK), MODEL_WIDTH ** -0.5, 0.1875)
    adapter_up_weights = gaussian(splits[12], (LAYER_COUNT, 2, ADAPTER_RANK, MODEL_WIDTH), 0.04, 0.23925781)
    return {"tokens": tokens, "cotangent": cotangent, "layer_norm_gain": layer_norm_gain, "layer_norm_bias": layer_norm_bias, "query_key_value_weight": query_key_value_weight, "query_value_bias": query_value_bias, "attention_out_weight": attention_out_weight, "output_projection_bias": output_projection_bias, "feed_up_weight": feed_up_weight, "feed_up_bias": feed_up_bias, "feed_down_weight": feed_down_weight, "adapter_down_maps": adapter_down_maps, "adapter_up_weights": adapter_up_weights}


@jax.custom_vjp
def low_rank_rows(v):
    return lax.optimization_barrier(v.astype(jnp.bfloat16)).astype(jnp.float32)

@jax.custom_vjp
def low_rank_gradient(v):
    return v

def low_keep(v):
    return (low_rank_rows(v), None)

def low_pass(kept, grad):
    return (grad,)

def back_keep(v):
    return (v, None)

def back_low(kept, grad):
    return (low_rank_rows(grad),)
low_rank_rows.defvjp(low_keep, low_pass)
low_rank_gradient.defvjp(back_keep, back_low)
adapter_scale = 8.0

def norm(hidden_state, norm_gain, bias):
    center = hidden_state - lax.optimization_barrier(jnp.mean(hidden_state, axis=-1, keepdims=True))
    spread = lax.optimization_barrier(jnp.mean(center * center, axis=-1, keepdims=True))
    return center * lax.rsqrt(spread + 1e-05) * norm_gain + bias

def matrix_product(left, right):
    return jnp.einsum('...d,de->...e', left, right, precision=lax.Precision.HIGHEST)

def attention(query_rows, keys, value_rows):
    group, length, model_size = query_rows.shape
    heads = model_size // HEAD
    q4 = query_rows.reshape(group, length, heads, HEAD)
    k4 = keys.reshape(group, length, heads, HEAD)
    v4 = value_rows.reshape(group, length, heads, HEAD)
    scores = low_rank_gradient(jnp.einsum('gqhe,gkhe->ghqk', q4, k4, precision=lax.Precision.HIGHEST) * 0.125)
    rows = lax.broadcasted_iota(jnp.int32, (length, length), 0)
    cols = lax.broadcasted_iota(jnp.int32, (length, length), 1)
    scores = jnp.where(cols <= rows, scores, -1e+30)
    top = lax.optimization_barrier(jnp.max(scores, axis=-1, keepdims=True))
    weights = jnp.exp(scores - top)
    probs = low_rank_rows(weights / lax.optimization_barrier(jnp.sum(weights, axis=-1, keepdims=True)))
    mixed = jnp.einsum('ghqk,gkhe->gqhe', probs, v4, precision=lax.Precision.HIGHEST)
    return mixed.reshape(group, length, model_size)

def single_layer(hidden_state, norm_gain, norm_shift, joint_projection_weight, frozen_query_value_bias, out_weight, projection_bias, up_weight, hidden_bias, down_weight, adapter_down, adapter_up_maps):
    model_size = hidden_state.shape[-1]
    adapter_width = adapter_down.shape[-1]
    normed = low_rank_rows(norm(hidden_state, norm_gain[0], norm_shift[0]))
    base_output = matrix_product(normed, joint_projection_weight)
    inner_hidden = low_rank_rows(low_rank_gradient(matrix_product(normed, jnp.concatenate([adapter_down[0], adapter_down[1]], axis=1))))
    query_rows = low_rank_rows(low_rank_gradient(base_output[..., :model_size] + frozen_query_value_bias[0] + adapter_scale * matrix_product(inner_hidden[..., :adapter_width], adapter_up_maps[0])))
    keys = low_rank_rows(low_rank_gradient(base_output[..., model_size:2 * model_size]))
    value_rows = low_rank_rows(low_rank_gradient(base_output[..., 2 * model_size:] + frozen_query_value_bias[1] + adapter_scale * matrix_product(inner_hidden[..., adapter_width:], adapter_up_maps[1])))
    mixed = low_rank_rows(low_rank_gradient(attention(query_rows, keys, value_rows)))
    middle = hidden_state + low_rank_gradient(matrix_product(mixed, out_weight) + projection_bias[0])
    second = low_rank_rows(norm(middle, norm_gain[1], norm_shift[1]))
    pre = low_rank_gradient(matrix_product(second, up_weight) + hidden_bias)
    acted = low_rank_rows(jax.nn.gelu(pre, approximate=True))
    return middle + low_rank_gradient(matrix_product(acted, down_weight) + projection_bias[1])

def reference(tokens, cotangent, layer_norm_gain, layer_norm_bias, query_key_value_weight, query_value_bias, attention_out_weight, output_projection_bias, feed_up_weight, feed_up_bias, feed_down_weight, adapter_down_maps, adapter_up_weights):
    single_float = jnp.float32
    joint_projection_weight = query_key_value_weight.astype(single_float)
    out_weight = attention_out_weight.astype(single_float)
    up_weight = feed_up_weight.astype(single_float)
    down_weight = feed_down_weight.astype(single_float)
    adapter_down = adapter_down_maps.astype(single_float)
    adapter_up_maps = adapter_up_weights.astype(single_float)
    group = math.gcd(DOCS, max(1, 4096 // LENGTH))
    steps_count = DOCS // group
    inputs = tokens.astype(single_float).reshape(steps_count, group, LENGTH, MODEL_WIDTH)
    grads_in = cotangent.astype(single_float).reshape(steps_count, group, LENGTH, MODEL_WIDTH)

    def run_model(hidden, adn, bupl):
        outs_list = []
        for layer_index in range(LAYER_COUNT):
            hidden = single_layer(hidden, layer_norm_gain[layer_index], layer_norm_bias[layer_index], joint_projection_weight[layer_index], query_value_bias[layer_index], out_weight[layer_index], output_projection_bias[layer_index], up_weight[layer_index], feed_up_bias[layer_index], down_weight[layer_index], adn[layer_index], bupl[layer_index])
            outs_list.append(hidden)
        return jnp.stack(outs_list)

    def step(carry, item):
        block_input, block_grad = item
        stacked_layers, pullback = jax.vjp(run_model, block_input, adapter_down, adapter_up_maps)
        pull_in = jnp.concatenate([jnp.zeros_like(stacked_layers[:-1]), block_grad[None]], axis=0)
        grad_x, grad_a, grad_b = pullback(pull_in)
        return ((carry[0] + grad_a, carry[1] + grad_b), (stacked_layers, grad_x))
    initialize = (jnp.zeros(adapter_down_maps.shape, single_float), jnp.zeros(adapter_up_weights.shape, single_float))
    (grad_a, grad_b), (stacked_layers, grad_x) = lax.scan(step, initialize, (inputs, grads_in))
    layer_outputs = jnp.transpose(stacked_layers, (1, 0, 2, 3, 4)).reshape(LAYER_COUNT, DOCS, LENGTH, MODEL_WIDTH)
    return (layer_outputs, grad_x.reshape(DOCS, LENGTH, MODEL_WIDTH), grad_a, grad_b)
```

```python
import functools
import jax
import jax.numpy as jnp
from jax import lax
from jax.experimental import pallas as pl
from jax.experimental.pallas import tpu as pltpu
from jax.sharding import PartitionSpec as P

HEAD = 64
LANES = 128
adapter_scale = 8.0
VMEM_BYTES = 58 * 1024 * 1024
low = jnp.bfloat16
full = jnp.float32


def dot(left, right):
    return jnp.dot(left, right, preferred_element_type=full)


def dot_nt(left, right):
    return lax.dot_general(left, right, (((1,), (1,)), ((), ())), preferred_element_type=full)


def dot_tn(left, right):
    return lax.dot_general(left, right, (((0,), (0,)), ((), ())), preferred_element_type=full)


def normalise(value):
    center = value - jnp.mean(value, axis=-1, keepdims=True)
    scale = lax.rsqrt(jnp.mean(center * center, axis=-1, keepdims=True) + 1e-05)
    return center * scale, scale


def norm_back(unit, scale, gain, grad):
    grad = grad * gain
    inner = jnp.mean(grad * unit, axis=-1, keepdims=True)
    return scale * (grad - jnp.mean(grad, axis=-1, keepdims=True) - unit * inner)


def vmem():
    return pl.BlockSpec(memory_space=pltpu.VMEM)


def hbm():
    return pl.BlockSpec(memory_space=pl.ANY)


def smem():
    return pl.BlockSpec(memory_space=pltpu.SMEM)


def params():
    return pltpu.CompilerParams(vmem_limit_bytes=VMEM_BYTES)


class Loads:
    def __init__(self, pieces, column, offsets, first, target, sems, parts):
        self.copies = []
        width = target.shape[1] // parts
        for part in range(parts):
            cols = pl.ds(part * width, width)
            source = pl.ds(column + part * width, width)
            row = []
            for index, piece in enumerate(pieces):
                start = pl.multiple_of(offsets[first + index], 16)
                row.append(
                    pltpu.make_async_copy(
                        piece.at[:, source],
                        target.at[pl.ds(start, piece.shape[0]), cols],
                        sems.at[index, part],
                    )
                )
            self.copies.append(row)

    def start(self):
        for row in self.copies:
            for copy in row:
                copy.start()

    def wait(self, part):
        for copy in self.copies[part]:
            copy.wait()


def total_rows(pieces):
    return sum(piece.shape[0] for piece in pieces)


def project_kernel(count, column, groups, offs, h_ref, gain, shift, bias, down, up, *rest):
    pieces, rest = rest[:count], rest[count:]
    outs, (u_ref, a_ref), (weight, sems) = rest[:groups], rest[groups : groups + 2], rest[groups + 2 :]
    parts = 3 * groups
    loads = Loads(pieces, column, offs, 1, weight, sems, parts)
    loads.start()
    member = offs[0]
    model = h_ref.shape[1]
    width = model // groups
    unit, _ = normalise(h_ref[...].astype(full))
    a = (unit * gain[...] + shift[...]).astype(low)
    a_ref[...] = a
    u = dot(a, down[...]).astype(low)
    u_ref[...] = u
    for part in range(parts):
        kind, group = part // groups, part % groups
        loads.wait(part)
        cols = pl.ds(part * width, width)
        value = dot(a, weight[:, cols])
        if kind != 1:
            at = pl.ds((kind // 2) * model + group * width, width)
            value = value + bias[:, at] + dot(u, up[:, at])
        value = value.astype(low)
        for step in range(groups):

            @pl.when(member == (group ^ step))
            def _():
                outs[step][:, pl.ds(kind * width, width)] = value


def project(offs, hidden, gain, shift, bias, down, up, pieces, groups):
    tokens, model = hidden.shape
    width = 3 * model // groups
    outs = [jax.ShapeDtypeStruct((tokens, width), low)] * groups
    outs += [jax.ShapeDtypeStruct((tokens, LANES), low), jax.ShapeDtypeStruct((tokens, model), low)]
    pieces, column = pieces
    count = len(pieces)
    flops = 2 * tokens * model * 3 * model
    result = pl.pallas_call(
        functools.partial(project_kernel, count, column, groups),
        out_shape=outs,
        in_specs=[smem()] + [vmem()] * 6 + [hbm()] * count,
        out_specs=[vmem()] * len(outs),
        scratch_shapes=[
            pltpu.VMEM((model, 3 * model), low),
            pltpu.SemaphoreType.DMA((count, 3 * groups)),
        ],
        compiler_params=params(),
        cost_estimate=pl.CostEstimate(
            flops=flops, bytes_accessed=2 * model * 3 * model + 10 * tokens * model, transcendentals=0
        ),
        name="project",
    )(offs, hidden, gain, shift, bias, down, up, *pieces)
    return result[:groups], result[groups], result[groups + 1]


def attend_kernel(groups, offs, *rest):
    pieces, rest = rest[:groups], rest[groups:]
    outs, (o_ref, lse_ref), (qkv, lse_cols, sems) = rest[:groups], rest[groups : groups + 2], rest[groups + 2 :]
    member = offs[0]
    count, width3 = pieces[0].shape
    width = width3 // 3
    length = count * groups
    pairs = width // LANES
    block = 256
    loads = []
    for step in range(groups):
        rows = pl.ds(pl.multiple_of((member ^ step) * count, count), count)
        copy = pltpu.make_async_copy(pieces[step], qkv.at[rows, :], sems.at[step])
        copy.start()
        loads.append(copy)
    for copy in loads:
        copy.wait()
    lane = lax.broadcasted_iota(jnp.int32, (1, LANES), 1)
    keep = [(lane < HEAD).astype(low), (lane >= HEAD).astype(low)]
    causal = lax.broadcasted_iota(jnp.int32, (block, block), 1) <= lax.broadcasted_iota(
        jnp.int32, (block, block), 0
    )
    lse_cols[...] = jnp.zeros_like(lse_cols)

    @pl.loop(0, pairs)
    def _(pair):
        at = pl.multiple_of(pair * LANES, LANES)
        for start in range(0, length, block):
            rows = pl.ds(start, block)
            q = qkv[rows, pl.ds(at, LANES)]
            k = qkv[pl.ds(0, start + block), pl.ds(width + at, LANES)]
            v = qkv[pl.ds(0, start + block), pl.ds(2 * width + at, LANES)]
            mixed = jnp.zeros((block, LANES), full)
            logs = lse_cols[rows, :]
            for head in range(2):
                scores = dot_nt(q * (keep[head] * 0.125), k)
                corner = jnp.where(causal, scores[:, start:], -1e30)
                if start:
                    scores = jnp.concatenate([scores[:, :start], corner], axis=1)
                else:
                    scores = corner
                top = jnp.max(scores, axis=1, keepdims=True)
                weights = jnp.exp(scores - top)
                total = jnp.sum(weights, axis=1, keepdims=True)
                part = dot(weights.astype(low), v * keep[head])
                mixed = mixed + part * (1.0 / total)
                logs = jnp.where(lane == 2 * pair + head, top + jnp.log(total), logs)
            lse_cols[rows, :] = logs
            o_ref[rows, pl.ds(at, LANES)] = mixed.astype(low)

    lse_ref[...] = lse_cols[...].T
    for step in range(groups):
        rows = pl.ds(pl.multiple_of((member ^ step) * count, count), count)
        outs[step][...] = o_ref[rows, :]


def attend(offs, pieces):
    groups = len(pieces)
    count, width3 = pieces[0].shape
    width, length = width3 // 3, count * groups
    outs = [jax.ShapeDtypeStruct((count, width), low)] * groups
    outs += [jax.ShapeDtypeStruct((length, width), low), jax.ShapeDtypeStruct((LANES, length), full)]
    result = pl.pallas_call(
        functools.partial(attend_kernel, groups),
        out_shape=outs,
        in_specs=[smem()] + [hbm()] * groups,
        out_specs=[vmem()] * len(outs),
        scratch_shapes=[
            pltpu.VMEM((length, width3), low),
            pltpu.VMEM((length, LANES), full),
            pltpu.SemaphoreType.DMA((groups,)),
        ],
        compiler_params=params(),
        cost_estimate=pl.CostEstimate(
            flops=8 * length * length * width, bytes_accessed=10 * length * width, transcendentals=length * length * width // HEAD
        ),
        name="attend",
    )(offs, *pieces)
    return result[:groups], result[groups], result[groups + 1]


def attend_back_kernel(groups, offs, *rest):
    pieces, grads, rest = rest[:groups], rest[groups : 2 * groups], rest[2 * groups :]
    (o_ref, lse_ref), rest = rest[:2], rest[2:]
    outs, (qkv, d_out, result, inner, sems) = rest[:groups], rest[groups:]
    member = offs[0]
    count, width3 = pieces[0].shape
    width = width3 // 3
    length = count * groups
    pairs = width // LANES
    block = 256
    loads = []
    for step in range(groups):
        rows = pl.ds(pl.multiple_of((member ^ step) * count, count), count)
        for kind, (source, target) in enumerate(((pieces[step], qkv), (grads[step], d_out))):
            copy = pltpu.make_async_copy(source, target.at[rows, :], sems.at[kind, step])
            copy.start()
            loads.append(copy)
    for copy in loads:
        copy.wait()
    lane = lax.broadcasted_iota(jnp.int32, (1, LANES), 1)
    keep = [(lane < HEAD).astype(low), (lane >= HEAD).astype(low)]
    causal = lax.broadcasted_iota(jnp.int32, (block, block), 0) <= lax.broadcasted_iota(
        jnp.int32, (block, block), 1
    )
    heads = width // HEAD
    of_head = (
        lax.broadcasted_iota(jnp.int32, (max(heads, 8), width), 1) // HEAD
        == lax.broadcasted_iota(jnp.int32, (max(heads, 8), width), 0)
    ).astype(low)
    product = d_out[...].astype(full) * o_ref[...].astype(full)
    high = product.astype(low)
    rest_of = (product - high.astype(full)).astype(low)
    inner[...] = dot_nt(of_head, high) + dot_nt(of_head, rest_of)

    @pl.loop(0, pairs)
    def _(pair):
        at = pl.multiple_of(pair * LANES, LANES)
        grad_k = jnp.zeros((length, LANES), full)
        grad_v = jnp.zeros((length, LANES), full)
        for start in reversed(range(0, length, block)):
            rows = pl.ds(start, block)
            upto = start + block
            q = qkv[rows, pl.ds(at, LANES)]
            d = d_out[rows, pl.ds(at, LANES)]
            k = qkv[pl.ds(0, upto), pl.ds(width + at, LANES)]
            v = qkv[pl.ds(0, upto), pl.ds(2 * width + at, LANES)]
            grad_q = jnp.zeros((block, LANES), full)
            for head in range(2):
                q_head = q * (keep[head] * 0.125)
                d_head = d * keep[head]
                scores = dot_nt(k, q_head)
                log_sum = lse_ref[pl.ds(2 * pair + head, 1), rows]
                probs = jnp.exp(scores - log_sum)
                corner = jnp.where(causal, probs[start:], 0.0)
                probs = jnp.concatenate([probs[:start], corner], axis=0) if start else corner
                d_probs = dot_nt(v, d_head)
                d_scores = (probs * (d_probs - inner[pl.ds(2 * pair + head, 1), rows])).astype(low)
                more_v = dot(probs.astype(low), d_head)
                more_k = dot(d_scores, q_head)
                if upto < length:
                    zeros = jnp.zeros((length - upto, LANES), full)
                    more_v = jnp.concatenate([more_v, zeros], axis=0)
                    more_k = jnp.concatenate([more_k, zeros], axis=0)
                grad_v = grad_v + more_v
                grad_k = grad_k + more_k
                grad_q = grad_q + dot_tn(d_scores, k * (keep[head] * 0.125))
            result[rows, pl.ds(at, LANES)] = grad_q.astype(low)
        result[:, pl.ds(width + at, LANES)] = grad_k.astype(low)
        result[:, pl.ds(2 * width + at, LANES)] = grad_v.astype(low)

    for step in range(groups):
        rows = pl.ds(pl.multiple_of((member ^ step) * count, count), count)
        outs[step][...] = result[rows, :]


def attend_back(offs, pieces, grads, mixed, lse):
    groups = len(pieces)
    count, width3 = pieces[0].shape
    width, length = width3 // 3, count * groups
    outs = [jax.ShapeDtypeStruct((count, width3), low)] * groups
    return pl.pallas_call(
        functools.partial(attend_back_kernel, groups),
        out_shape=outs,
        in_specs=[smem()] + [hbm()] * (2 * groups) + [vmem()] * 2,
        out_specs=[vmem()] * len(outs),
        scratch_shapes=[
            pltpu.VMEM((length, width3), low),
            pltpu.VMEM((length, width), low),
            pltpu.VMEM((length, width3), low),
            pltpu.VMEM((max(width // HEAD, 8), length), full),
            pltpu.SemaphoreType.DMA((2, groups)),
        ],
        compiler_params=params(),
        cost_estimate=pl.CostEstimate(
            flops=20 * length * length * width, bytes_accessed=16 * length * width, transcendentals=length * length * width // HEAD
        ),
        name="attend_back",
    )(offs, *pieces, *grads, mixed, lse)


def mix_kernel(count, column, groups, offs, h_ref, bias, gain, shift, *rest):
    mixed, pieces, rest = rest[:groups], rest[groups : groups + count], rest[groups + count :]
    m_ref, c_ref, weight, sems = rest
    loads = Loads(pieces, column, offs, 1, weight, sems, 1)
    loads.start()
    loads.wait(0)
    width = mixed[0].shape[1]
    total = h_ref[...].astype(full) + bias[...]
    for step in range(groups):
        rows = pl.ds(pl.multiple_of((offs[0] ^ step) * width, width), width)
        total = total + dot(mixed[step][...], weight[rows, :])
    m_ref[...] = total
    unit, _ = normalise(total)
    c_ref[...] = (unit * gain[...] + shift[...]).astype(low)


def mix(offs, hidden, bias, gain, shift, mixed, pieces):
    pieces, column = pieces
    groups, count = len(mixed), len(pieces)
    tokens, model = hidden.shape
    return pl.pallas_call(
        functools.partial(mix_kernel, count, column, groups),
        out_shape=[jax.ShapeDtypeStruct((tokens, model), full), jax.ShapeDtypeStruct((tokens, model), low)],
        in_specs=[smem()] + [vmem()] * (4 + groups) + [hbm()] * count,
        out_specs=[vmem()] * 2,
        scratch_shapes=[pltpu.VMEM((model, model), low), pltpu.SemaphoreType.DMA((count, 1))],
        compiler_params=params(),
        cost_estimate=pl.CostEstimate(
            flops=2 * tokens * model * model, bytes_accessed=2 * model * model + 12 * tokens * model, transcendentals=0
        ),
        name="mix",
    )(offs, hidden, bias, gain, shift, *mixed, *pieces)


ROOT = 0.7978845608028654
CUBE = 0.044715


def feed_kernel(ups, downs, columns, parts, offs, c_ref, m_ref, up_bias, down_bias, *rest):
    up_pieces, down_pieces, rest = rest[:ups], rest[ups : ups + downs], rest[ups + downs :]
    h_ref, low_ref, slope_ref, up, down, acted, up_sems, down_sems = rest
    up_loads = Loads(up_pieces, columns[0], offs, 0, up, up_sems, parts)
    down_loads = Loads(down_pieces, columns[1], offs, ups, down, down_sems, 1)
    up_loads.start()
    down_loads.start()
    width = up.shape[1] // parts
    c = c_ref[...]
    for part in range(parts):
        cols = pl.ds(part * width, width)
        up_loads.wait(part)
        z = dot(c, up[:, cols]) + up_bias[:, cols]
        square = z * z
        t = jnp.tanh(ROOT * z * (1.0 + CUBE * square))
        half = 0.5 * (1.0 + t)
        acted[:, cols] = (z * half).astype(low)
        slope_ref[:, cols] = (
            half + z * (0.5 * ROOT) * (1.0 - t * t) * (1.0 + 3.0 * CUBE * square)
        ).astype(low)
    down_loads.wait(0)
    model = c_ref.shape[1]
    step = 256
    for start in range(0, model, step):
        cols = pl.ds(start, step)
        after = m_ref[:, cols] + (dot(acted[...], down[:, cols]) + down_bias[:, cols])
        h_ref[:, cols] = after
        low_ref[:, cols] = after.astype(low)


def feed(offs, second, middle, up_bias, down_bias, up_pieces, down_pieces):
    tokens, model = middle.shape
    hidden = up_bias.shape[1]
    (up_pieces, up_column), (down_pieces, down_column) = up_pieces, down_pieces
    ups, downs = len(up_pieces), len(down_pieces)
    parts = 8
    return pl.pallas_call(
        functools.partial(feed_kernel, ups, downs, (up_column, down_column), parts),
        out_shape=[
            jax.ShapeDtypeStruct((tokens, model), full),
            jax.ShapeDtypeStruct((tokens, model), low),
            jax.ShapeDtypeStruct((tokens, hidden), low),
        ],
        in_specs=[smem()] + [vmem()] * 4 + [hbm()] * (ups + downs),
        out_specs=[vmem()] * 3,
        scratch_shapes=[
            pltpu.VMEM((model, hidden), low),
            pltpu.VMEM((hidden, model), low),
            pltpu.VMEM((tokens, hidden), low),
            pltpu.SemaphoreType.DMA((ups, parts)),
            pltpu.SemaphoreType.DMA((downs, 1)),
        ],
        compiler_params=params(),
        cost_estimate=pl.CostEstimate(
            flops=4 * tokens * model * hidden, bytes_accessed=4 * model * hidden + 4 * tokens * hidden, transcendentals=tokens * hidden
        ),
        name="feed",
    )(offs, second, middle, up_bias, down_bias, *up_pieces, *down_pieces)


def feed_back_kernel(ups, downs, outs_count, columns, groups, parts, offs, g_ref, m_ref, slope_ref, gain, *rest):
    up_pieces, rest = rest[:ups], rest[ups:]
    down_pieces, rest = rest[:downs], rest[downs:]
    out_pieces, rest = rest[:outs_count], rest[outs_count:]
    mid_ref, rest = rest[0], rest[1:]
    outs, rest = rest[:groups], rest[groups:]
    up, down, out, d_pre, d_second, up_sems, down_sems, out_sems = rest
    down_loads = Loads(down_pieces, columns[1], offs, 1 + ups, down, down_sems, 1)
    up_loads = Loads(up_pieces, columns[0], offs, 1, up, up_sems, 1)
    out_loads = Loads(out_pieces, columns[2], offs, 1 + ups + downs, out, out_sems, 1)
    down_loads.start()
    up_loads.start()
    out_loads.start()
    hidden = down.shape[0]
    model = up.shape[0]
    width = hidden // parts
    g = g_ref[...].astype(low)
    down_loads.wait(0)
    for part in range(parts):
        cols = pl.ds(part * width, width)
        d_acted = dot_nt(g, down[cols, :])
        d_pre[:, cols] = (d_acted * slope_ref[:, cols].astype(full)).astype(low)
    up_loads.wait(0)
    step = 256
    for start in range(0, model, step):
        cols = pl.ds(start, step)
        d_second[:, cols] = dot_nt(d_pre[...], up[cols, :])
    unit, scale = normalise(m_ref[...])
    grad = g_ref[...].astype(full) + norm_back(unit, scale, gain[...], d_second[...])
    mid_ref[...] = grad
    grad = grad.astype(low)
    out_loads.wait(0)
    width = model // groups
    for group in range(groups):
        value = dot_nt(grad, out[pl.ds(group * width, width), :]).astype(low)
        for step in range(groups):

            @pl.when(offs[0] == (group ^ step))
            def _():
                outs[step][...] = value


def feed_back(offs, grad, middle, slope, gain, up_pieces, down_pieces, out_pieces, groups):
    tokens, model = middle.shape
    hidden = slope.shape[1]
    (up_pieces, up_column), (down_pieces, down_column) = up_pieces, down_pieces
    out_pieces, out_column = out_pieces
    columns = (up_column, down_column, out_column)
    ups, downs, outs_count = len(up_pieces), len(down_pieces), len(out_pieces)
    parts = 8
    result = pl.pallas_call(
        functools.partial(feed_back_kernel, ups, downs, outs_count, columns, groups, parts),
        out_shape=[jax.ShapeDtypeStruct((tokens, model), full)]
        + [jax.ShapeDtypeStruct((tokens, model // groups), low)] * groups,
        in_specs=[smem()] + [vmem()] * 4 + [hbm()] * (ups + downs + outs_count),
        out_specs=[vmem()] * (1 + groups),
        scratch_shapes=[
            pltpu.VMEM((model, hidden), low),
            pltpu.VMEM((hidden, model), low),
            pltpu.VMEM((model, model), low),
            pltpu.VMEM((tokens, hidden), low),
            pltpu.VMEM((tokens, model), full),
            pltpu.SemaphoreType.DMA((ups, 1)),
            pltpu.SemaphoreType.DMA((downs, 1)),
            pltpu.SemaphoreType.DMA((outs_count, 1)),
        ],
        compiler_params=params(),
        cost_estimate=pl.CostEstimate(
            flops=4 * tokens * model * hidden + 2 * tokens * model * model,
            bytes_accessed=4 * model * hidden + 4 * tokens * hidden,
            transcendentals=0,
        ),
        name="feed_back",
    )(offs, grad, middle, slope, gain, *up_pieces, *down_pieces, *out_pieces)
    return result[0], result[1:]


def project_back_kernel(count, column, groups, offs, mid_ref, h_ref, gain, a_ref, u_ref, down, up, *rest):
    grads, pieces, rest = rest[:groups], rest[groups : groups + count], rest[groups + count :]
    g_ref, low_ref, grad_a, grad_b, weight, d_all, d_normed, sems = rest
    loads = Loads(pieces, column, offs, 1, weight, sems, 1)
    loads.start()
    model = h_ref.shape[1]
    width = model // groups
    for step in range(groups):
        for kind in range(3):
            at = pl.multiple_of(kind * model + (offs[0] ^ step) * width, width)
            d_all[:, pl.ds(at, width)] = grads[step][:, pl.ds(kind * width, width)]
    d_query = d_all[:, pl.ds(0, model)]
    d_value = d_all[:, pl.ds(2 * model, model)]
    u = u_ref[...]
    lane = lax.broadcasted_iota(jnp.int32, (1, LANES), 1)
    half = 4
    u_query = jnp.where(lane < half, u, 0).astype(low)
    u_value = jnp.where(lane >= half, u, 0).astype(low)
    by_rank = dot_tn(u_query, d_query) + dot_tn(u_value, d_value)
    grad_b[...] = adapter_scale * by_rank[:8]
    d_inner = (
        dot_nt(d_query, up[:, pl.ds(0, model)]) + dot_nt(d_value, up[:, pl.ds(model, model)])
    ).astype(low)
    grad_a[...] = dot_tn(d_inner, a_ref[...])[:8]
    loads.wait(0)
    step = 256
    for start in range(0, model, step):
        rows = pl.ds(start, step)
        d_normed[:, rows] = dot_nt(d_all[...], weight[rows, :]) + dot_nt(d_inner, down[rows, :])
    unit, scale = normalise(h_ref[...].astype(full))
    grad = mid_ref[...] + norm_back(unit, scale, gain[...], d_normed[...])
    g_ref[...] = grad
    low_ref[...] = grad.astype(low)


def project_back(offs, mid, hidden, gain, normed, inner, down, up, grads, pieces):
    pieces, column = pieces
    groups, count = len(grads), len(pieces)
    tokens, model = hidden.shape
    return pl.pallas_call(
        functools.partial(project_back_kernel, count, column, groups),
        out_shape=[
            jax.ShapeDtypeStruct((tokens, model), full),
            jax.ShapeDtypeStruct((tokens, model), low),
            jax.ShapeDtypeStruct((8, model), full),
            jax.ShapeDtypeStruct((8, model), full),
        ],
        in_specs=[smem()] + [vmem()] * (7 + groups) + [hbm()] * count,
        out_specs=[vmem()] * 4,
        scratch_shapes=[
            pltpu.VMEM((model, 3 * model), low),
            pltpu.VMEM((tokens, 3 * model), low),
            pltpu.VMEM((tokens, model), full),
            pltpu.SemaphoreType.DMA((count, 1)),
        ],
        compiler_params=params(),
        cost_estimate=pl.CostEstimate(
            flops=2 * tokens * model * 3 * model, bytes_accessed=6 * model * model + 24 * tokens * model, transcendentals=0
        ),
        name="project_back",
    )(offs, mid, hidden, gain, normed, inner, down, up, *grads, *pieces)

def reshard_perms(sp_size, dp_size):
    quarter = sp_size // 4
    perms = []
    for part in range(2):
        perm = []
        for s in range(sp_size):
            for d in range(dp_size):
                doc = 2 * (d & 1) + ((s & 1) ^ part)
                member = s >> 1
                target_sp = doc * quarter + (member >> 1)
                target_dp = 2 * (d >> 1) + (member & 1)
                perm.append((s * dp_size + d, target_sp * dp_size + target_dp))
        perms.append(perm)
    return perms


def member_perm(sp_size, dp_size, step):
    quarter = sp_size // 4
    perm = []
    for s in range(sp_size):
        for d in range(dp_size):
            doc, high = s // quarter, s % quarter
            member = (2 * high + (d & 1)) ^ step
            target_sp = doc * quarter + (member >> 1)
            target_dp = 2 * (d >> 1) + (member & 1)
            perm.append((s * dp_size + d, target_sp * dp_size + target_dp))
    return perm


class Plan:
    def __init__(self, sp_size, dp_size):
        self.sp_size, self.dp_size = sp_size, dp_size
        self.members = sp_size // 2
        self.perms = reshard_perms(sp_size, dp_size)
        self.back = [[(b, a) for a, b in perm] for perm in self.perms]
        self.s = lax.axis_index("sp")
        self.d = lax.axis_index("dp")
        quarter = sp_size // 4
        self.doc = self.s // quarter
        self.member = 2 * (self.s % quarter) + (self.d & 1)

    def gather_doc(self, blocks):
        odd = self.s & 1
        got = []
        for part in range(2):
            block = lax.dynamic_index_in_dim(blocks, odd ^ part, 0, keepdims=False)
            got.append(lax.ppermute(block, ("sp", "dp"), self.perms[part]))
        flip = (self.doc & 1) == 1
        first = jnp.where(flip, got[1], got[0])
        second = jnp.where(flip, got[0], got[1])
        return jnp.concatenate([first, second], axis=0)

    def scatter_doc(self, rows):
        half = rows.shape[0] // 2
        blocks = rows.reshape(2, half, rows.shape[1])
        got = []
        for part in range(2):
            block = lax.dynamic_index_in_dim(blocks, (self.doc & 1) ^ part, 0, keepdims=False)
            got.append(lax.ppermute(block, ("sp", "dp"), self.back[part]))
        flip = (self.s & 1) == 1
        first = jnp.where(flip, got[1], got[0])
        second = jnp.where(flip, got[0], got[1])
        return jnp.stack([first, second])

    def swap(self, parts):
        out = [parts[0]]
        for step in range(1, self.members):
            perm = member_perm(self.sp_size, self.dp_size, step)
            out.append(lax.ppermute(parts[step], ("sp", "dp"), perm))
        return out


def all_sum(value, sp_size, dp_size):
    total = sp_size * dp_size
    step = 1
    while step < total:
        value = value + lax.ppermute(
            value, ("sp", "dp"), [(i, i ^ step) for i in range(total)]
        )
        step *= 2
    return value


def fetch(plan, shard):
    if plan.sp_size != 4:
        return [lax.all_gather(shard, ("sp", "dp"), axis=0, tiled=True)], [0]
    block = lax.all_gather(shard, "dp", axis=0, tiled=True)
    rows = block.shape[0]
    half, quarter = rows // 2, rows // 4
    s, core = plan.s, plan.d & 1
    mine = lax.dynamic_slice_in_dim(block, core * half, half, axis=0)
    over_x = [(i, i ^ 1) for i in range(4)]
    over_y = [(i, i ^ 2) for i in range(4)]
    over_core = [(i, i ^ 1) for i in range(plan.dp_size)]
    from_x = lax.ppermute(mine, "sp", over_x)
    from_y = lax.ppermute(mine, "sp", over_y)
    far_first = lax.ppermute(from_y[:quarter], "sp", over_x)
    far_second = lax.ppermute(from_x[quarter:], "sp", over_y)
    got = [from_x, from_y, far_first, far_second]
    got += [lax.ppermute(piece, "dp", over_core) for piece in got]
    starts = []
    for near in (core, 1 - core):
        base = near * half
        starts += [(s ^ 1) * rows + base, (s ^ 2) * rows + base]
        starts += [(s ^ 3) * rows + base, (s ^ 3) * rows + base + quarter]
    return [block] + got, [s * rows] + starts


def on_device(
    tokens,
    cotangent,
    layer_norm_gain,
    layer_norm_bias,
    query_key_value_weight,
    query_value_bias,
    attention_out_weight,
    output_projection_bias,
    feed_up_weight,
    feed_up_bias,
    feed_down_weight,
    adapter_down_maps,
    adapter_up_weights,
):
    layers = query_key_value_weight.shape[0]
    model = tokens.shape[2]
    rank = adapter_down_maps.shape[3]
    plan = Plan(lax.axis_size("sp"), lax.axis_size("dp"))
    groups = plan.members
    member = plan.member.astype(jnp.int32)

    def table(*entries):
        return jnp.stack([jnp.asarray(entry, jnp.int32) for entry in entries])

    weights = []
    for layer in range(layers):
        if layer == 0:
            joined = [
                query_key_value_weight[layer],
                jnp.concatenate([attention_out_weight[layer], feed_up_weight[layer]], axis=1),
            ]
        else:
            joined = [
                jnp.concatenate(
                    [query_key_value_weight[layer], attention_out_weight[layer], feed_up_weight[layer]],
                    axis=1,
                )
            ]
        got = [fetch(plan, shard) for shard in joined]
        down, starts_down = fetch(plan, feed_down_weight[layer])
        starts = got[0][1]
        if layer == 0:
            qkv, out, up = (got[0][0], 0), (got[1][0], 0), (got[1][0], model)
        else:
            qkv, out, up = (got[0][0], 0), (got[0][0], 3 * model), (got[0][0], 4 * model)
        weights.append((qkv, out, up, (down, 0), starts, starts_down))

    adapters = []
    for layer in range(layers):
        down = jnp.concatenate([adapter_down_maps[layer, 0], adapter_down_maps[layer, 1]], axis=1)
        down = jnp.pad(down, ((0, 0), (0, LANES - 2 * rank)))
        up = adapter_up_weights[layer] * jnp.asarray(adapter_scale, low)
        up = jnp.concatenate(
            [
                jnp.pad(up[0], ((0, LANES - rank), (0, 0))),
                jnp.pad(up[1], ((rank, LANES - 2 * rank), (0, 0))),
            ],
            axis=1,
        )
        adapters.append((down, up))

    hidden = plan.gather_doc(tokens)
    grad = plan.gather_doc(cotangent)
    saved, outputs = [], []
    for layer in range(layers):
        qkv_w, out_w, up_w, down_w, starts, starts_down = weights[layer]
        gain, shift = layer_norm_gain[layer], layer_norm_bias[layer]
        down, up = adapters[layer]
        offs = table(member, *starts)
        bias = query_value_bias[layer].reshape(1, 2 * model)
        parts, inner, normed = project(
            offs, hidden, gain[:1], shift[:1], bias, down, up, qkv_w, groups
        )
        parts = plan.swap(parts)
        mixed_parts, mixed, lse = attend(offs, parts)
        mixed_parts = plan.swap(mixed_parts)
        middle, second = mix(
            offs, hidden, output_projection_bias[layer, :1], gain[1:], shift[1:], mixed_parts, out_w
        )
        after, after_low, slope = feed(
            table(*starts, *starts_down),
            second,
            middle,
            feed_up_bias[layer : layer + 1],
            output_projection_bias[layer, 1:],
            up_w,
            down_w,
        )
        saved.append((hidden, normed, inner, parts, mixed, lse, middle, slope))
        outputs.append(plan.scatter_doc(after_low).astype(full))
        hidden = after
    sums = [None] * layers
    for layer in reversed(range(layers)):
        qkv_w, out_w, up_w, down_w, starts, starts_down = weights[layer]
        hidden, normed, inner, parts, mixed, lse, middle, slope = saved[layer]
        gain = layer_norm_gain[layer]
        down, up = adapters[layer]
        offs = table(member, *starts)
        mid, d_mixed = feed_back(
            table(member, *starts, *starts_down, *starts),
            grad,
            middle,
            slope,
            gain[1:],
            up_w,
            down_w,
            out_w,
            groups,
        )
        d_mixed = plan.swap(d_mixed)
        grads = plan.swap(attend_back(offs, parts, d_mixed, mixed, lse))
        grad, grad_low, grad_a, grad_b = project_back(
            offs, mid, hidden, gain[:1], normed, inner, down, up, grads, qkv_w
        )
        sums[layer] = all_sum(jnp.concatenate([grad_a, grad_b]), plan.sp_size, plan.dp_size)
    total = jnp.stack(sums).reshape(layers, 2, 8, model)[:, :, : 2 * rank]
    total = total.reshape(layers, 2, 2, rank, model)
    grad_tokens = plan.scatter_doc(grad_low).astype(full)
    return (jnp.stack(outputs), grad_tokens, total[:, 0].swapaxes(-1, -2), total[:, 1])


def solution(mesh):
    in_specs = (
        P("dp", "sp", None),
        P("dp", "sp", None),
        P(),
        P(),
        P(None, ("sp", "dp"), None),
        P(),
        P(None, ("sp", "dp"), None),
        P(),
        P(None, ("sp", "dp"), None),
        P(),
        P(None, ("sp", "dp"), None),
        P(),
        P(),
    )
    out_specs = (P(None, "dp", "sp", None), P("dp", "sp", None), P(), P())
    return jax.shard_map(
        on_device, mesh=mesh, in_specs=in_specs, out_specs=out_specs, check_vma=False
    )
```

```python
import functools
import jax
import jax.numpy as jnp
from jax import lax
from jax.experimental import pallas as pl
from jax.experimental.pallas import tpu as pltpu
from jax.sharding import PartitionSpec as P

HEAD = 64
LANES = 128
adapter_scale = 8.0
VMEM_BYTES = 58 * 1024 * 1024
low = jnp.bfloat16
full = jnp.float32


def dot(left, right):
    return jnp.dot(left, right, preferred_element_type=full)


def dot_nt(left, right):
    return lax.dot_general(left, right, (((1,), (1,)), ((), ())), preferred_element_type=full)


def dot_tn(left, right):
    return lax.dot_general(left, right, (((0,), (0,)), ((), ())), preferred_element_type=full)


def normalise(value):
    center = value - jnp.mean(value, axis=-1, keepdims=True)
    scale = lax.rsqrt(jnp.mean(center * center, axis=-1, keepdims=True) + 1e-05)
    return center * scale, scale


def norm_back(unit, scale, gain, grad):
    grad = grad * gain
    inner = jnp.mean(grad * unit, axis=-1, keepdims=True)
    return scale * (grad - jnp.mean(grad, axis=-1, keepdims=True) - unit * inner)


def vmem():
    return pl.BlockSpec(memory_space=pltpu.VMEM)


def hbm():
    return pl.BlockSpec(memory_space=pl.ANY)


def smem():
    return pl.BlockSpec(memory_space=pltpu.SMEM)


def brief():
    return pl.CostEstimate(flops=1000, bytes_accessed=1000, transcendentals=0)


def params():
    return pltpu.CompilerParams(vmem_limit_bytes=VMEM_BYTES)


class Copies:
    def __init__(self, sems):
        self.sems, self.used, self.open = sems, 0, []

    def start(self, source, target):
        copy = pltpu.make_async_copy(source, target, self.sems.at[self.used])
        self.used += 1
        copy.start()
        return copy

    def send(self, source, target):
        self.open.append(self.start(source, target))

    def finish(self):
        for copy in self.open:
            copy.wait()

    def rows(self, pieces, column, offsets, first, target, parts=1):
        width = target.shape[1] // parts
        result = []
        for part in range(parts):
            cols = pl.ds(part * width, width)
            source = pl.ds(column + part * width, width)
            row = []
            for index, piece in enumerate(pieces):
                start = pl.multiple_of(offsets[first + index], 64)
                rows = pl.ds(start, piece.shape[0])
                row.append(self.start(piece.at[:, source], target.at[rows, cols]))
            result.append(row)
        return result


def wait_all(copies):
    for copy in copies:
        copy.wait()


def call(kernel, name, outs, scalars, small, large, scratch, sems):
    return pl.pallas_call(
        kernel,
        out_shape=outs,
        in_specs=[smem()] * len(scalars) + [vmem()] * len(small) + [hbm()] * len(large),
        out_specs=[hbm()] * len(outs),
        scratch_shapes=[pltpu.VMEM(shape, kind) for shape, kind in scratch]
        + [pltpu.SemaphoreType.DMA((sems,))],
        compiler_params=params(),
        cost_estimate=brief(),
        name=name,
    )(*scalars, *small, *large)


def sized(kind, *shape):
    return jax.ShapeDtypeStruct(shape, kind)


def project_kernel(count, column, groups, offs, gain, shift, bias, down, up, h_hbm, *rest):
    pieces, rest = rest[:count], rest[count:]
    outs, (u_hbm, a_hbm), rest = rest[:groups], rest[groups : groups + 2], rest[groups + 2 :]
    h_ref, weight, result, a_ref, u_ref, sems = rest
    move = Copies(sems)
    h_copy = move.start(h_hbm, h_ref)
    parts = 3 * groups
    loads = move.rows(pieces, column, offs, 1, weight, parts)
    member = offs[0]
    model = h_ref.shape[1]
    width = model // groups
    h_copy.wait()
    unit, _ = normalise(h_ref[...].astype(full))
    a = (unit * gain[...] + shift[...]).astype(low)
    a_ref[...] = a
    move.send(a_ref, a_hbm)
    u = dot(a, down[...]).astype(low)
    u_ref[...] = u
    move.send(u_ref, u_hbm)
    for part in range(parts):
        kind, group = part // groups, part % groups
        wait_all(loads[part])
        cols = pl.ds(part * width, width)
        value = dot(a, weight[:, cols])
        if kind != 1:
            at = pl.ds((kind // 2) * model + group * width, width)
            value = value + bias[:, at] + dot(u, up[:, at])
        result[:, cols] = value.astype(low)
        if group + 1 == groups:
            for step in range(groups):
                source = pl.multiple_of(kind * model + (member ^ step) * width, width)
                move.send(result.at[:, pl.ds(source, width)], outs[step].at[:, pl.ds(kind * width, width)])
    move.finish()


def project(offs, hidden, gain, shift, bias, down, up, pieces, groups):
    pieces, column = pieces
    tokens, model = hidden.shape
    outs = [sized(low, tokens, 3 * model // groups)] * groups
    outs += [sized(low, tokens, LANES), sized(low, tokens, model)]
    count = len(pieces)
    result = call(
        functools.partial(project_kernel, count, column, groups),
        "project",
        outs,
        [offs],
        [gain, shift, bias, down, up],
        [hidden, *pieces],
        [
            ((tokens, model), hidden.dtype),
            ((model, 3 * model), low),
            ((tokens, 3 * model), low),
            ((tokens, model), low),
            ((tokens, LANES), low),
        ],
        1 + count * 3 * groups + 2 + 3 * groups,
    )
    return result[:groups], result[groups], result[groups + 1]


def mix_kernel(count, column, groups, offs, bias, gain, shift, h_hbm, *rest):
    mixed, pieces, rest = rest[:groups], rest[groups : groups + count], rest[groups + count :]
    m_hbm, c_hbm, h_ref, o_ref, weight, m_ref, c_ref, sems = rest
    move = Copies(sems)
    width = mixed[0].shape[1]
    loads = []
    for step in range(groups):
        at = pl.multiple_of((offs[0] ^ step) * width, width)
        loads.append(move.start(mixed[step], o_ref.at[:, pl.ds(at, width)]))
    loads += move.rows(pieces, column, offs, 1, weight)[0]
    loads.append(move.start(h_hbm, h_ref))
    wait_all(loads)
    step = h_ref.shape[0] // 2
    for start in (0, step):
        rows = pl.ds(start, step)
        total = h_ref[rows, :].astype(full) + (dot(o_ref[rows, :], weight[...]) + bias[...])
        m_ref[rows, :] = total
        move.send(m_ref.at[rows, :], m_hbm.at[rows, :])
        unit, _ = normalise(total)
        c_ref[rows, :] = (unit * gain[...] + shift[...]).astype(low)
        move.send(c_ref.at[rows, :], c_hbm.at[rows, :])
    move.finish()


def mix(offs, hidden, bias, gain, shift, mixed, pieces):
    pieces, column = pieces
    groups, count = len(mixed), len(pieces)
    tokens, model = hidden.shape
    return call(
        functools.partial(mix_kernel, count, column, groups),
        "mix",
        [sized(full, tokens, model), sized(low, tokens, model)],
        [offs],
        [bias, gain, shift],
        [hidden, *mixed, *pieces],
        [
            ((tokens, model), hidden.dtype),
            ((tokens, model), low),
            ((model, model), low),
            ((tokens, model), full),
            ((tokens, model), low),
        ],
        1 + groups + count + 4,
    )


ROOT = 0.7978845608028654
CUBE = 0.044715


def feed_up_kernel(count, column, parts, offs, up_bias, c_hbm, *rest):
    pieces, (acted_hbm, slope_hbm, c_ref, up, acted, slope, sems) = rest[:count], rest[count:]
    move = Copies(sems)
    c_copy = move.start(c_hbm, c_ref)
    loads = move.rows(pieces, column, offs, 1, up, parts)
    width = up.shape[1] // parts
    c_copy.wait()
    c = c_ref[...]
    for part in range(parts):
        cols = pl.ds(part * width, width)
        wait_all(loads[part])
        z = dot(c, up[:, cols]) + up_bias[:, cols]
        square = z * z
        t = jnp.tanh(z * (ROOT + (ROOT * CUBE) * square))
        half = 0.5 + 0.5 * t
        acted[:, cols] = (z * half).astype(low)
        slope[:, cols] = (
            half + z * (1.0 - t * t) * (0.5 * ROOT + (1.5 * ROOT * CUBE) * square)
        ).astype(low)
        move.send(acted.at[:, cols], acted_hbm.at[:, cols])
        move.send(slope.at[:, cols], slope_hbm.at[:, cols])
    move.finish()


def feed_up(offs, second, up_bias, pieces):
    pieces, column = pieces
    tokens, model = second.shape
    hidden = up_bias.shape[1]
    count, parts = len(pieces), 8
    return call(
        functools.partial(feed_up_kernel, count, column, parts),
        "feed_up",
        [sized(low, tokens, hidden)] * 2,
        [offs],
        [up_bias],
        [second, *pieces],
        [
            ((tokens, model), low),
            ((model, hidden), low),
            ((tokens, hidden), low),
            ((tokens, hidden), low),
        ],
        1 + count * parts + 2 * parts,
    )


def chunks(pieces, offs, first, entries, most=512):
    if entries > len(pieces):
        rows = pieces[0].shape[0] // 4
        stripe = 128
        per = most // stripe
        for block in range(4):
            for start in range(0, rows // stripe, per):
                sources = [(0, (4 * (start + i) + block) * stripe, stripe) for i in range(per)]
                yield sources, pl.multiple_of(offs[first + block] + start * stripe, 256), most
        return
    for index, piece in enumerate(pieces):
        for start in range(0, piece.shape[0], most):
            rows = min(most, piece.shape[0] - start)
            yield [(index, start, rows)], pl.multiple_of(offs[first + index] + start, 256), rows


def load_chunk(move, pieces, sources, column, target, at):
    copies = []
    for index, start, rows in sources:
        source = pieces[index].at[pl.ds(start, rows), pl.ds(column, target.shape[1])]
        copies.append(move.start(source, target.at[pl.ds(at, rows), :]))
        at += rows
    return copies


def feed_down_kernel(count, column, entries, offs, bias, y_hbm, m_hbm, *rest):
    pieces, (h_hbm, low_hbm, y_ref, total, h_low, down, sems) = rest[:count], rest[count:]
    move = Copies(sems)
    m_copy = move.start(m_hbm, total)
    parts = []
    at = 0
    for sources, row, rows in chunks(pieces, offs, 1, entries):
        copies = [move.start(y_hbm.at[:, pl.ds(row, rows)], y_ref.at[:, pl.ds(at, rows)])]
        copies += load_chunk(move, pieces, sources, column, down, at)
        parts.append((at, rows, copies))
        at += rows
    m_copy.wait()
    total[...] += bias[...]
    for at, rows, copies in parts:
        wait_all(copies)
        total[...] += dot(y_ref[:, pl.ds(at, rows)], down[pl.ds(at, rows), :])
    move.send(total, h_hbm)
    h_low[...] = total[...].astype(low)
    move.send(h_low, low_hbm)
    move.finish()


def feed_down(offs, acted, middle, bias, pieces):
    pieces, column = pieces
    tokens, hidden = acted.shape
    model = middle.shape[1]
    count = len(pieces)
    return call(
        functools.partial(feed_down_kernel, count, column, offs.shape[0] - 1),
        "feed_down",
        [sized(full, tokens, model), sized(low, tokens, model)],
        [offs],
        [bias],
        [acted, middle, *pieces],
        [
            ((tokens, hidden), low),
            ((tokens, model), full),
            ((tokens, model), low),
            ((hidden, model), low),
        ],
        64,
    )


def feed_back_kernel(entries, ups, downs, outs_count, columns, groups, offs, gain, g_hbm, m_hbm, slope_hbm, *rest):
    up_pieces, rest = rest[:ups], rest[ups:]
    down_pieces, rest = rest[:downs], rest[downs:]
    out_pieces, rest = rest[:outs_count], rest[outs_count:]
    mid_hbm, rest = rest[0], rest[1:]
    outs, rest = rest[:groups], rest[groups:]
    g_ref, m_ref, slope, up, down, out, d_pre, d_second, mixed, sems = rest
    move = Copies(sems)
    g_copy = move.start(g_hbm, g_ref)
    parts = []
    at = 0
    for sources, row, rows in chunks(down_pieces, offs, 1 + ups, entries):
        cols, where = pl.ds(row, rows), pl.ds(at, rows)
        copies = load_chunk(move, down_pieces, sources, columns[1], down, at)
        copies.append(move.start(slope_hbm.at[:, cols], slope.at[:, where]))
        parts.append((where, cols, copies))
        at += rows
    up_loads = move.rows(up_pieces, columns[0], offs, 1, up)[0]
    m_copy = move.start(m_hbm, m_ref)
    out_loads = move.rows(out_pieces, columns[2], offs, 1 + ups + entries, out)[0]
    model = up.shape[0]
    g_copy.wait()
    g = g_ref[...].astype(low)
    for where, cols, copies in parts:
        wait_all(copies)
        d_acted = dot_nt(g, down[where, :])
        d_pre[:, cols] = (d_acted * slope[:, where].astype(full)).astype(low)
    wait_all(up_loads)
    step = 256
    for start in range(0, model, step):
        cols = pl.ds(start, step)
        d_second[:, cols] = dot_nt(d_pre[...], up[cols, :])
    m_copy.wait()
    unit, scale = normalise(m_ref[...])
    grad = g_ref[...].astype(full) + norm_back(unit, scale, gain[...], d_second[...])
    m_ref[...] = grad
    move.send(m_ref, mid_hbm)
    grad = grad.astype(low)
    wait_all(out_loads)
    width = model // groups
    for group in range(groups):
        cols = pl.ds(group * width, width)
        mixed[:, cols] = dot_nt(grad, out[cols, :]).astype(low)
    for step in range(groups):
        at = pl.multiple_of((offs[0] ^ step) * width, width)
        move.send(mixed.at[:, pl.ds(at, width)], outs[step])
    move.finish()


def feed_back(offs, grad, middle, slope, gain, up_pieces, down_pieces, out_pieces, groups):
    (up_pieces, up_column), (down_pieces, down_column) = up_pieces, down_pieces
    out_pieces, out_column = out_pieces
    columns = (up_column, down_column, out_column)
    tokens, model = middle.shape
    hidden = slope.shape[1]
    ups, downs, outs_count = len(up_pieces), len(down_pieces), len(out_pieces)
    result = call(
        functools.partial(feed_back_kernel, offs.shape[0] - 1 - ups - outs_count, ups, downs, outs_count, columns, groups),
        "feed_back",
        [sized(full, tokens, model)] + [sized(low, tokens, model // groups)] * groups,
        [offs],
        [gain],
        [grad, middle, slope, *up_pieces, *down_pieces, *out_pieces],
        [
            ((tokens, model), grad.dtype),
            ((tokens, model), full),
            ((tokens, hidden), low),
            ((model, hidden), low),
            ((hidden, model), low),
            ((model, model), low),
            ((tokens, hidden), low),
            ((tokens, model), full),
            ((tokens, model), low),
        ],
        96,
    )
    return result[0], result[1:]


def adapt_back_kernel(groups, rank, offs, up, a_hbm, u_hbm, *rest):
    grads, rest = rest[:groups], rest[groups:]
    grad_a_hbm, grad_b_hbm, d_inner_hbm, a_ref, u_ref, d_pair, d_inner, grad_a, grad_b, sems = rest
    move = Copies(sems)
    model = a_ref.shape[1]
    width = model // groups
    loads = [move.start(u_hbm, u_ref)]
    for place, kind in enumerate((0, 2)):
        for step in range(groups):
            at = pl.multiple_of(place * model + (offs[0] ^ step) * width, width)
            source = grads[step].at[:, pl.ds(kind * width, width)]
            loads.append(move.start(source, d_pair.at[:, pl.ds(at, width)]))
    a_copy = move.start(a_hbm, a_ref)
    wait_all(loads)
    d_inner[...] = dot_nt(d_pair[...], up[...]).astype(low)
    move.send(d_inner, d_inner_hbm)
    u = u_ref[...]
    lane = lax.broadcasted_iota(jnp.int32, (1, LANES), 1)
    u_query = jnp.where(lane < rank, u, 0).astype(low)
    u_value = jnp.where(lane >= rank, u, 0).astype(low)
    by_rank = dot_tn(u_query, d_pair[:, pl.ds(0, model)]) + dot_tn(u_value, d_pair[:, pl.ds(model, model)])
    grad_b[...] = adapter_scale * by_rank[:8]
    move.send(grad_b, grad_b_hbm)
    a_copy.wait()
    grad_a[...] = dot_tn(d_inner[...], a_ref[...])[:8]
    move.send(grad_a, grad_a_hbm)
    move.finish()


def adapt_back(normed, inner, up, grads, offs, rank):
    groups = len(grads)
    tokens, model = normed.shape
    return call(
        functools.partial(adapt_back_kernel, groups, rank),
        "adapt_back",
        [sized(full, 8, model), sized(full, 8, model), sized(low, tokens, LANES)],
        [offs],
        [up],
        [normed, inner, *grads],
        [
            ((tokens, model), low),
            ((tokens, LANES), low),
            ((tokens, 2 * model), low),
            ((tokens, LANES), low),
            ((8, model), full),
            ((8, model), full),
        ],
        2 + 2 * groups + 3,
    )


def project_back_kernel(count, column, groups, offs, gain, down, inner_hbm, mid_hbm, h_hbm, *rest):
    grads, pieces, rest = rest[:groups], rest[groups : groups + count], rest[groups + count :]
    g_hbm, low_hbm, d_inner, mid_ref, h_ref, weight, d_all, d_normed, g_low, sems = rest
    move = Copies(sems)
    model = h_ref.shape[1]
    width = model // groups
    loads = [move.start(inner_hbm, d_inner)]
    for kind in range(3):
        for step in range(groups):
            at = pl.multiple_of(kind * model + (offs[0] ^ step) * width, width)
            source = grads[step].at[:, pl.ds(kind * width, width)]
            loads.append(move.start(source, d_all.at[:, pl.ds(at, width)]))
    weights = move.rows(pieces, column, offs, 1, weight)[0]
    later = [move.start(h_hbm, h_ref), move.start(mid_hbm, mid_ref)]
    wait_all(loads)
    wait_all(weights)
    step = 256
    for start in range(0, model, step):
        rows = pl.ds(start, step)
        d_normed[:, rows] = dot_nt(d_all[...], weight[rows, :]) + dot_nt(d_inner[...], down[rows, :])
    wait_all(later)
    unit, scale = normalise(h_ref[...].astype(full))
    grad = mid_ref[...] + norm_back(unit, scale, gain[...], d_normed[...])
    g_low[...] = grad.astype(low)
    move.send(g_low, low_hbm)
    mid_ref[...] = grad
    move.send(mid_ref, g_hbm)
    move.finish()


def project_back(offs, mid, hidden, gain, d_inner, down, grads, pieces):
    pieces, column = pieces
    groups, count = len(grads), len(pieces)
    tokens, model = hidden.shape
    return call(
        functools.partial(project_back_kernel, count, column, groups),
        "project_back",
        [sized(full, tokens, model), sized(low, tokens, model)],
        [offs],
        [gain, down],
        [d_inner, mid, hidden, *grads, *pieces],
        [
            ((tokens, LANES), low),
            ((tokens, model), full),
            ((tokens, model), hidden.dtype),
            ((model, 3 * model), low),
            ((tokens, 3 * model), low),
            ((tokens, model), full),
            ((tokens, model), low),
        ],
        1 + 3 * groups + count + 2 + 2,
    )


def attend_kernel(groups, offs, *rest):
    pieces, rest = rest[:groups], rest[groups:]
    outs, (o_ref, lse_ref), (qkv, lse_cols, sems) = rest[:groups], rest[groups : groups + 2], rest[groups + 2 :]
    member = offs[0]
    count, width3 = pieces[0].shape
    width = width3 // 3
    length = count * groups
    pairs = width // LANES
    block = 256
    loads = []
    for step in range(groups):
        rows = pl.ds(pl.multiple_of((member ^ step) * count, count), count)
        copy = pltpu.make_async_copy(pieces[step], qkv.at[rows, :], sems.at[step])
        copy.start()
        loads.append(copy)
    for copy in loads:
        copy.wait()
    lane = lax.broadcasted_iota(jnp.int32, (1, LANES), 1)
    keep = [(lane < HEAD).astype(low), (lane >= HEAD).astype(low)]
    causal = lax.broadcasted_iota(jnp.int32, (block, block), 1) <= lax.broadcasted_iota(
        jnp.int32, (block, block), 0
    )
    lse_cols[...] = jnp.zeros_like(lse_cols)

    @pl.loop(0, pairs)
    def _(pair):
        at = pl.multiple_of(pair * LANES, LANES)
        for start in range(0, length, block):
            rows = pl.ds(start, block)
            q = qkv[rows, pl.ds(at, LANES)]
            k = qkv[pl.ds(0, start + block), pl.ds(width + at, LANES)]
            v = qkv[pl.ds(0, start + block), pl.ds(2 * width + at, LANES)]
            mixed = jnp.zeros((block, LANES), full)
            logs = lse_cols[rows, :]
            for head in range(2):
                scores = dot_nt(q * (keep[head] * 0.125), k)
                corner = jnp.where(causal, scores[:, start:], -1e30)
                if start:
                    scores = jnp.concatenate([scores[:, :start], corner], axis=1)
                else:
                    scores = corner
                top = jnp.max(scores, axis=1, keepdims=True)
                weights = jnp.exp(scores - top)
                total = jnp.sum(weights, axis=1, keepdims=True)
                part = dot(weights.astype(low), v * keep[head])
                mixed = mixed + part * (1.0 / total)
                logs = jnp.where(lane == 2 * pair + head, top + jnp.log(total), logs)
            lse_cols[rows, :] = logs
            o_ref[rows, pl.ds(at, LANES)] = mixed.astype(low)

    lse_ref[...] = lse_cols[...].T
    for step in range(groups):
        rows = pl.ds(pl.multiple_of((member ^ step) * count, count), count)
        outs[step][...] = o_ref[rows, :]


def attend(offs, pieces):
    groups = len(pieces)
    count, width3 = pieces[0].shape
    width, length = width3 // 3, count * groups
    outs = [jax.ShapeDtypeStruct((count, width), low)] * groups
    outs += [jax.ShapeDtypeStruct((length, width), low), jax.ShapeDtypeStruct((LANES, length), full)]
    result = pl.pallas_call(
        functools.partial(attend_kernel, groups),
        out_shape=outs,
        in_specs=[smem()] + [hbm()] * groups,
        out_specs=[vmem()] * len(outs),
        scratch_shapes=[
            pltpu.VMEM((length, width3), low),
            pltpu.VMEM((length, LANES), full),
            pltpu.SemaphoreType.DMA((groups,)),
        ],
        compiler_params=params(),
        cost_estimate=brief(),
        name="attend",
    )(offs, *pieces)
    return result[:groups], result[groups], result[groups + 1]


def attend_back_kernel(groups, offs, *rest):
    pieces, grads, rest = rest[:groups], rest[groups : 2 * groups], rest[2 * groups :]
    (o_ref, lse_ref), rest = rest[:2], rest[2:]
    outs, (qkv, d_out, result, inner, sems) = rest[:groups], rest[groups:]
    member = offs[0]
    count, width3 = pieces[0].shape
    width = width3 // 3
    length = count * groups
    pairs = width // LANES
    block = 256
    loads = []
    for step in range(groups):
        rows = pl.ds(pl.multiple_of((member ^ step) * count, count), count)
        for kind, (source, target) in enumerate(((pieces[step], qkv), (grads[step], d_out))):
            copy = pltpu.make_async_copy(source, target.at[rows, :], sems.at[kind, step])
            copy.start()
            loads.append(copy)
    for copy in loads:
        copy.wait()
    lane = lax.broadcasted_iota(jnp.int32, (1, LANES), 1)
    keep = [(lane < HEAD).astype(low), (lane >= HEAD).astype(low)]
    causal = lax.broadcasted_iota(jnp.int32, (block, block), 0) <= lax.broadcasted_iota(
        jnp.int32, (block, block), 1
    )
    heads = width // HEAD
    of_head = (
        lax.broadcasted_iota(jnp.int32, (max(heads, 8), width), 1) // HEAD
        == lax.broadcasted_iota(jnp.int32, (max(heads, 8), width), 0)
    ).astype(low)
    product = d_out[...].astype(full) * o_ref[...].astype(full)
    high = product.astype(low)
    rest_of = (product - high.astype(full)).astype(low)
    inner[...] = dot_nt(of_head, high) + dot_nt(of_head, rest_of)

    @pl.loop(0, pairs)
    def _(pair):
        at = pl.multiple_of(pair * LANES, LANES)
        grad_k = jnp.zeros((length, LANES), full)
        grad_v = jnp.zeros((length, LANES), full)
        for start in reversed(range(0, length, block)):
            rows = pl.ds(start, block)
            upto = start + block
            q = qkv[rows, pl.ds(at, LANES)]
            d = d_out[rows, pl.ds(at, LANES)]
            k = qkv[pl.ds(0, upto), pl.ds(width + at, LANES)]
            v = qkv[pl.ds(0, upto), pl.ds(2 * width + at, LANES)]
            grad_q = jnp.zeros((block, LANES), full)
            for head in range(2):
                q_head = q * (keep[head] * 0.125)
                d_head = d * keep[head]
                scores = dot_nt(k, q_head)
                log_sum = lse_ref[pl.ds(2 * pair + head, 1), rows]
                probs = jnp.exp(scores - log_sum)
                corner = jnp.where(causal, probs[start:], 0.0)
                probs = jnp.concatenate([probs[:start], corner], axis=0) if start else corner
                d_probs = dot_nt(v, d_head)
                d_scores = (probs * (d_probs - inner[pl.ds(2 * pair + head, 1), rows])).astype(low)
                more_v = dot(probs.astype(low), d_head)
                more_k = dot(d_scores, q_head)
                if upto < length:
                    zeros = jnp.zeros((length - upto, LANES), full)
                    more_v = jnp.concatenate([more_v, zeros], axis=0)
                    more_k = jnp.concatenate([more_k, zeros], axis=0)
                grad_v = grad_v + more_v
                grad_k = grad_k + more_k
                grad_q = grad_q + dot_tn(d_scores, k * (keep[head] * 0.125))
            result[rows, pl.ds(at, LANES)] = grad_q.astype(low)
        result[:, pl.ds(width + at, LANES)] = grad_k.astype(low)
        result[:, pl.ds(2 * width + at, LANES)] = grad_v.astype(low)

    for step in range(groups):
        rows = pl.ds(pl.multiple_of((member ^ step) * count, count), count)
        outs[step][...] = result[rows, :]


def attend_back(offs, pieces, grads, mixed, lse):
    groups = len(pieces)
    count, width3 = pieces[0].shape
    width, length = width3 // 3, count * groups
    outs = [jax.ShapeDtypeStruct((count, width3), low)] * groups
    return pl.pallas_call(
        functools.partial(attend_back_kernel, groups),
        out_shape=outs,
        in_specs=[smem()] + [hbm()] * (2 * groups) + [vmem()] * 2,
        out_specs=[vmem()] * len(outs),
        scratch_shapes=[
            pltpu.VMEM((length, width3), low),
            pltpu.VMEM((length, width), low),
            pltpu.VMEM((length, width3), low),
            pltpu.VMEM((max(width // HEAD, 8), length), full),
            pltpu.SemaphoreType.DMA((2, groups)),
        ],
        compiler_params=params(),
        cost_estimate=brief(),
        name="attend_back",
    )(offs, *pieces, *grads, mixed, lse)


def reshard_perms(sp_size, dp_size):
    quarter = sp_size // 4
    perms = []
    for part in range(2):
        perm = []
        for s in range(sp_size):
            for d in range(dp_size):
                doc = 2 * (d & 1) + ((s & 1) ^ part)
                member = s >> 1
                target_sp = doc * quarter + (member >> 1)
                target_dp = 2 * (d >> 1) + (member & 1)
                perm.append((s * dp_size + d, target_sp * dp_size + target_dp))
        perms.append(perm)
    return perms


def member_perm(sp_size, dp_size, step):
    quarter = sp_size // 4
    perm = []
    for s in range(sp_size):
        for d in range(dp_size):
            doc, high = s // quarter, s % quarter
            member = (2 * high + (d & 1)) ^ step
            target_sp = doc * quarter + (member >> 1)
            target_dp = 2 * (d >> 1) + (member & 1)
            perm.append((s * dp_size + d, target_sp * dp_size + target_dp))
    return perm


class Plan:
    def __init__(self, sp_size, dp_size):
        self.sp_size, self.dp_size = sp_size, dp_size
        self.members = sp_size // 2
        self.perms = reshard_perms(sp_size, dp_size)
        self.back = [[(b, a) for a, b in perm] for perm in self.perms]
        self.s = lax.axis_index("sp")
        self.d = lax.axis_index("dp")
        quarter = sp_size // 4
        self.doc = self.s // quarter
        self.member = 2 * (self.s % quarter) + (self.d & 1)

    def gather_start(self, blocks):
        got = []
        for part in range(2):
            block = lax.dynamic_index_in_dim(blocks, (self.s & 1) ^ part, 0, keepdims=False)
            got.append(lax.ppermute(block, ("sp", "dp"), self.perms[part]))
        return got

    def gather_finish(self, got):
        flip = (self.doc & 1) == 1
        first = jnp.where(flip, got[1], got[0])
        second = jnp.where(flip, got[0], got[1])
        return jnp.concatenate([first, second], axis=0)

    def gather_doc(self, blocks):
        return self.gather_finish(self.gather_start(blocks))

    def scatter_start(self, rows):
        half = rows.shape[0] // 2
        blocks = rows.reshape(2, half, rows.shape[1])
        got = []
        for part in range(2):
            block = lax.dynamic_index_in_dim(blocks, (self.doc & 1) ^ part, 0, keepdims=False)
            got.append(lax.ppermute(block, ("sp", "dp"), self.back[part]))
        return got

    def scatter_finish(self, got):
        flip = (self.s & 1) == 1
        first = jnp.where(flip, got[1], got[0])
        second = jnp.where(flip, got[0], got[1])
        return jnp.stack([first, second])

    def scatter_doc(self, rows):
        return self.scatter_finish(self.scatter_start(rows))

    def swap(self, parts):
        out = [parts[0]]
        for step in range(1, self.members):
            perm = member_perm(self.sp_size, self.dp_size, step)
            out.append(lax.ppermute(parts[step], ("sp", "dp"), perm))
        return out


def all_sum(value, sp_size, dp_size):
    total = sp_size * dp_size
    step = 1
    while step < total:
        value = value + lax.ppermute(
            value, ("sp", "dp"), [(i, i ^ step) for i in range(total)]
        )
        step *= 2
    return value


def after(value, *earlier):
    return lax.optimization_barrier((value, *earlier))[0]


class Clock:
    def __init__(self):
        self.event = ()

    def tick(self, *values):
        self.event = values

    def tied(self, *values):
        if not self.event:
            return values if len(values) > 1 else values[0]
        got = lax.optimization_barrier((*values, *self.event))[: len(values)]
        return got if len(values) > 1 else got[0]


class Fetch:
    def __init__(self, plan, clock, shard):
        self.plan, self.clock = plan, clock
        self.whole = plan.sp_size != 4
        shard = clock.tied(shard)
        if self.whole:
            self.block = lax.all_gather(shard, ("sp", "dp"), axis=0, tiled=True)
            self.side = self.corner = self.block
            return
        self.block = lax.all_gather(shard, "dp", axis=0, tiled=True)
        sp_size, dp_size = plan.sp_size, plan.dp_size
        self.over_core = [(i, i ^ 1) for i in range(dp_size)]
        places = [(s, d) for s in range(sp_size) for d in range(dp_size)]
        self.first_way = [(s * dp_size + d, (s ^ (1 << (d & 1))) * dp_size + d) for s, d in places]
        self.second_way = [(s * dp_size + d, (s ^ (2 >> (d & 1))) * dp_size + d) for s, d in places]

    def near(self):
        if not self.whole:
            block = self.clock.tied(self.block)
            self.side = lax.ppermute(block, ("sp", "dp"), self.first_way)

    def far(self):
        if self.whole:
            return
        rows = self.block.shape[0]
        self.side = self.clock.tied(self.side)
        half = lax.dynamic_slice_in_dim(self.side, (self.plan.d & 1) * (rows // 2), rows // 2, axis=0)
        self.corner = lax.ppermute(half, ("sp", "dp"), self.second_way)
        self.other_side = lax.ppermute(self.side, "dp", self.over_core)

    def pieces(self):
        plan = self.plan
        if self.whole:
            return [self.block], [0]
        corner = self.clock.tied(self.corner)
        other_corner = lax.ppermute(corner, "dp", self.over_core)
        rows = self.block.shape[0]
        s, core = plan.s, plan.d & 1
        half = rows // 2
        starts = [
            s * rows,
            (s ^ (1 << core)) * rows,
            (s ^ (2 >> core)) * rows,
            (s ^ 3) * rows + core * half,
            (s ^ 3) * rows + (1 - core) * half,
        ]
        return [self.block, self.side, self.other_side, corner, other_corner], starts


class Wide:
    def __init__(self, plan, clock, shard):
        self.plan, self.clock = plan, clock
        self.whole = plan.sp_size != 4
        shard = clock.tied(shard)
        self.parts = [shard]
        if not self.whole:
            for step in range(1, 4):
                way = [(i, i ^ step) for i in range(4)]
                self.parts.append(lax.ppermute(shard, "sp", way))

    def gather(self):
        parts = self.clock.tied(*self.parts) if len(self.parts) > 1 else self.parts
        axes = ("sp", "dp") if self.whole else "dp"
        self.block = lax.all_gather(jnp.concatenate(parts), axes, axis=0, tiled=True)

    def pieces(self):
        if self.whole:
            return [self.block], [0]
        rows = self.block.shape[0] // 4
        return [self.block], [(self.plan.s ^ step) * rows for step in range(4)]


def on_device(
    tokens,
    cotangent,
    layer_norm_gain,
    layer_norm_bias,
    query_key_value_weight,
    query_value_bias,
    attention_out_weight,
    output_projection_bias,
    feed_up_weight,
    feed_up_bias,
    feed_down_weight,
    adapter_down_maps,
    adapter_up_weights,
):
    layers = query_key_value_weight.shape[0]
    model = tokens.shape[2]
    rank = adapter_down_maps.shape[3]
    plan = Plan(lax.axis_size("sp"), lax.axis_size("dp"))
    clock = Clock()
    groups = plan.members
    member = plan.member.astype(jnp.int32)

    def table(*entries):
        return jnp.stack([jnp.asarray(entry, jnp.int32) for entry in entries])

    adapters = []
    for layer in range(layers):
        down = jnp.concatenate([adapter_down_maps[layer, 0], adapter_down_maps[layer, 1]], axis=1)
        down = jnp.pad(down, ((0, 0), (0, LANES - 2 * rank)))
        up = adapter_up_weights[layer] * jnp.asarray(adapter_scale, low)
        up = jnp.concatenate(
            [
                jnp.pad(up[0], ((0, LANES - rank), (0, 0))),
                jnp.pad(up[1], ((rank, LANES - 2 * rank), (0, 0))),
            ],
            axis=1,
        )
        adapters.append((down, up))

    def request(layer, kind):
        if layer == layers:
            return None
        if (layer, kind) == (layers - 1, 2):
            wide.gather()
            wide.side = wide.block
            return wide
        if kind == 0:
            shard = query_key_value_weight[layer]
        elif kind == 1:
            shard = jnp.concatenate([attention_out_weight[layer], feed_up_weight[layer]], axis=1)
        else:
            shard = feed_down_weight[layer]
        return Fetch(plan, clock, shard)

    saved, outputs = [], []
    ready = {}
    qkv_fetch = request(0, 0)
    hidden = plan.gather_doc(tokens)
    clock.tick(hidden)
    out_fetch = request(0, 1)
    down_fetch = request(0, 2)
    wide = Wide(plan, clock, feed_down_weight[layers - 1])
    clock.tick(*wide.parts)
    qkv_fetch.near()
    clock.tick(hidden)
    qkv_fetch.far()
    clock.tick(qkv_fetch.side)
    out_fetch.near()
    for layer in range(layers):
        last = layer + 1 == layers
        gain, shift = layer_norm_gain[layer], layer_norm_bias[layer]
        down, up = adapters[layer]
        clock.tick(hidden, qkv_fetch.corner)
        ready[layer, 0] = qkv_fetch.pieces()
        qkv, starts = ready[layer, 0]
        offs = table(member, *starts)
        bias = query_value_bias[layer].reshape(1, 2 * model)
        clock.tick(out_fetch.block)
        next_qkv = request(layer + 1, 0)
        parts, inner, normed = project(
            offs, clock.tied(hidden), gain[:1], shift[:1], bias, down, up, (qkv, 0), groups
        )
        clock.tick(*parts)
        out_fetch.far()
        parts = plan.swap(parts)
        clock.tick(out_fetch.side)
        if not last:
            down_fetch.near()
        parts[0] = clock.tied(parts[0])
        mixed_parts, mixed, lse = attend(offs, parts)
        clock.tick(mixed)
        next_out = request(layer + 1, 1)
        mixed_parts = plan.swap(mixed_parts)
        clock.tick(mixed, out_fetch.corner)
        next_down = request(layer + 1, 2)
        if last:
            sent = plan.gather_start(after(cotangent, mixed))
        ready[layer, 1] = out_fetch.pieces()
        out_up, starts = ready[layer, 1]
        if not last:
            clock.tick(down_fetch.side)
            mixed_parts[0] = clock.tied(mixed_parts[0])
        offs = table(member, *starts)
        middle, second = mix(
            offs,
            hidden,
            output_projection_bias[layer, :1],
            gain[1:],
            shift[1:],
            mixed_parts,
            (out_up, 0),
        )
        if not last:
            down_fetch.far()
            clock.tick(down_fetch.side)
            next_qkv.near()
            clock.tick(next_qkv.block)
        acted, slope = feed_up(
            offs, clock.tied(second), feed_up_bias[layer : layer + 1], (out_up, model)
        )
        clock.tick(acted)
        if last:
            sent = clock.tied(*sent)
            grad = plan.gather_finish(sent)
        else:
            next_out.near()
            clock.tick(acted, down_fetch.corner)
        ready[layer, 2] = down_fetch.pieces()
        saved.append((hidden, normed, inner, parts, mixed, lse, middle, acted, slope))
        down_w, starts = ready[layer, 2]
        if not last:
            clock.tick(next_out.block)
            hidden, after_low = feed_down(
                table(member, *starts),
                clock.tied(acted),
                middle,
                output_projection_bias[layer, 1:],
                (down_w, 0),
            )
            clock.tick(hidden)
            next_qkv.far()
            outputs.append(plan.scatter_start(after_low))
            qkv_fetch, out_fetch, down_fetch = next_qkv, next_out, next_down
    sums = [None] * layers
    waiting = outputs.pop()
    for layer in reversed(range(layers)):
        hidden, normed, inner, parts, mixed, lse, middle, acted, slope = saved[layer]
        gain = layer_norm_gain[layer]
        down, up = adapters[layer]
        (qkv, starts), (out_up, starts_up) = ready[layer, 0], ready[layer, 1]
        down_w, starts_down = ready[layer, 2]
        offs = table(member, *starts)
        mid, d_mixed = feed_back(
            table(member, *starts_up, *starts_down, *starts_up),
            grad,
            middle,
            slope,
            gain[1:],
            (out_up, model),
            (down_w, 0),
            (out_up, 0),
            groups,
        )
        d_mixed = plan.swap(d_mixed)
        if layer + 1 == layers:
            _, after_low = feed_down(
                table(member, *starts_down),
                after(acted, mid),
                middle,
                output_projection_bias[layer, 1:],
                (down_w, 0),
            )
            outputs_late = [plan.scatter_start(after_low)]
            d_mixed[0] = after(d_mixed[0], after_low)
        grads = list(attend_back(offs, parts, d_mixed, mixed, lse))
        if waiting:
            grads[1], *arrived = lax.optimization_barrier((grads[1], *waiting))
            outputs.append(arrived)
        if outputs_late:
            waiting = outputs_late.pop()
        else:
            waiting = []
        grads = plan.swap(grads)
        grad_a, grad_b, d_inner = adapt_back(normed, inner, up, grads, offs, rank)
        grad, grad_low = project_back(
            offs, mid, hidden, gain[:1], after(d_inner, grad_a), down, grads, (qkv, 0)
        )
        sums[layer] = jnp.concatenate([grad_a, grad_b])
    total = all_sum(jnp.stack(sums), plan.sp_size, plan.dp_size).reshape(layers, 2, 8, model)[:, :, : 2 * rank]
    total = total.reshape(layers, 2, 2, rank, model)
    grad_tokens = plan.scatter_doc(grad_low).astype(full)
    outputs = [plan.scatter_finish(got).astype(full) for got in outputs]
    return (jnp.stack(outputs), grad_tokens, total[:, 0].swapaxes(-1, -2), total[:, 1])


def solution(mesh):
    in_specs = (
        P("dp", "sp", None),
        P("dp", "sp", None),
        P(),
        P(),
        P(None, ("sp", "dp"), None),
        P(),
        P(None, ("sp", "dp"), None),
        P(),
        P(None, ("sp", "dp"), None),
        P(),
        P(None, ("sp", "dp"), None),
        P(),
        P(),
    )
    out_specs = (P(None, "dp", "sp", None), P("dp", "sp", None), P(), P())
    return jax.shard_map(
        on_device, mesh=mesh, in_specs=in_specs, out_specs=out_specs, check_vma=False
    )
```

```python
import functools
import jax
import jax.numpy as jnp
from jax import lax
from jax.experimental import pallas as pl
from jax.experimental.pallas import tpu as pltpu
from jax.sharding import PartitionSpec as P

HEAD = 64
LANES = 128
adapter_scale = 8.0
VMEM_BYTES = 58 * 1024 * 1024
low = jnp.bfloat16
full = jnp.float32


def dot(left, right):
    return jnp.dot(left, right, preferred_element_type=full)


def dot_nt(left, right):
    return lax.dot_general(left, right, (((1,), (1,)), ((), ())), preferred_element_type=full)


def dot_tn(left, right):
    return lax.dot_general(left, right, (((0,), (0,)), ((), ())), preferred_element_type=full)


def normalise(value):
    center = value - jnp.mean(value, axis=-1, keepdims=True)
    scale = lax.rsqrt(jnp.mean(center * center, axis=-1, keepdims=True) + 1e-05)
    return center * scale, scale


def norm_back(unit, scale, gain, grad):
    grad = grad * gain
    inner = jnp.mean(grad * unit, axis=-1, keepdims=True)
    return scale * (grad - jnp.mean(grad, axis=-1, keepdims=True) - unit * inner)


def vmem():
    return pl.BlockSpec(memory_space=pltpu.VMEM)


def hbm():
    return pl.BlockSpec(memory_space=pl.ANY)


def smem():
    return pl.BlockSpec(memory_space=pltpu.SMEM)


def brief():
    return pl.CostEstimate(flops=1000, bytes_accessed=1000, transcendentals=0)


def params():
    return pltpu.CompilerParams(vmem_limit_bytes=VMEM_BYTES)


class Copies:
    def __init__(self, sems):
        self.sems, self.used, self.open = sems, 0, []

    def start(self, source, target):
        copy = pltpu.make_async_copy(source, target, self.sems.at[self.used])
        self.used += 1
        copy.start()
        return copy

    def send(self, source, target):
        self.open.append(self.start(source, target))

    def finish(self):
        for copy in self.open:
            copy.wait()

    def rows(self, pieces, column, offsets, first, target, parts=1):
        width = target.shape[1] // parts
        result = []
        for part in range(parts):
            cols = pl.ds(part * width, width)
            source = pl.ds(column + part * width, width)
            row = []
            for index, piece in enumerate(pieces):
                start = pl.multiple_of(offsets[first + index], 64)
                rows = pl.ds(start, piece.shape[0])
                row.append(self.start(piece.at[:, source], target.at[rows, cols]))
            result.append(row)
        return result


def wait_all(copies):
    while copies:
        copies.pop(0).wait()


def call(kernel, name, outs, scalars, small, large, scratch, sems):
    return pl.pallas_call(
        kernel,
        out_shape=outs,
        in_specs=[smem()] * len(scalars) + [vmem()] * len(small) + [hbm()] * len(large),
        out_specs=[hbm()] * len(outs),
        scratch_shapes=[pltpu.VMEM(shape, kind) for shape, kind in scratch]
        + [pltpu.SemaphoreType.DMA((sems,))],
        compiler_params=params(),
        cost_estimate=brief(),
        name=name,
    )(*scalars, *small, *large)


def sized(kind, *shape):
    return jax.ShapeDtypeStruct(shape, kind)


def project_kernel(count, column, groups, offs, gain, shift, bias, down, up, h_hbm, *rest):
    pieces, rest = rest[:count], rest[count:]
    outs, (u_hbm, a_hbm), rest = rest[:groups], rest[groups : groups + 2], rest[groups + 2 :]
    h_ref, weight, result, a_ref, u_ref, sems = rest
    move = Copies(sems)
    h_copy = move.start(h_hbm, h_ref)
    parts = 3 * groups
    loads = move.rows(pieces, column, offs, 1, weight, parts)
    member = offs[0]
    model = h_ref.shape[1]
    width = model // groups
    h_copy.wait()
    unit, _ = normalise(h_ref[...].astype(full))
    a = (unit * gain[...] + shift[...]).astype(low)
    a_ref[...] = a
    move.send(a_ref, a_hbm)
    u = dot(a, down[...]).astype(low)
    u_ref[...] = u
    move.send(u_ref, u_hbm)
    for part in range(parts):
        kind, group = part // groups, part % groups
        wait_all(loads[part])
        cols = pl.ds(part * width, width)
        value = dot(a, weight[:, cols])
        if kind != 1:
            at = pl.ds((kind // 2) * model + group * width, width)
            value = value + bias[:, at] + dot(u, up[:, at])
        result[:, cols] = value.astype(low)
        if group + 1 == groups:
            for step in range(groups):
                source = pl.multiple_of(kind * model + (member ^ step) * width, width)
                move.send(result.at[:, pl.ds(source, width)], outs[step].at[:, pl.ds(kind * width, width)])
    move.finish()


def project(offs, hidden, gain, shift, bias, down, up, pieces, groups):
    pieces, column = pieces
    tokens, model = hidden.shape
    outs = [sized(low, tokens, 3 * model // groups)] * groups
    outs += [sized(low, tokens, LANES), sized(low, tokens, model)]
    count = len(pieces)
    result = call(
        functools.partial(project_kernel, count, column, groups),
        "project",
        outs,
        [offs],
        [gain, shift, bias, down, up],
        [hidden, *pieces],
        [
            ((tokens, model), hidden.dtype),
            ((model, 3 * model), low),
            ((tokens, 3 * model), low),
            ((tokens, model), low),
            ((tokens, LANES), low),
        ],
        1 + count * 3 * groups + 2 + 3 * groups,
    )
    return result[:groups], result[groups], result[groups + 1]


def mix_kernel(count, column, groups, offs, bias, gain, shift, h_hbm, *rest):
    mixed, pieces, rest = rest[:groups], rest[groups : groups + count], rest[groups + count :]
    m_hbm, c_hbm, h_ref, o_ref, weight, m_ref, c_ref, sems = rest
    move = Copies(sems)
    width = mixed[0].shape[1]
    loads = []
    for step in range(groups):
        at = pl.multiple_of((offs[0] ^ step) * width, width)
        loads.append(move.start(mixed[step], o_ref.at[:, pl.ds(at, width)]))
    loads += move.rows(pieces, column, offs, 1, weight)[0]
    loads.append(move.start(h_hbm, h_ref))
    wait_all(loads)
    step = h_ref.shape[0] // 2
    for start in (0, step):
        rows = pl.ds(start, step)
        total = h_ref[rows, :].astype(full) + (dot(o_ref[rows, :], weight[...]) + bias[...])
        m_ref[rows, :] = total
        move.send(m_ref.at[rows, :], m_hbm.at[rows, :])
        unit, _ = normalise(total)
        c_ref[rows, :] = (unit * gain[...] + shift[...]).astype(low)
        move.send(c_ref.at[rows, :], c_hbm.at[rows, :])
    move.finish()


def mix(offs, hidden, bias, gain, shift, mixed, pieces):
    pieces, column = pieces
    groups, count = len(mixed), len(pieces)
    tokens, model = hidden.shape
    return call(
        functools.partial(mix_kernel, count, column, groups),
        "mix",
        [sized(full, tokens, model), sized(low, tokens, model)],
        [offs],
        [bias, gain, shift],
        [hidden, *mixed, *pieces],
        [
            ((tokens, model), hidden.dtype),
            ((tokens, model), low),
            ((model, model), low),
            ((tokens, model), full),
            ((tokens, model), low),
        ],
        1 + groups + count + 4,
    )


SOME = 128
ROOT = 0.7978845608028654
CUBE = 0.044715


def feed_up_kernel(count, column, parts, offs, up_bias, c_hbm, *rest):
    pieces, (acted_hbm, slope_hbm, c_ref, up, acted, slope, sems) = rest[:count], rest[count:]
    move = Copies(sems)
    c_copy = move.start(c_hbm, c_ref)
    loads = move.rows(pieces, column, offs, 1, up, parts)
    width = up.shape[1] // parts
    c_copy.wait()
    tokens = c_ref.shape[0]
    some = min(tokens, SOME)
    for part in range(parts):
        cols = pl.ds(part * width, width)
        wait_all(loads[part])
        for start in range(0, tokens, some):
            rows = pl.ds(start, some)
            z = dot(c_ref[rows, :], up[:, cols]) + up_bias[:, cols]
            square = z * z
            t = jnp.tanh(z * (ROOT + (ROOT * CUBE) * square))
            half = 0.5 + 0.5 * t
            acted[rows, cols] = (z * half).astype(low)
            slope[rows, cols] = (
                half + z * (1.0 - t * t) * (0.5 * ROOT + (1.5 * ROOT * CUBE) * square)
            ).astype(low)
        move.send(acted.at[:, cols], acted_hbm.at[:, cols])
        move.send(slope.at[:, cols], slope_hbm.at[:, cols])
    move.finish()


def feed_up(offs, second, up_bias, pieces):
    pieces, column = pieces
    tokens, model = second.shape
    hidden = up_bias.shape[1]
    count, parts = len(pieces), 8
    return call(
        functools.partial(feed_up_kernel, count, column, parts),
        "feed_up",
        [sized(low, tokens, hidden)] * 2,
        [offs],
        [up_bias],
        [second, *pieces],
        [
            ((tokens, model), low),
            ((model, hidden), low),
            ((tokens, hidden), low),
            ((tokens, hidden), low),
        ],
        1 + count * parts + 2 * parts,
    )


def chunks(pieces, offs, first, entries, most=512):
    if entries > len(pieces):
        rows = pieces[0].shape[0] // 4
        stripe = 128
        per = most // stripe
        for block in range(4):
            for start in range(0, rows // stripe, per):
                sources = [(0, (4 * (start + i) + block) * stripe, stripe) for i in range(per)]
                yield sources, pl.multiple_of(offs[first + block] + start * stripe, 256), most
        return
    for index, piece in enumerate(pieces):
        for start in range(0, piece.shape[0], most):
            rows = min(most, piece.shape[0] - start)
            yield [(index, start, rows)], pl.multiple_of(offs[first + index] + start, 256), rows


def load_chunk(move, pieces, sources, column, target, at):
    copies = []
    for index, start, rows in sources:
        source = pieces[index].at[pl.ds(start, rows), pl.ds(column, target.shape[1])]
        copies.append(move.start(source, target.at[pl.ds(at, rows), :]))
        at += rows
    return copies


def feed_down_kernel(count, column, entries, offs, bias, y_hbm, m_hbm, *rest):
    pieces, (h_hbm, low_hbm, y_ref, total, h_low, down, sems) = rest[:count], rest[count:]
    move = Copies(sems)
    m_copy = move.start(m_hbm, total)
    parts = []
    at = 0
    for sources, row, rows in chunks(pieces, offs, 1, entries):
        copies = [move.start(y_hbm.at[:, pl.ds(row, rows)], y_ref.at[:, pl.ds(at, rows)])]
        copies += load_chunk(move, pieces, sources, column, down, at)
        parts.append((at, rows, copies))
        at += rows
    m_copy.wait()
    total[...] += bias[...]
    for at, rows, copies in parts:
        wait_all(copies)
        total[...] += dot(y_ref[:, pl.ds(at, rows)], down[pl.ds(at, rows), :])
    move.send(total, h_hbm)
    h_low[...] = total[...].astype(low)
    move.send(h_low, low_hbm)
    move.finish()


def feed_down(offs, acted, middle, bias, pieces):
    pieces, column = pieces
    tokens, hidden = acted.shape
    model = middle.shape[1]
    count = len(pieces)
    return call(
        functools.partial(feed_down_kernel, count, column, offs.shape[0] - 1),
        "feed_down",
        [sized(full, tokens, model), sized(low, tokens, model)],
        [offs],
        [bias],
        [acted, middle, *pieces],
        [
            ((tokens, hidden), low),
            ((tokens, model), full),
            ((tokens, model), low),
            ((hidden, model), low),
        ],
        64,
    )


def feed_back_kernel(entries, ups, downs, outs_count, columns, groups, offs, gain, g_hbm, m_hbm, slope_hbm, *rest):
    up_pieces, rest = rest[:ups], rest[ups:]
    down_pieces, rest = rest[:downs], rest[downs:]
    out_pieces, rest = rest[:outs_count], rest[outs_count:]
    mid_hbm, rest = rest[0], rest[1:]
    outs, rest = rest[:groups], rest[groups:]
    g_ref, m_ref, slope, up, down, out, d_pre, d_second, mixed, sems = rest
    move = Copies(sems)
    g_copy = move.start(g_hbm, g_ref)
    parts = []
    at = 0
    for sources, row, rows in chunks(down_pieces, offs, 1 + ups, entries):
        cols, where = pl.ds(row, rows), pl.ds(at, rows)
        copies = load_chunk(move, down_pieces, sources, columns[1], down, at)
        copies.append(move.start(slope_hbm.at[:, cols], slope.at[:, where]))
        parts.append((where, cols, copies))
        at += rows
    up_loads = move.rows(up_pieces, columns[0], offs, 1, up)[0]
    m_copy = move.start(m_hbm, m_ref)
    out_loads = move.rows(out_pieces, columns[2], offs, 1 + ups + entries, out)[0]
    model = up.shape[0]
    g_copy.wait()
    g = g_ref[...].astype(low)
    for where, cols, copies in parts:
        wait_all(copies)
        d_acted = dot_nt(g, down[where, :])
        d_pre[:, cols] = (d_acted * slope[:, where].astype(full)).astype(low)
    wait_all(up_loads)
    step = 256
    for start in range(0, model, step):
        cols = pl.ds(start, step)
        d_second[:, cols] = dot_nt(d_pre[...], up[cols, :])
    m_copy.wait()
    unit, scale = normalise(m_ref[...])
    grad = g_ref[...].astype(full) + norm_back(unit, scale, gain[...], d_second[...])
    m_ref[...] = grad
    move.send(m_ref, mid_hbm)
    grad = grad.astype(low)
    wait_all(out_loads)
    width = model // groups
    for group in range(groups):
        cols = pl.ds(group * width, width)
        mixed[:, cols] = dot_nt(grad, out[cols, :]).astype(low)
    for step in range(groups):
        at = pl.multiple_of((offs[0] ^ step) * width, width)
        move.send(mixed.at[:, pl.ds(at, width)], outs[step])
    move.finish()


def feed_back(offs, grad, middle, slope, gain, up_pieces, down_pieces, out_pieces, groups):
    (up_pieces, up_column), (down_pieces, down_column) = up_pieces, down_pieces
    out_pieces, out_column = out_pieces
    columns = (up_column, down_column, out_column)
    tokens, model = middle.shape
    hidden = slope.shape[1]
    ups, downs, outs_count = len(up_pieces), len(down_pieces), len(out_pieces)
    result = call(
        functools.partial(feed_back_kernel, offs.shape[0] - 1 - ups - outs_count, ups, downs, outs_count, columns, groups),
        "feed_back",
        [sized(full, tokens, model)] + [sized(low, tokens, model // groups)] * groups,
        [offs],
        [gain],
        [grad, middle, slope, *up_pieces, *down_pieces, *out_pieces],
        [
            ((tokens, model), grad.dtype),
            ((tokens, model), full),
            ((tokens, hidden), low),
            ((model, hidden), low),
            ((hidden, model), low),
            ((model, model), low),
            ((tokens, hidden), low),
            ((tokens, model), full),
            ((tokens, model), low),
        ],
        96,
    )
    return result[0], result[1:]


def adapt_back_kernel(groups, rank, offs, up, a_hbm, u_hbm, *rest):
    grads, rest = rest[:groups], rest[groups:]
    grad_a_hbm, grad_b_hbm, d_inner_hbm, a_ref, u_ref, d_pair, d_inner, grad_a, grad_b, sems = rest
    move = Copies(sems)
    model = a_ref.shape[1]
    width = model // groups
    loads = [move.start(u_hbm, u_ref)]
    for place, kind in enumerate((0, 2)):
        for step in range(groups):
            at = pl.multiple_of(place * model + (offs[0] ^ step) * width, width)
            source = grads[step].at[:, pl.ds(kind * width, width)]
            loads.append(move.start(source, d_pair.at[:, pl.ds(at, width)]))
    a_copy = move.start(a_hbm, a_ref)
    wait_all(loads)
    d_inner[...] = dot_nt(d_pair[...], up[...]).astype(low)
    move.send(d_inner, d_inner_hbm)
    u = u_ref[...]
    lane = lax.broadcasted_iota(jnp.int32, (1, LANES), 1)
    u_query = jnp.where(lane < rank, u, 0).astype(low)
    u_value = jnp.where(lane >= rank, u, 0).astype(low)
    by_rank = dot_tn(u_query, d_pair[:, pl.ds(0, model)]) + dot_tn(u_value, d_pair[:, pl.ds(model, model)])
    grad_b[...] = adapter_scale * by_rank[:8]
    move.send(grad_b, grad_b_hbm)
    a_copy.wait()
    grad_a[...] = dot_tn(d_inner[...], a_ref[...])[:8]
    move.send(grad_a, grad_a_hbm)
    move.finish()


def adapt_back(normed, inner, up, grads, offs, rank):
    groups = len(grads)
    tokens, model = normed.shape
    return call(
        functools.partial(adapt_back_kernel, groups, rank),
        "adapt_back",
        [sized(full, 8, model), sized(full, 8, model), sized(low, tokens, LANES)],
        [offs],
        [up],
        [normed, inner, *grads],
        [
            ((tokens, model), low),
            ((tokens, LANES), low),
            ((tokens, 2 * model), low),
            ((tokens, LANES), low),
            ((8, model), full),
            ((8, model), full),
        ],
        2 + 2 * groups + 3,
    )


def project_back_kernel(count, column, groups, half, offs, gain, down, inner_hbm, mid_hbm, h_hbm, *rest):
    grads, pieces, rest = rest[:groups], rest[groups : groups + count], rest[groups + count :]
    outs, rest = rest[:1], rest[1:]
    d_inner, mid_ref, h_ref, weight, d_all, d_normed, g_low, sems = rest
    move = Copies(sems)
    tokens, model = h_ref.shape
    width = model // groups
    at = pl.multiple_of(offs[1 + count] * tokens, tokens) if half else 0
    mine = pl.ds(at, tokens)
    loads = [move.start(inner_hbm.at[mine, :], d_inner)]
    for kind in range(3):
        for step in range(groups):
            to = pl.multiple_of(kind * model + (offs[0] ^ step) * width, width)
            source = grads[step].at[mine, pl.ds(kind * width, width)]
            loads.append(move.start(source, d_all.at[:, pl.ds(to, width)]))
    weights = move.rows(pieces, column, offs, 1, weight)[0]
    later = [move.start(h_hbm.at[mine, :], h_ref), move.start(mid_hbm.at[mine, :], mid_ref)]
    wait_all(loads)
    wait_all(weights)
    step = 256
    for start in range(0, model, step):
        cols = pl.ds(start, step)
        d_normed[:, cols] = dot_nt(d_all[...], weight[cols, :])
    wait_all(later)
    unit, scale = normalise(h_ref[...].astype(full))
    through = d_normed[...] + dot_nt(d_inner[...], down[...])
    grad = mid_ref[...] + norm_back(unit, scale, gain[...], through)
    g_low[...] = grad.astype(low)
    if half:
        move.send(g_low, outs[0])
    else:
        mid_ref[...] = grad
        move.send(mid_ref, outs[0])
    move.finish()


def project_back(offs, mid, hidden, gain, d_inner, down, grads, pieces, half=False):
    pieces, column = pieces
    groups, count = len(grads), len(pieces)
    tokens, model = hidden.shape
    if half:
        tokens = tokens // 2
    return call(
        functools.partial(project_back_kernel, count, column, groups, half),
        "project_back",
        [sized(low, tokens, model)] if half else [sized(full, tokens, model)],
        [offs],
        [gain, down],
        [d_inner, mid, hidden, *grads, *pieces],
        [
            ((tokens, LANES), low),
            ((tokens, model), full),
            ((tokens, model), hidden.dtype),
            ((model, 3 * model), low),
            ((tokens, 3 * model), low),
            ((tokens, model), full),
            ((tokens, model), low),
        ],
        1 + 3 * groups + count + 2 + 2,
    )[0]


BLOCK = 256


def causal_corner(block):
    keys = lax.broadcasted_iota(jnp.int32, (block, block), 0)
    return keys <= lax.broadcasted_iota(jnp.int32, (block, block), 1)


def head_masks():
    lane = lax.broadcasted_iota(jnp.int32, (1, LANES), 1)
    return [(lane < HEAD).astype(low), (lane >= HEAD).astype(low)]


def attend_kernel(groups, offs, *rest):
    pieces, rest = rest[:groups], rest[groups:]
    outs, (o_hbm, lse_hbm), rest = rest[:groups], rest[groups : groups + 2], rest[groups + 2 :]
    qkv, v_turned, o_turned, o_ref, lse, sems = rest
    move = Copies(sems)
    member = offs[0]
    count, width3 = pieces[0].shape
    width = width3 // 3
    length = count * groups
    pairs = width // LANES
    block = min(BLOCK, length)
    places = [
        pl.ds(pl.multiple_of((member ^ step) * count, count), count) for step in range(groups)
    ]
    loads = []
    for pair in range(pairs):
        row = []
        for kind in (2, 1, 0):
            cols = pl.ds(kind * width + pair * LANES, LANES)
            for step in range(groups):
                row.append(move.start(pieces[step].at[:, cols], qkv.at[places[step], cols]))
        loads.append(row)
    keep = head_masks()
    causal = causal_corner(block)
    if lse.shape[0] > 2 * pairs:
        lse[...] = jnp.zeros_like(lse)
    for pair in range(pairs):
        at = pair * LANES
        here = pl.ds(at, LANES)
        wait_all(loads[pair])
        v_turned[...] = qkv[:, pl.ds(2 * width + at, LANES)].T
        for start in range(0, length, block):
            rows = pl.ds(start, block)
            upto = start + block
            q = qkv[rows, here]
            k = qkv[pl.ds(0, upto), pl.ds(width + at, LANES)]
            scores = [dot_nt(k, q * (keep[head] * 0.125)) for head in range(2)]
            for head in range(2):
                where = pl.ds(head * HEAD, HEAD)
                value = scores[head]
                corner = jnp.where(causal, value[start:], -1e30)
                value = jnp.concatenate([value[:start], corner], axis=0) if start else corner
                top = jnp.max(value, axis=0, keepdims=True)
                weights = jnp.exp(value - top)
                total = jnp.sum(weights, axis=0, keepdims=True)
                mixed = dot(v_turned[where, pl.ds(0, upto)], weights.astype(low))
                o_turned[where, rows] = (mixed * (1.0 / total)).astype(low)
                lse[pl.ds(2 * pair + head, 1), rows] = top + jnp.log(total)
        o_ref[:, here] = o_turned[...].T
        move.send(o_ref.at[:, here], o_hbm.at[:, here])
        for step in range(groups):
            move.send(o_ref.at[places[step], here], outs[step].at[:, here])
    move.send(lse, lse_hbm)
    move.finish()


def attend(offs, pieces):
    groups = len(pieces)
    count, width3 = pieces[0].shape
    width, length = width3 // 3, count * groups
    heads = max(8, width // HEAD)
    pairs = width // LANES
    result = call(
        functools.partial(attend_kernel, groups),
        "attend",
        [sized(low, count, width)] * groups + [sized(low, length, width), sized(full, heads, length)],
        [offs],
        [],
        pieces,
        [
            ((length, width3), low),
            ((LANES, length), low),
            ((LANES, length), low),
            ((length, width), low),
            ((heads, length), full),
        ],
        pairs * (4 * groups + 1) + 1,
    )
    return result[:groups], result[groups], result[groups + 1]


def attend_back_kernel(groups, offs, o_hbm, lse_hbm, *rest):
    pieces, grads, rest = rest[:groups], rest[groups : 2 * groups], rest[2 * groups :]
    outs, rest = rest[:groups], rest[groups:]
    qkv, d_out, o_ref, lse, k_turned, q_turned, result, inner, sum_k, sum_v, sems = rest
    move = Copies(sems)
    member = offs[0]
    count, width3 = pieces[0].shape
    width = width3 // 3
    length = count * groups
    pairs = width // LANES
    block = min(BLOCK, length)
    places = [
        pl.ds(pl.multiple_of((member ^ step) * count, count), count) for step in range(groups)
    ]
    first = [move.start(grads[step], d_out.at[places[step], :]) for step in range(groups)]
    first.append(move.start(o_hbm, o_ref))
    loads = []
    for kind in (1, 0, 2):
        cols = pl.ds(kind * width, width)
        loads.append(
            [move.start(pieces[i].at[:, cols], qkv.at[places[i], cols]) for i in range(groups)]
        )
    lse_copy = move.start(lse_hbm, lse)
    keep = head_masks()
    causal = causal_corner(block)
    heads = lse.shape[0]
    of_head = (
        lax.broadcasted_iota(jnp.int32, (heads, width), 1) // HEAD
        == lax.broadcasted_iota(jnp.int32, (heads, width), 0)
    ).astype(low)
    wait_all(first)
    product = d_out[...].astype(full) * o_ref[...].astype(full)
    high = product.astype(low)
    rest_of = (product - high.astype(full)).astype(low)
    inner[...] = dot_nt(of_head, high) + dot_nt(of_head, rest_of)
    wait_all(loads[0])
    k_turned[...] = qkv[:, pl.ds(width, width)].T
    wait_all(loads[1])
    wait_all(loads[2])
    lse_copy.wait()

    def pair_step(pair):
        at = pair * LANES
        for start in reversed(range(0, length, block)):
            rows = pl.ds(start, block)
            upto = start + block
            past = pl.ds(0, upto)
            q = qkv[rows, pl.ds(at, LANES)]
            d = d_out[rows, pl.ds(at, LANES)]
            k = qkv[past, pl.ds(width + at, LANES)]
            v = qkv[past, pl.ds(2 * width + at, LANES)]
            q_heads = [q * (keep[head] * 0.125) for head in range(2)]
            d_heads = [d * keep[head] for head in range(2)]
            scores = [dot_nt(k, q_heads[head]) for head in range(2)]
            d_probs = [dot_nt(v, d_heads[head]) for head in range(2)]
            more_k = more_v = None
            for head in range(2):
                line = pl.ds(2 * pair + head, 1)
                probs = jnp.exp(scores[head] - lse[line, rows])
                corner = jnp.where(causal, probs[start:], 0.0)
                probs = jnp.concatenate([probs[:start], corner], axis=0) if start else corner
                d_scores = (probs * (d_probs[head] - inner[line, rows])).astype(low)
                part_v = dot(probs.astype(low), d_heads[head])
                part_k = dot(d_scores, q_heads[head])
                more_v = part_v if more_v is None else more_v + part_v
                more_k = part_k if more_k is None else more_k + part_k
                where = pl.ds(at + head * HEAD, HEAD)
                q_turned[where, rows] = (0.125 * dot(k_turned[where, past], d_scores)).astype(low)
            if upto == length:
                sum_v[...] = more_v
                sum_k[...] = more_k
            else:
                sum_v[past, :] += more_v
                sum_k[past, :] += more_k
        result[:, pl.ds(width + at, LANES)] = sum_k[...].astype(low)
        result[:, pl.ds(2 * width + at, LANES)] = sum_v[...].astype(low)

    for pair in range(pairs):
        pair_step(pair)
    result[:, pl.ds(0, width)] = q_turned[...].T
    for step in range(groups):
        move.send(result.at[places[step], :], outs[step])
    move.finish()


def attend_back(offs, pieces, grads, mixed, lse):
    groups = len(pieces)
    count, width3 = pieces[0].shape
    width, length = width3 // 3, count * groups
    heads = lse.shape[0]
    return call(
        functools.partial(attend_back_kernel, groups),
        "attend_back",
        [sized(low, count, width3)] * groups,
        [offs],
        [],
        [mixed, lse, *pieces, *grads],
        [
            ((length, width3), low),
            ((length, width), low),
            ((length, width), low),
            ((heads, length), full),
            ((width, length), low),
            ((width, length), low),
            ((length, width3), low),
            ((heads, length), full),
            ((length, LANES), full),
            ((length, LANES), full),
        ],
        5 * groups + 2,
    )


def reshard_perms(sp_size, dp_size):
    quarter = sp_size // 4
    perms = []
    for part in range(2):
        perm = []
        for s in range(sp_size):
            for d in range(dp_size):
                doc = 2 * (d & 1) + ((s & 1) ^ part)
                member = s >> 1
                target_sp = doc * quarter + (member >> 1)
                target_dp = 2 * (d >> 1) + (member & 1)
                perm.append((s * dp_size + d, target_sp * dp_size + target_dp))
        perms.append(perm)
    return perms


def member_perm(sp_size, dp_size, step):
    quarter = sp_size // 4
    perm = []
    for s in range(sp_size):
        for d in range(dp_size):
            doc, high = s // quarter, s % quarter
            member = (2 * high + (d & 1)) ^ step
            target_sp = doc * quarter + (member >> 1)
            target_dp = 2 * (d >> 1) + (member & 1)
            perm.append((s * dp_size + d, target_sp * dp_size + target_dp))
    return perm


class Plan:
    def __init__(self, sp_size, dp_size):
        self.sp_size, self.dp_size = sp_size, dp_size
        self.members = sp_size // 2
        self.perms = reshard_perms(sp_size, dp_size)
        self.back = [[(b, a) for a, b in perm] for perm in self.perms]
        self.s = lax.axis_index("sp")
        self.d = lax.axis_index("dp")
        quarter = sp_size // 4
        self.doc = self.s // quarter
        self.member = 2 * (self.s % quarter) + (self.d & 1)

    def gather_start(self, blocks):
        got = []
        for part in range(2):
            block = lax.dynamic_index_in_dim(blocks, (self.s & 1) ^ part, 0, keepdims=False)
            got.append(lax.ppermute(block, ("sp", "dp"), self.perms[part]))
        return got

    def gather_finish(self, got):
        flip = (self.doc & 1) == 1
        first = jnp.where(flip, got[1], got[0])
        second = jnp.where(flip, got[0], got[1])
        return jnp.concatenate([first, second], axis=0)

    def gather_doc(self, blocks):
        return self.gather_finish(self.gather_start(blocks))

    def scatter_start(self, rows):
        half = rows.shape[0] // 2
        blocks = rows.reshape(2, half, rows.shape[1])
        got = []
        for part in range(2):
            block = lax.dynamic_index_in_dim(blocks, (self.doc & 1) ^ part, 0, keepdims=False)
            got.append(lax.ppermute(block, ("sp", "dp"), self.back[part]))
        return got

    def scatter_finish(self, got):
        flip = (self.s & 1) == 1
        first = jnp.where(flip, got[1], got[0])
        second = jnp.where(flip, got[0], got[1])
        return jnp.stack([first, second])

    def scatter_doc(self, rows):
        return self.scatter_finish(self.scatter_start(rows))

    def swap(self, parts):
        out = [parts[0]]
        for step in range(1, self.members):
            perm = member_perm(self.sp_size, self.dp_size, step)
            out.append(lax.ppermute(parts[step], ("sp", "dp"), perm))
        return out


def add_from(value, step, total):
    return value + lax.ppermute(value, ("sp", "dp"), [(i, i ^ step) for i in range(total)])


def after(value, *earlier):
    return lax.optimization_barrier((value, *earlier))[0]


class Clock:
    def __init__(self):
        self.event = ()

    def tick(self, *values):
        self.event = values

    def tied(self, *values):
        if not self.event:
            return values if len(values) > 1 else values[0]
        got = lax.optimization_barrier((*values, *self.event))[: len(values)]
        return got if len(values) > 1 else got[0]


class Fetch:
    def __init__(self, plan, clock, shard):
        self.plan, self.clock = plan, clock
        self.whole = plan.sp_size != 4
        shard = clock.tied(shard)
        if self.whole:
            self.block = lax.all_gather(shard, ("sp", "dp"), axis=0, tiled=True)
            self.side = self.corner = self.block
            return
        self.block = lax.all_gather(shard, "dp", axis=0, tiled=True)
        sp_size, dp_size = plan.sp_size, plan.dp_size
        self.over_core = [(i, i ^ 1) for i in range(dp_size)]
        places = [(s, d) for s in range(sp_size) for d in range(dp_size)]
        self.first_way = [(s * dp_size + d, (s ^ (1 << (d & 1))) * dp_size + d) for s, d in places]
        self.second_way = [(s * dp_size + d, (s ^ (2 >> (d & 1))) * dp_size + d) for s, d in places]

    def split(self, columns):
        both = []
        for cols in (slice(None, columns), slice(columns, None)):
            part = object.__new__(Fetch)
            part.__dict__.update(self.__dict__)
            part.block = self.block[:, cols]
            if self.whole:
                part.side = part.corner = part.block
            both.append(part)
        return both

    def near(self):
        if not self.whole:
            block = self.clock.tied(self.block)
            self.side = lax.ppermute(block, ("sp", "dp"), self.first_way)

    def far(self):
        if self.whole:
            return
        rows = self.block.shape[0]
        self.side = self.clock.tied(self.side)
        half = lax.dynamic_slice_in_dim(self.side, (self.plan.d & 1) * (rows // 2), rows // 2, axis=0)
        self.corner = lax.ppermute(half, ("sp", "dp"), self.second_way)
        self.other_side = lax.ppermute(self.side, "dp", self.over_core)

    def pieces(self):
        plan = self.plan
        if self.whole:
            return [self.block], [0]
        corner = self.clock.tied(self.corner)
        other_corner = lax.ppermute(corner, "dp", self.over_core)
        rows = self.block.shape[0]
        s, core = plan.s, plan.d & 1
        half = rows // 2
        starts = [
            s * rows,
            (s ^ (1 << core)) * rows,
            (s ^ (2 >> core)) * rows,
            (s ^ 3) * rows + core * half,
            (s ^ 3) * rows + (1 - core) * half,
        ]
        return [self.block, self.side, self.other_side, corner, other_corner], starts


class Wide:
    def __init__(self, plan, clock, shard):
        self.plan, self.clock = plan, clock
        self.whole = plan.sp_size != 4
        shard = clock.tied(shard)
        self.parts = [shard]
        if not self.whole:
            for step in range(1, 4):
                way = [(i, i ^ step) for i in range(4)]
                self.parts.append(lax.ppermute(shard, "sp", way))

    def gather(self):
        parts = self.clock.tied(*self.parts) if len(self.parts) > 1 else self.parts
        axes = ("sp", "dp") if self.whole else "dp"
        self.block = lax.all_gather(jnp.concatenate(parts), axes, axis=0, tiled=True)

    def pieces(self):
        if self.whole:
            return [self.block], [0]
        rows = self.block.shape[0] // 4
        return [self.block], [(self.plan.s ^ step) * rows for step in range(4)]


def on_device(
    tokens,
    cotangent,
    layer_norm_gain,
    layer_norm_bias,
    query_key_value_weight,
    query_value_bias,
    attention_out_weight,
    output_projection_bias,
    feed_up_weight,
    feed_up_bias,
    feed_down_weight,
    adapter_down_maps,
    adapter_up_weights,
):
    layers = query_key_value_weight.shape[0]
    model = tokens.shape[2]
    rank = adapter_down_maps.shape[3]
    plan = Plan(lax.axis_size("sp"), lax.axis_size("dp"))
    clock = Clock()
    groups = plan.members
    member = plan.member.astype(jnp.int32)

    def table(*entries):
        return jnp.stack([jnp.asarray(entry, jnp.int32) for entry in entries])

    adapters = []
    for layer in range(layers):
        down = jnp.concatenate([adapter_down_maps[layer, 0], adapter_down_maps[layer, 1]], axis=1)
        down = jnp.pad(down, ((0, 0), (0, LANES - 2 * rank)))
        up = adapter_up_weights[layer] * jnp.asarray(adapter_scale, low)
        up = jnp.concatenate(
            [
                jnp.pad(up[0], ((0, LANES - rank), (0, 0))),
                jnp.pad(up[1], ((rank, LANES - 2 * rank), (0, 0))),
            ],
            axis=1,
        )
        adapters.append((down, up))

    def request(layer, *kinds):
        shards = []
        for kind in kinds:
            if kind == 0:
                shards.append(query_key_value_weight[layer])
            elif kind == 1:
                shards += [attention_out_weight[layer], feed_up_weight[layer]]
            else:
                shards.append(feed_down_weight[layer])
        shard = jnp.concatenate(shards, axis=1) if len(shards) > 1 else shards[0]
        return Fetch(plan, clock, shard)

    saved, outputs = [], []
    ready = {}
    qkv_fetch = request(0, 0)
    wide = Wide(plan, clock, feed_down_weight[layers - 1])
    sent = plan.gather_start(tokens)
    clock.tick(*wide.parts, *sent)
    hidden = plan.gather_finish(clock.tied(*sent))
    clock.tick(hidden)
    out_fetch = request(0, 1)
    down_fetch = request(0, 2)
    clock.tick(*wide.parts)
    qkv_fetch.near()
    clock.tick(hidden)
    qkv_fetch.far()
    clock.tick(qkv_fetch.side)
    out_fetch.near()
    for layer in range(layers):
        last = layer + 1 == layers
        gain, shift = layer_norm_gain[layer], layer_norm_bias[layer]
        down, up = adapters[layer]
        clock.tick(hidden, qkv_fetch.corner)
        ready[layer, 0] = qkv_fetch.pieces()
        if not last:
            following = request(layer + 1, 0, 1)
        qkv, starts = ready[layer, 0]
        offs = table(member, *starts)
        bias = query_value_bias[layer].reshape(1, 2 * model)
        clock.tick(out_fetch.block)
        parts, inner, normed = project(
            offs, clock.tied(hidden), gain[:1], shift[:1], bias, down, up, (qkv, 0), groups
        )
        clock.tick(*parts)
        out_fetch.far()
        if not last:
            clock.tick(out_fetch.side, *parts)
            if layer + 2 == layers:
                wide.gather()
                next_down = wide
            else:
                next_down = request(layer + 1, 2)
        parts = plan.swap(parts)
        clock.tick(out_fetch.side)
        if not last:
            down_fetch.near()
        parts[0] = clock.tied(parts[0])
        mixed_parts, mixed, lse = attend(offs, parts)
        clock.tick(mixed)
        mixed_parts = plan.swap(mixed_parts)
        clock.tick(mixed, out_fetch.corner)
        ready[layer, 1] = out_fetch.pieces()
        out_up, starts = ready[layer, 1]
        if not last:
            clock.tick(down_fetch.side)
            mixed_parts[0] = clock.tied(mixed_parts[0])
        offs = table(member, *starts)
        middle, second = mix(
            offs,
            hidden,
            output_projection_bias[layer, :1],
            gain[1:],
            shift[1:],
            mixed_parts,
            (out_up, 0),
        )
        if not last:
            down_fetch.far()
            clock.tick(down_fetch.side)
            next_qkv, next_out = following.split(3 * model)
            next_qkv.near()
            clock.tick(next_qkv.block)
        acted, slope = feed_up(
            offs, clock.tied(second), feed_up_bias[layer : layer + 1], (out_up, model)
        )
        clock.tick(acted)
        if last:
            sent = clock.tied(*plan.gather_start(after(cotangent, second)))
            grad = plan.gather_finish(sent)
        else:
            next_out.near()
            clock.tick(acted, down_fetch.corner)
        ready[layer, 2] = down_fetch.pieces()
        saved.append((hidden, normed, inner, parts, mixed, lse, middle, acted, slope))
        down_w, starts = ready[layer, 2]
        if not last:
            clock.tick(next_out.block)
            hidden, after_low = feed_down(
                table(member, *starts),
                clock.tied(acted),
                middle,
                output_projection_bias[layer, 1:],
                (down_w, 0),
            )
            clock.tick(hidden)
            next_qkv.far()
            outputs.append(plan.scatter_start(after_low))
            qkv_fetch, out_fetch, down_fetch = next_qkv, next_out, next_down
    sums = [None] * layers
    waiting = outputs.pop()
    for layer in reversed(range(layers)):
        hidden, normed, inner, parts, mixed, lse, middle, acted, slope = saved[layer]
        gain = layer_norm_gain[layer]
        down, up = adapters[layer]
        (qkv, starts), (out_up, starts_up) = ready[layer, 0], ready[layer, 1]
        down_w, starts_down = ready[layer, 2]
        offs = table(member, *starts)
        mid, d_mixed = feed_back(
            table(member, *starts_up, *starts_down, *starts_up),
            grad,
            middle,
            slope,
            gain[1:],
            (out_up, model),
            (down_w, 0),
            (out_up, 0),
            groups,
        )
        d_mixed = plan.swap(d_mixed)
        if layer + 1 == layers:
            _, after_low = feed_down(
                table(member, *starts_down),
                after(acted, mid),
                middle,
                output_projection_bias[layer, 1:],
                (down_w, 0),
            )
            outputs_late = [plan.scatter_start(after_low)]
            d_mixed[0] = after(d_mixed[0], after_low)
        grads = list(attend_back(offs, parts, d_mixed, mixed, lse))
        if waiting:
            grads[1], *arrived = lax.optimization_barrier((grads[1], *waiting))
            outputs.append(arrived)
        if outputs_late:
            waiting = outputs_late.pop()
        else:
            waiting = []
        grads = plan.swap(grads)
        grad_a, grad_b, d_inner = adapt_back(normed, inner, up, grads, offs, rank)
        sums[layer] = jnp.concatenate([grad_a, grad_b])
        if layer:
            d_inner = after(d_inner, grad_a)
            grad = project_back(offs, mid, hidden, gain[:1], d_inner, down, grads, (qkv, 0))
    total = jnp.stack(sums)
    flat = plan.sp_size * plan.dp_size
    steps = [1 << bit for bit in range(flat.bit_length() - 1)]
    for step in steps[:1]:
        total = add_from(total, step, flat)
    sent = []
    for half in range(2):
        if half + 1 < len(steps):
            total = add_from(total, steps[half + 1], flat)
        which = (plan.doc & 1) ^ half
        back = project_back(
            table(member, *starts, which),
            mid,
            hidden,
            gain[:1],
            d_inner,
            down,
            grads,
            (qkv, 0),
            half=True,
        )
        total, back = lax.optimization_barrier((total, back))
        sent.append(lax.ppermute(back, ("sp", "dp"), plan.back[half]))
        d_inner = after(d_inner, back)
    for step in steps[3:]:
        total = add_from(total, step, flat)
    grad_tokens = plan.scatter_finish(sent).astype(full)
    total = total.reshape(layers, 2, 8, model)[:, :, : 2 * rank]
    total = total.reshape(layers, 2, 2, rank, model)
    outputs = [plan.scatter_finish(got).astype(full) for got in outputs]
    return (jnp.stack(outputs), grad_tokens, total[:, 0].swapaxes(-1, -2), total[:, 1])


def solution(mesh):
    in_specs = (
        P("dp", "sp", None),
        P("dp", "sp", None),
        P(),
        P(),
        P(None, ("sp", "dp"), None),
        P(),
        P(None, ("sp", "dp"), None),
        P(),
        P(None, ("sp", "dp"), None),
        P(),
        P(None, ("sp", "dp"), None),
        P(),
        P(),
    )
    out_specs = (P(None, "dp", "sp", None), P("dp", "sp", None), P(), P())
    return jax.shard_map(
        on_device, mesh=mesh, in_specs=in_specs, out_specs=out_specs, check_vma=False
    )
```

```python
import functools
import jax
import jax.numpy as jnp
from jax import lax
from jax.experimental import pallas as pl
from jax.experimental.pallas import tpu as pltpu
from jax.sharding import PartitionSpec as P

HEAD = 64
LANES = 128
adapter_scale = 8.0
VMEM_BYTES = 58 * 1024 * 1024
BACK_VMEM_BYTES = 50 * 1024 * 1024
low = jnp.bfloat16
full = jnp.float32


def dot(left, right):
    return jnp.dot(left, right, preferred_element_type=full)


def dot_nt(left, right):
    return lax.dot_general(left, right, (((1,), (1,)), ((), ())), preferred_element_type=full)


def dot_tn(left, right):
    return lax.dot_general(left, right, (((0,), (0,)), ((), ())), preferred_element_type=full)


def normalise(value):
    center = value - jnp.mean(value, axis=-1, keepdims=True)
    scale = lax.rsqrt(jnp.mean(center * center, axis=-1, keepdims=True) + 1e-05)
    return center * scale, scale


def norm_back(unit, scale, gain, grad):
    grad = grad * gain
    inner = jnp.mean(grad * unit, axis=-1, keepdims=True)
    return scale * (grad - jnp.mean(grad, axis=-1, keepdims=True) - unit * inner)


def vmem():
    return pl.BlockSpec(memory_space=pltpu.VMEM)


def hbm():
    return pl.BlockSpec(memory_space=pl.ANY)


def smem():
    return pl.BlockSpec(memory_space=pltpu.SMEM)


def brief():
    return pl.CostEstimate(flops=1000, bytes_accessed=1000, transcendentals=0)


def params(name):
    back = name.endswith("_back")
    return pltpu.CompilerParams(vmem_limit_bytes=BACK_VMEM_BYTES if back else VMEM_BYTES)


class Copies:
    def __init__(self, sems):
        self.sems, self.used, self.open = sems, 0, []

    def start(self, source, target):
        copy = pltpu.make_async_copy(source, target, self.sems.at[self.used])
        self.used += 1
        copy.start()
        return copy

    def send(self, source, target):
        self.open.append(self.start(source, target))

    def finish(self):
        for copy in self.open:
            copy.wait()

    def rows(self, pieces, column, offsets, first, target, parts=1):
        width = target.shape[1] // parts
        result = []
        for part in range(parts):
            cols = pl.ds(part * width, width)
            source = pl.ds(column + part * width, width)
            row = []
            for index, piece in enumerate(pieces):
                start = pl.multiple_of(offsets[first + index], 64)
                rows = pl.ds(start, piece.shape[0])
                row.append(self.start(piece.at[:, source], target.at[rows, cols]))
            result.append(row)
        return result


def wait_all(copies):
    while copies:
        copies.pop(0).wait()


def call(kernel, name, outs, scalars, small, large, scratch, sems):
    return pl.pallas_call(
        kernel,
        out_shape=outs,
        in_specs=[smem()] * len(scalars) + [vmem()] * len(small) + [hbm()] * len(large),
        out_specs=[hbm()] * len(outs),
        scratch_shapes=[pltpu.VMEM(shape, kind) for shape, kind in scratch]
        + [pltpu.SemaphoreType.DMA((sems,))],
        compiler_params=params(name),
        cost_estimate=brief(),
        name=name,
    )(*scalars, *small, *large)


def sized(kind, *shape):
    return jax.ShapeDtypeStruct(shape, kind)


def project_kernel(count, column, groups, offs, gain, shift, bias, down, up, h_hbm, *rest):
    pieces, rest = rest[:count], rest[count:]
    outs, (u_hbm, a_hbm), rest = rest[:groups], rest[groups : groups + 2], rest[groups + 2 :]
    h_ref, weight, result, a_ref, u_ref, sems = rest
    move = Copies(sems)
    h_copy = move.start(h_hbm, h_ref)
    parts = 3 * groups
    loads = move.rows(pieces, column, offs, 1, weight, parts)
    member = offs[0]
    model = h_ref.shape[1]
    width = model // groups
    h_copy.wait()
    unit, _ = normalise(h_ref[...].astype(full))
    a = (unit * gain[...] + shift[...]).astype(low)
    a_ref[...] = a
    move.send(a_ref, a_hbm)
    u = dot(a, down[...]).astype(low)
    u_ref[...] = u
    move.send(u_ref, u_hbm)
    for part in range(parts):
        kind, group = part // groups, part % groups
        wait_all(loads[part])
        cols = pl.ds(part * width, width)
        value = dot(a, weight[:, cols])
        if kind != 1:
            at = pl.ds((kind // 2) * model + group * width, width)
            value = value + bias[:, at] + dot(u, up[:, at])
        result[:, cols] = value.astype(low)
        if group + 1 == groups:
            for step in range(groups):
                source = pl.multiple_of(kind * model + (member ^ step) * width, width)
                move.send(result.at[:, pl.ds(source, width)], outs[step].at[:, pl.ds(kind * width, width)])
    move.finish()


def project(offs, hidden, gain, shift, bias, down, up, pieces, groups):
    pieces, column = pieces
    tokens, model = hidden.shape
    outs = [sized(low, tokens, 3 * model // groups)] * groups
    outs += [sized(low, tokens, LANES), sized(low, tokens, model)]
    count = len(pieces)
    result = call(
        functools.partial(project_kernel, count, column, groups),
        "project",
        outs,
        [offs],
        [gain, shift, bias, down, up],
        [hidden, *pieces],
        [
            ((tokens, model), hidden.dtype),
            ((model, 3 * model), low),
            ((tokens, 3 * model), low),
            ((tokens, model), low),
            ((tokens, LANES), low),
        ],
        1 + count * 3 * groups + 2 + 3 * groups,
    )
    return result[:groups], result[groups], result[groups + 1]


def mix_kernel(count, column, groups, offs, bias, gain, shift, h_hbm, *rest):
    mixed, pieces, rest = rest[:groups], rest[groups : groups + count], rest[groups + count :]
    m_hbm, c_hbm, h_ref, o_ref, weight, m_ref, c_ref, sems = rest
    move = Copies(sems)
    width = mixed[0].shape[1]
    loads = []
    for step in range(groups):
        at = pl.multiple_of((offs[0] ^ step) * width, width)
        loads.append(move.start(mixed[step], o_ref.at[:, pl.ds(at, width)]))
    loads += move.rows(pieces, column, offs, 1, weight)[0]
    loads.append(move.start(h_hbm, h_ref))
    wait_all(loads)
    step = h_ref.shape[0] // 2
    for start in (0, step):
        rows = pl.ds(start, step)
        total = h_ref[rows, :].astype(full) + (dot(o_ref[rows, :], weight[...]) + bias[...])
        m_ref[rows, :] = total
        move.send(m_ref.at[rows, :], m_hbm.at[rows, :])
        unit, _ = normalise(total)
        c_ref[rows, :] = (unit * gain[...] + shift[...]).astype(low)
        move.send(c_ref.at[rows, :], c_hbm.at[rows, :])
    move.finish()


def mix(offs, hidden, bias, gain, shift, mixed, pieces):
    pieces, column = pieces
    groups, count = len(mixed), len(pieces)
    tokens, model = hidden.shape
    return call(
        functools.partial(mix_kernel, count, column, groups),
        "mix",
        [sized(full, tokens, model), sized(low, tokens, model)],
        [offs],
        [bias, gain, shift],
        [hidden, *mixed, *pieces],
        [
            ((tokens, model), hidden.dtype),
            ((tokens, model), low),
            ((model, model), low),
            ((tokens, model), full),
            ((tokens, model), low),
        ],
        1 + groups + count + 4,
    )


SOME = 128
ROOT = 0.7978845608028654
CUBE = 0.044715


def feed_up_kernel(count, column, parts, offs, up_bias, c_hbm, *rest):
    pieces, (acted_hbm, slope_hbm, c_ref, up, acted, slope, sems) = rest[:count], rest[count:]
    move = Copies(sems)
    c_copy = move.start(c_hbm, c_ref)
    loads = move.rows(pieces, column, offs, 1, up, parts)
    width = up.shape[1] // parts
    c_copy.wait()
    tokens = c_ref.shape[0]
    some = min(tokens, SOME)
    for part in range(parts):
        cols = pl.ds(part * width, width)
        wait_all(loads[part])
        for start in range(0, tokens, some):
            rows = pl.ds(start, some)
            z = dot(c_ref[rows, :], up[:, cols]) + up_bias[:, cols]
            square = z * z
            t = jnp.tanh(z * (ROOT + (ROOT * CUBE) * square))
            half = 0.5 + 0.5 * t
            acted[rows, cols] = (z * half).astype(low)
            slope[rows, cols] = (
                half + z * (1.0 - t * t) * (0.5 * ROOT + (1.5 * ROOT * CUBE) * square)
            ).astype(low)
        move.send(acted.at[:, cols], acted_hbm.at[:, cols])
        move.send(slope.at[:, cols], slope_hbm.at[:, cols])
    move.finish()


def feed_up(offs, second, up_bias, pieces):
    pieces, column = pieces
    tokens, model = second.shape
    hidden = up_bias.shape[1]
    count, parts = len(pieces), 4
    return call(
        functools.partial(feed_up_kernel, count, column, parts),
        "feed_up",
        [sized(low, tokens, hidden)] * 2,
        [offs],
        [up_bias],
        [second, *pieces],
        [
            ((tokens, model), low),
            ((model, hidden), low),
            ((tokens, hidden), low),
            ((tokens, hidden), low),
        ],
        1 + count * parts + 2 * parts,
    )


def chunks(pieces, offs, first, entries, most=512):
    if entries > len(pieces):
        rows = pieces[0].shape[0] // 4
        stripe = 128
        per = most // stripe
        for block in range(4):
            for start in range(0, rows // stripe, per):
                sources = [(0, (4 * (start + i) + block) * stripe, stripe) for i in range(per)]
                yield sources, pl.multiple_of(offs[first + block] + start * stripe, 256), most
        return
    for index, piece in enumerate(pieces):
        for start in range(0, piece.shape[0], most):
            rows = min(most, piece.shape[0] - start)
            yield [(index, start, rows)], pl.multiple_of(offs[first + index] + start, 256), rows


def load_chunk(move, pieces, sources, column, target, at):
    copies = []
    for index, start, rows in sources:
        source = pieces[index].at[pl.ds(start, rows), pl.ds(column, target.shape[1])]
        copies.append(move.start(source, target.at[pl.ds(at, rows), :]))
        at += rows
    return copies


def feed_down_kernel(count, column, entries, offs, bias, y_hbm, m_hbm, *rest):
    pieces, (h_hbm, low_hbm, y_ref, total, h_low, down, sems) = rest[:count], rest[count:]
    move = Copies(sems)
    m_copy = move.start(m_hbm, total)
    parts = []
    at = 0
    for sources, row, rows in chunks(pieces, offs, 1, entries):
        copies = [move.start(y_hbm.at[:, pl.ds(row, rows)], y_ref.at[:, pl.ds(at, rows)])]
        copies += load_chunk(move, pieces, sources, column, down, at)
        parts.append((at, rows, copies))
        at += rows
    m_copy.wait()
    total[...] += bias[...]
    for at, rows, copies in parts:
        wait_all(copies)
        total[...] += dot(y_ref[:, pl.ds(at, rows)], down[pl.ds(at, rows), :])
    move.send(total, h_hbm)
    h_low[...] = total[...].astype(low)
    move.send(h_low, low_hbm)
    move.finish()


def feed_down(offs, acted, middle, bias, pieces):
    pieces, column = pieces
    tokens, hidden = acted.shape
    model = middle.shape[1]
    count = len(pieces)
    return call(
        functools.partial(feed_down_kernel, count, column, offs.shape[0] - 1),
        "feed_down",
        [sized(full, tokens, model), sized(low, tokens, model)],
        [offs],
        [bias],
        [acted, middle, *pieces],
        [
            ((tokens, hidden), low),
            ((tokens, model), full),
            ((tokens, model), low),
            ((hidden, model), low),
        ],
        64,
    )


def feed_back_kernel(entries, ups, downs, outs_count, columns, groups, offs, gain, g_hbm, m_hbm, slope_hbm, *rest):
    up_pieces, rest = rest[:ups], rest[ups:]
    down_pieces, rest = rest[:downs], rest[downs:]
    out_pieces, rest = rest[:outs_count], rest[outs_count:]
    mid_hbm, rest = rest[0], rest[1:]
    outs, rest = rest[:groups], rest[groups:]
    g_ref, m_ref, slope, up, down, out, d_pre, d_second, mixed, sems = rest
    move = Copies(sems)
    g_copy = move.start(g_hbm, g_ref)
    parts = []
    at = 0
    for sources, row, rows in chunks(down_pieces, offs, 1 + ups, entries):
        cols, where = pl.ds(row, rows), pl.ds(at, rows)
        copies = load_chunk(move, down_pieces, sources, columns[1], down, at)
        copies.append(move.start(slope_hbm.at[:, cols], slope.at[:, where]))
        parts.append((where, cols, copies))
        at += rows
    up_loads = move.rows(up_pieces, columns[0], offs, 1, up)[0]
    m_copy = move.start(m_hbm, m_ref)
    out_loads = move.rows(out_pieces, columns[2], offs, 1 + ups + entries, out)[0]
    model = up.shape[0]
    g_copy.wait()
    g = g_ref[...].astype(low)
    for where, cols, copies in parts:
        wait_all(copies)
        d_acted = dot_nt(g, down[where, :])
        d_pre[:, cols] = (d_acted * slope[:, where].astype(full)).astype(low)
    wait_all(up_loads)
    step = 256
    for start in range(0, model, step):
        cols = pl.ds(start, step)
        d_second[:, cols] = dot_nt(d_pre[...], up[cols, :])
    m_copy.wait()
    unit, scale = normalise(m_ref[...])
    grad = g_ref[...].astype(full) + norm_back(unit, scale, gain[...], d_second[...])
    m_ref[...] = grad
    move.send(m_ref, mid_hbm)
    grad = grad.astype(low)
    wait_all(out_loads)
    width = model // groups
    for group in range(groups):
        cols = pl.ds(group * width, width)
        mixed[:, cols] = dot_nt(grad, out[cols, :]).astype(low)
    for step in range(groups):
        at = pl.multiple_of((offs[0] ^ step) * width, width)
        move.send(mixed.at[:, pl.ds(at, width)], outs[step])
    move.finish()


def feed_back(offs, grad, middle, slope, gain, up_pieces, down_pieces, out_pieces, groups):
    (up_pieces, up_column), (down_pieces, down_column) = up_pieces, down_pieces
    out_pieces, out_column = out_pieces
    columns = (up_column, down_column, out_column)
    tokens, model = middle.shape
    hidden = slope.shape[1]
    ups, downs, outs_count = len(up_pieces), len(down_pieces), len(out_pieces)
    result = call(
        functools.partial(feed_back_kernel, offs.shape[0] - 1 - ups - outs_count, ups, downs, outs_count, columns, groups),
        "feed_back",
        [sized(full, tokens, model)] + [sized(low, tokens, model // groups)] * groups,
        [offs],
        [gain],
        [grad, middle, slope, *up_pieces, *down_pieces, *out_pieces],
        [
            ((tokens, model), grad.dtype),
            ((tokens, model), full),
            ((tokens, hidden), low),
            ((model, hidden), low),
            ((hidden, model), low),
            ((model, model), low),
            ((tokens, hidden), low),
            ((tokens, model), full),
            ((tokens, model), low),
        ],
        96,
    )
    return result[0], result[1:]


def adapt_back_kernel(groups, rank, offs, up, a_hbm, u_hbm, *rest):
    grads, rest = rest[:groups], rest[groups:]
    grad_a_hbm, grad_b_hbm, d_inner_hbm, a_ref, u_ref, d_pair, d_inner, grad_a, grad_b, sems = rest
    move = Copies(sems)
    model = a_ref.shape[1]
    width = model // groups
    loads = [move.start(u_hbm, u_ref)]
    for place, kind in enumerate((0, 2)):
        for step in range(groups):
            at = pl.multiple_of(place * model + (offs[0] ^ step) * width, width)
            source = grads[step].at[:, pl.ds(kind * width, width)]
            loads.append(move.start(source, d_pair.at[:, pl.ds(at, width)]))
    a_copy = move.start(a_hbm, a_ref)
    wait_all(loads)
    d_inner[...] = dot_nt(d_pair[...], up[...]).astype(low)
    move.send(d_inner, d_inner_hbm)
    u = u_ref[...]
    lane = lax.broadcasted_iota(jnp.int32, (1, LANES), 1)
    u_query = jnp.where(lane < rank, u, 0).astype(low)
    u_value = jnp.where(lane >= rank, u, 0).astype(low)
    by_rank = dot_tn(u_query, d_pair[:, pl.ds(0, model)]) + dot_tn(u_value, d_pair[:, pl.ds(model, model)])
    grad_b[...] = adapter_scale * by_rank[:8]
    move.send(grad_b, grad_b_hbm)
    a_copy.wait()
    grad_a[...] = dot_tn(d_inner[...], a_ref[...])[:8]
    move.send(grad_a, grad_a_hbm)
    move.finish()


def adapt_back(normed, inner, up, grads, offs, rank):
    groups = len(grads)
    tokens, model = normed.shape
    return call(
        functools.partial(adapt_back_kernel, groups, rank),
        "adapt_back",
        [sized(full, 8, model), sized(full, 8, model), sized(low, tokens, LANES)],
        [offs],
        [up],
        [normed, inner, *grads],
        [
            ((tokens, model), low),
            ((tokens, LANES), low),
            ((tokens, 2 * model), low),
            ((tokens, LANES), low),
            ((8, model), full),
            ((8, model), full),
        ],
        2 + 2 * groups + 3,
    )


def project_back_kernel(count, column, groups, half, offs, gain, down, inner_hbm, mid_hbm, h_hbm, *rest):
    grads, pieces, rest = rest[:groups], rest[groups : groups + count], rest[groups + count :]
    outs, rest = rest[:1], rest[1:]
    d_inner, mid_ref, h_ref, weight, d_all, d_normed, g_low, sems = rest
    move = Copies(sems)
    tokens, model = h_ref.shape
    width = model // groups
    at = pl.multiple_of(offs[1 + count] * tokens, tokens) if half else 0
    mine = pl.ds(at, tokens)
    loads = [move.start(inner_hbm.at[mine, :], d_inner)]
    for kind in range(3):
        for step in range(groups):
            to = pl.multiple_of(kind * model + (offs[0] ^ step) * width, width)
            source = grads[step].at[mine, pl.ds(kind * width, width)]
            loads.append(move.start(source, d_all.at[:, pl.ds(to, width)]))
    weights = move.rows(pieces, column, offs, 1, weight)[0]
    later = [move.start(h_hbm.at[mine, :], h_ref), move.start(mid_hbm.at[mine, :], mid_ref)]
    wait_all(loads)
    wait_all(weights)
    step = 256
    for start in range(0, model, step):
        cols = pl.ds(start, step)
        d_normed[:, cols] = dot_nt(d_all[...], weight[cols, :])
    wait_all(later)
    unit, scale = normalise(h_ref[...].astype(full))
    through = d_normed[...] + dot_nt(d_inner[...], down[...])
    grad = mid_ref[...] + norm_back(unit, scale, gain[...], through)
    g_low[...] = grad.astype(low)
    if half:
        move.send(g_low, outs[0])
    else:
        mid_ref[...] = grad
        move.send(mid_ref, outs[0])
    move.finish()


def project_back(offs, mid, hidden, gain, d_inner, down, grads, pieces, half=False):
    pieces, column = pieces
    groups, count = len(grads), len(pieces)
    tokens, model = hidden.shape
    if half:
        tokens = tokens // 2
    return call(
        functools.partial(project_back_kernel, count, column, groups, half),
        "project_back",
        [sized(low, tokens, model)] if half else [sized(full, tokens, model)],
        [offs],
        [gain, down],
        [d_inner, mid, hidden, *grads, *pieces],
        [
            ((tokens, LANES), low),
            ((tokens, model), full),
            ((tokens, model), hidden.dtype),
            ((model, 3 * model), low),
            ((tokens, 3 * model), low),
            ((tokens, model), full),
            ((tokens, model), low),
        ],
        1 + 3 * groups + count + 2 + 2,
    )[0]


def between_back_kernel(
    qkvs, ups, downs, outs_count, entries, columns, groups, offs, gain, earlier_gain, down_map,
    inner_hbm, mid_hbm, h_hbm, m_hbm, slope_hbm, *rest
):
    grads, rest = rest[:groups], rest[groups:]
    qkv_pieces, rest = rest[:qkvs], rest[qkvs:]
    up_pieces, rest = rest[:ups], rest[ups:]
    down_pieces, rest = rest[:downs], rest[downs:]
    out_pieces, rest = rest[:outs_count], rest[outs_count:]
    mid_out, rest = rest[0], rest[1:]
    outs, rest = rest[:groups], rest[groups:]
    d_inner, g_ref, h_ref, m_ref, qkv, d_all, slope, up, down, out, d_pre, d_second, mixed, sems = rest
    move = Copies(sems)
    tokens, model = h_ref.shape
    width = model // groups
    loads = [move.start(inner_hbm, d_inner)]
    for kind in range(3):
        for step in range(groups):
            to = pl.multiple_of(kind * model + (offs[0] ^ step) * width, width)
            source = grads[step].at[:, pl.ds(kind * width, width)]
            loads.append(move.start(source, d_all.at[:, pl.ds(to, width)]))
    loads += move.rows(qkv_pieces, columns[3], offs, 1, qkv)[0]
    later = [move.start(h_hbm, h_ref), move.start(mid_hbm, g_ref)]
    parts = []
    at = 0
    first = 1 + qkvs
    for sources, row, rows in chunks(down_pieces, offs, first + ups, entries):
        cols, where = pl.ds(row, rows), pl.ds(at, rows)
        copies = load_chunk(move, down_pieces, sources, columns[1], down, at)
        copies.append(move.start(slope_hbm.at[:, cols], slope.at[:, where]))
        parts.append((where, cols, copies))
        at += rows
    up_loads = move.rows(up_pieces, columns[0], offs, first, up)[0]
    m_copy = move.start(m_hbm, m_ref)
    out_loads = move.rows(out_pieces, columns[2], offs, first + ups + entries, out)[0]
    wait_all(loads)
    step = 256
    for start in range(0, model, step):
        cols = pl.ds(start, step)
        d_second[:, cols] = dot_nt(d_all[...], qkv[cols, :])
    wait_all(later)
    unit, scale = normalise(h_ref[...])
    through = d_second[...] + dot_nt(d_inner[...], down_map[...])
    g_ref[...] = g_ref[...] + norm_back(unit, scale, gain[...], through)
    g = g_ref[...].astype(low)
    for where, cols, copies in parts:
        wait_all(copies)
        d_acted = dot_nt(g, down[where, :])
        d_pre[:, cols] = (d_acted * slope[:, where].astype(full)).astype(low)
    wait_all(up_loads)
    for start in range(0, model, step):
        cols = pl.ds(start, step)
        d_second[:, cols] = dot_nt(d_pre[...], up[cols, :])
    m_copy.wait()
    unit, scale = normalise(m_ref[...])
    grad = g_ref[...] + norm_back(unit, scale, earlier_gain[...], d_second[...])
    m_ref[...] = grad
    move.send(m_ref, mid_out)
    grad = grad.astype(low)
    wait_all(out_loads)
    for group in range(groups):
        cols = pl.ds(group * width, width)
        mixed[:, cols] = dot_nt(grad, out[cols, :]).astype(low)
    for step in range(groups):
        at = pl.multiple_of((offs[0] ^ step) * width, width)
        move.send(mixed.at[:, pl.ds(at, width)], outs[step])
    move.finish()


def between_back(
    offs, entries, mid, hidden, gain, d_inner, down_map, grads, qkv_pieces,
    middle, slope, earlier_gain, up_pieces, down_pieces, out_pieces
):
    (qkv_pieces, qkv_column), (up_pieces, up_column) = qkv_pieces, up_pieces
    (down_pieces, down_column), (out_pieces, out_column) = down_pieces, out_pieces
    columns = (up_column, down_column, out_column, qkv_column)
    tokens, model = middle.shape
    hidden_width, groups = slope.shape[1], len(grads)
    counts = [len(p) for p in (qkv_pieces, up_pieces, down_pieces, out_pieces)]
    result = call(
        functools.partial(between_back_kernel, *counts, entries, columns, groups),
        "between_back",
        [sized(full, tokens, model)] + [sized(low, tokens, model // groups)] * groups,
        [offs],
        [gain, earlier_gain, down_map],
        [d_inner, mid, hidden, middle, slope, *grads]
        + [*qkv_pieces, *up_pieces, *down_pieces, *out_pieces],
        [
            ((tokens, LANES), low),
            ((tokens, model), full),
            ((tokens, model), full),
            ((tokens, model), full),
            ((model, 3 * model), low),
            ((tokens, 3 * model), low),
            ((tokens, hidden_width), low),
            ((model, hidden_width), low),
            ((hidden_width, model), low),
            ((model, model), low),
            ((tokens, hidden_width), low),
            ((tokens, model), full),
            ((tokens, model), low),
        ],
        128,
    )
    return result[0], result[1:]


BLOCK = 256


def causal_corner(block):
    keys = lax.broadcasted_iota(jnp.int32, (block, block), 0)
    return keys <= lax.broadcasted_iota(jnp.int32, (block, block), 1)


def head_masks():
    lane = lax.broadcasted_iota(jnp.int32, (1, LANES), 1)
    return [(lane < HEAD).astype(low), (lane >= HEAD).astype(low)]


def attend_kernel(groups, offs, *rest):
    pieces, rest = rest[:groups], rest[groups:]
    outs, (o_hbm, lse_hbm), rest = rest[:groups], rest[groups : groups + 2], rest[groups + 2 :]
    qkv, v_turned, o_turned, o_ref, lse, sems = rest
    move = Copies(sems)
    member = offs[0]
    count, width3 = pieces[0].shape
    width = width3 // 3
    length = count * groups
    pairs = width // LANES
    block = min(BLOCK, length)
    places = [
        pl.ds(pl.multiple_of((member ^ step) * count, count), count) for step in range(groups)
    ]
    loads = []
    for pair in range(pairs):
        row = []
        for kind in (2, 1, 0):
            cols = pl.ds(kind * width + pair * LANES, LANES)
            for step in range(groups):
                row.append(move.start(pieces[step].at[:, cols], qkv.at[places[step], cols]))
        loads.append(row)
    keep = head_masks()
    causal = causal_corner(block)
    if lse.shape[0] > 2 * pairs:
        lse[...] = jnp.zeros_like(lse)
    for pair in range(pairs):
        at = pair * LANES
        here = pl.ds(at, LANES)
        wait_all(loads[pair])
        v_turned[...] = qkv[:, pl.ds(2 * width + at, LANES)].T
        for start in range(0, length, block):
            rows = pl.ds(start, block)
            upto = start + block
            q = qkv[rows, here]
            k = qkv[pl.ds(0, upto), pl.ds(width + at, LANES)]
            scores = [dot_nt(k, q * (keep[head] * 0.125)) for head in range(2)]
            for head in range(2):
                where = pl.ds(head * HEAD, HEAD)
                value = scores[head]
                corner = jnp.where(causal, value[start:], -1e30)
                value = jnp.concatenate([value[:start], corner], axis=0) if start else corner
                top = jnp.max(value, axis=0, keepdims=True)
                weights = jnp.exp(value - top)
                total = jnp.sum(weights, axis=0, keepdims=True)
                mixed = dot(v_turned[where, pl.ds(0, upto)], weights.astype(low))
                o_turned[where, rows] = (mixed * (1.0 / total)).astype(low)
                lse[pl.ds(2 * pair + head, 1), rows] = top + jnp.log(total)
        o_ref[:, here] = o_turned[...].T
        move.send(o_ref.at[:, here], o_hbm.at[:, here])
        for step in range(groups):
            move.send(o_ref.at[places[step], here], outs[step].at[:, here])
    move.send(lse, lse_hbm)
    move.finish()


def attend(offs, pieces):
    groups = len(pieces)
    count, width3 = pieces[0].shape
    width, length = width3 // 3, count * groups
    heads = max(8, width // HEAD)
    pairs = width // LANES
    result = call(
        functools.partial(attend_kernel, groups),
        "attend",
        [sized(low, count, width)] * groups + [sized(low, length, width), sized(full, heads, length)],
        [offs],
        [],
        pieces,
        [
            ((length, width3), low),
            ((LANES, length), low),
            ((LANES, length), low),
            ((length, width), low),
            ((heads, length), full),
        ],
        pairs * (4 * groups + 1) + 1,
    )
    return result[:groups], result[groups], result[groups + 1]


def attend_back_kernel(groups, offs, o_hbm, lse_hbm, *rest):
    pieces, grads, rest = rest[:groups], rest[groups : 2 * groups], rest[2 * groups :]
    outs, rest = rest[:groups], rest[groups:]
    qkv, d_out, o_ref, lse, k_turned, q_turned, result, inner, sum_k, sum_v, sems = rest
    move = Copies(sems)
    member = offs[0]
    count, width3 = pieces[0].shape
    width = width3 // 3
    length = count * groups
    pairs = width // LANES
    block = min(BLOCK, length)
    places = [
        pl.ds(pl.multiple_of((member ^ step) * count, count), count) for step in range(groups)
    ]
    first = [move.start(grads[step], d_out.at[places[step], :]) for step in range(groups)]
    first.append(move.start(o_hbm, o_ref))
    loads = []
    for kind in (1, 0, 2):
        cols = pl.ds(kind * width, width)
        loads.append(
            [move.start(pieces[i].at[:, cols], qkv.at[places[i], cols]) for i in range(groups)]
        )
    lse_copy = move.start(lse_hbm, lse)
    keep = head_masks()
    causal = causal_corner(block)
    heads = lse.shape[0]
    of_head = (
        lax.broadcasted_iota(jnp.int32, (heads, width), 1) // HEAD
        == lax.broadcasted_iota(jnp.int32, (heads, width), 0)
    ).astype(low)
    wait_all(first)
    product = d_out[...].astype(full) * o_ref[...].astype(full)
    high = product.astype(low)
    rest_of = (product - high.astype(full)).astype(low)
    inner[...] = dot_nt(of_head, high) + dot_nt(of_head, rest_of)
    wait_all(loads[0])
    k_turned[...] = qkv[:, pl.ds(width, width)].T
    wait_all(loads[1])
    wait_all(loads[2])
    lse_copy.wait()

    def pair_step(pair):
        at = pair * LANES
        for start in reversed(range(0, length, block)):
            rows = pl.ds(start, block)
            upto = start + block
            past = pl.ds(0, upto)
            q = qkv[rows, pl.ds(at, LANES)]
            d = d_out[rows, pl.ds(at, LANES)]
            k = qkv[past, pl.ds(width + at, LANES)]
            v = qkv[past, pl.ds(2 * width + at, LANES)]
            q_heads = [q * (keep[head] * 0.125) for head in range(2)]
            d_heads = [d * keep[head] for head in range(2)]
            scores = [dot_nt(k, q_heads[head]) for head in range(2)]
            d_probs = [dot_nt(v, d_heads[head]) for head in range(2)]
            more_k = more_v = None
            for head in range(2):
                line = pl.ds(2 * pair + head, 1)
                probs = jnp.exp(scores[head] - lse[line, rows])
                corner = jnp.where(causal, probs[start:], 0.0)
                probs = jnp.concatenate([probs[:start], corner], axis=0) if start else corner
                d_scores = (probs * (d_probs[head] - inner[line, rows])).astype(low)
                part_v = dot(probs.astype(low), d_heads[head])
                part_k = dot(d_scores, q_heads[head])
                more_v = part_v if more_v is None else more_v + part_v
                more_k = part_k if more_k is None else more_k + part_k
                where = pl.ds(at + head * HEAD, HEAD)
                q_turned[where, rows] = (0.125 * dot(k_turned[where, past], d_scores)).astype(low)
            if upto == length:
                sum_v[...] = more_v
                sum_k[...] = more_k
            else:
                sum_v[past, :] += more_v
                sum_k[past, :] += more_k
        result[:, pl.ds(width + at, LANES)] = sum_k[...].astype(low)
        result[:, pl.ds(2 * width + at, LANES)] = sum_v[...].astype(low)

    for pair in range(pairs):
        pair_step(pair)
    result[:, pl.ds(0, width)] = q_turned[...].T
    for step in range(groups):
        move.send(result.at[places[step], :], outs[step])
    move.finish()


def attend_back(offs, pieces, grads, mixed, lse):
    groups = len(pieces)
    count, width3 = pieces[0].shape
    width, length = width3 // 3, count * groups
    heads = lse.shape[0]
    return call(
        functools.partial(attend_back_kernel, groups),
        "attend_back",
        [sized(low, count, width3)] * groups,
        [offs],
        [],
        [mixed, lse, *pieces, *grads],
        [
            ((length, width3), low),
            ((length, width), low),
            ((length, width), low),
            ((heads, length), full),
            ((width, length), low),
            ((width, length), low),
            ((length, width3), low),
            ((heads, length), full),
            ((length, LANES), full),
            ((length, LANES), full),
        ],
        5 * groups + 2,
    )


def reshard_perms(sp_size, dp_size):
    quarter = sp_size // 4
    perms = []
    for part in range(2):
        perm = []
        for s in range(sp_size):
            for d in range(dp_size):
                doc = 2 * (d & 1) + ((s & 1) ^ part)
                member = s >> 1
                target_sp = doc * quarter + (member >> 1)
                target_dp = 2 * (d >> 1) + (member & 1)
                perm.append((s * dp_size + d, target_sp * dp_size + target_dp))
        perms.append(perm)
    return perms


def member_perm(sp_size, dp_size, step):
    quarter = sp_size // 4
    perm = []
    for s in range(sp_size):
        for d in range(dp_size):
            doc, high = s // quarter, s % quarter
            member = (2 * high + (d & 1)) ^ step
            target_sp = doc * quarter + (member >> 1)
            target_dp = 2 * (d >> 1) + (member & 1)
            perm.append((s * dp_size + d, target_sp * dp_size + target_dp))
    return perm


class Plan:
    def __init__(self, sp_size, dp_size):
        self.sp_size, self.dp_size = sp_size, dp_size
        self.members = sp_size // 2
        self.perms = reshard_perms(sp_size, dp_size)
        self.back = [[(b, a) for a, b in perm] for perm in self.perms]
        self.s = lax.axis_index("sp")
        self.d = lax.axis_index("dp")
        quarter = sp_size // 4
        self.doc = self.s // quarter
        self.member = 2 * (self.s % quarter) + (self.d & 1)

    def gather_start(self, blocks):
        got = []
        for part in range(2):
            block = lax.dynamic_index_in_dim(blocks, (self.s & 1) ^ part, 0, keepdims=False)
            got.append(lax.ppermute(block, ("sp", "dp"), self.perms[part]))
        return got

    def gather_finish(self, got):
        flip = (self.doc & 1) == 1
        first = jnp.where(flip, got[1], got[0])
        second = jnp.where(flip, got[0], got[1])
        return jnp.concatenate([first, second], axis=0)

    def gather_doc(self, blocks):
        return self.gather_finish(self.gather_start(blocks))

    def scatter_start(self, rows):
        half = rows.shape[0] // 2
        blocks = rows.reshape(2, half, rows.shape[1])
        got = []
        for part in range(2):
            block = lax.dynamic_index_in_dim(blocks, (self.doc & 1) ^ part, 0, keepdims=False)
            got.append(lax.ppermute(block, ("sp", "dp"), self.back[part]))
        return got

    def scatter_finish(self, got):
        flip = (self.s & 1) == 1
        first = jnp.where(flip, got[1], got[0])
        second = jnp.where(flip, got[0], got[1])
        return jnp.stack([first, second])

    def scatter_doc(self, rows):
        return self.scatter_finish(self.scatter_start(rows))

    def swap(self, parts):
        out = [parts[0]]
        for step in range(1, self.members):
            perm = member_perm(self.sp_size, self.dp_size, step)
            out.append(lax.ppermute(parts[step], ("sp", "dp"), perm))
        return out


def add_from(value, step, total):
    return value + lax.ppermute(value, ("sp", "dp"), [(i, i ^ step) for i in range(total)])


def after(value, *earlier):
    return lax.optimization_barrier((value, *earlier))[0]


class Clock:
    def __init__(self):
        self.event = ()

    def tick(self, *values):
        self.event = values

    def tied(self, *values):
        if not self.event:
            return values if len(values) > 1 else values[0]
        got = lax.optimization_barrier((*values, *self.event))[: len(values)]
        return got if len(values) > 1 else got[0]


class Fetch:
    def __init__(self, plan, clock, shard):
        self.plan, self.clock = plan, clock
        self.whole = plan.sp_size != 4
        shard = clock.tied(shard)
        if self.whole:
            self.block = lax.all_gather(shard, ("sp", "dp"), axis=0, tiled=True)
            self.side = self.corner = self.block
            return
        self.block = lax.all_gather(shard, "dp", axis=0, tiled=True)
        sp_size, dp_size = plan.sp_size, plan.dp_size
        self.over_core = [(i, i ^ 1) for i in range(dp_size)]
        places = [(s, d) for s in range(sp_size) for d in range(dp_size)]
        self.first_way = [(s * dp_size + d, (s ^ (1 << (d & 1))) * dp_size + d) for s, d in places]
        self.second_way = [(s * dp_size + d, (s ^ (2 >> (d & 1))) * dp_size + d) for s, d in places]

    def split(self, columns):
        both = []
        for cols in (slice(None, columns), slice(columns, None)):
            part = object.__new__(Fetch)
            part.__dict__.update(self.__dict__)
            part.block = self.block[:, cols]
            if self.whole:
                part.side = part.corner = part.block
            both.append(part)
        return both

    def near(self):
        if not self.whole:
            block = self.clock.tied(self.block)
            self.side = lax.ppermute(block, ("sp", "dp"), self.first_way)

    def far(self):
        if self.whole:
            return
        rows = self.block.shape[0]
        self.side = self.clock.tied(self.side)
        half = lax.dynamic_slice_in_dim(self.side, (self.plan.d & 1) * (rows // 2), rows // 2, axis=0)
        self.corner = lax.ppermute(half, ("sp", "dp"), self.second_way)
        self.other_side = lax.ppermute(self.side, "dp", self.over_core)

    def pieces(self):
        plan = self.plan
        if self.whole:
            return [self.block], [0]
        corner = self.clock.tied(self.corner)
        other_corner = lax.ppermute(corner, "dp", self.over_core)
        rows = self.block.shape[0]
        s, core = plan.s, plan.d & 1
        half = rows // 2
        starts = [
            s * rows,
            (s ^ (1 << core)) * rows,
            (s ^ (2 >> core)) * rows,
            (s ^ 3) * rows + core * half,
            (s ^ 3) * rows + (1 - core) * half,
        ]
        return [self.block, self.side, self.other_side, corner, other_corner], starts


class Wide:
    def __init__(self, plan, clock, shard):
        self.plan, self.clock = plan, clock
        self.whole = plan.sp_size != 4
        shard = clock.tied(shard)
        self.parts = [shard]
        if not self.whole:
            for step in range(1, 4):
                way = [(i, i ^ step) for i in range(4)]
                self.parts.append(lax.ppermute(shard, "sp", way))

    def gather(self):
        parts = self.clock.tied(*self.parts) if len(self.parts) > 1 else self.parts
        axes = ("sp", "dp") if self.whole else "dp"
        self.block = lax.all_gather(jnp.concatenate(parts), axes, axis=0, tiled=True)

    def pieces(self):
        if self.whole:
            return [self.block], [0]
        rows = self.block.shape[0] // 4
        return [self.block], [(self.plan.s ^ step) * rows for step in range(4)]


def on_device(
    tokens,
    cotangent,
    layer_norm_gain,
    layer_norm_bias,
    query_key_value_weight,
    query_value_bias,
    attention_out_weight,
    output_projection_bias,
    feed_up_weight,
    feed_up_bias,
    feed_down_weight,
    adapter_down_maps,
    adapter_up_weights,
):
    layers = query_key_value_weight.shape[0]
    model = tokens.shape[2]
    rank = adapter_down_maps.shape[3]
    plan = Plan(lax.axis_size("sp"), lax.axis_size("dp"))
    clock = Clock()
    groups = plan.members
    member = plan.member.astype(jnp.int32)

    def table(*entries):
        return jnp.stack([jnp.asarray(entry, jnp.int32) for entry in entries])

    adapters = []
    for layer in range(layers):
        down = jnp.concatenate([adapter_down_maps[layer, 0], adapter_down_maps[layer, 1]], axis=1)
        down = jnp.pad(down, ((0, 0), (0, LANES - 2 * rank)))
        up = adapter_up_weights[layer] * jnp.asarray(adapter_scale, low)
        up = jnp.concatenate(
            [
                jnp.pad(up[0], ((0, LANES - rank), (0, 0))),
                jnp.pad(up[1], ((rank, LANES - 2 * rank), (0, 0))),
            ],
            axis=1,
        )
        adapters.append((down, up))

    def request(layer, *kinds):
        shards = []
        for kind in kinds:
            if kind == 0:
                shards.append(query_key_value_weight[layer])
            elif kind == 1:
                shards += [attention_out_weight[layer], feed_up_weight[layer]]
            else:
                shards.append(feed_down_weight[layer])
        shard = jnp.concatenate(shards, axis=1) if len(shards) > 1 else shards[0]
        return Fetch(plan, clock, shard)

    saved, outputs = [], []
    ready = {}
    qkv_fetch = request(0, 0)
    wide = Wide(plan, clock, feed_down_weight[layers - 1])
    sent = plan.gather_start(tokens)
    clock.tick(*wide.parts, *sent)
    hidden = plan.gather_finish(clock.tied(*sent))
    clock.tick(hidden)
    out_fetch = request(0, 1)
    down_fetch = request(0, 2)
    clock.tick(*wide.parts)
    qkv_fetch.near()
    clock.tick(hidden)
    qkv_fetch.far()
    clock.tick(qkv_fetch.side)
    out_fetch.near()
    for layer in range(layers):
        last = layer + 1 == layers
        gain, shift = layer_norm_gain[layer], layer_norm_bias[layer]
        down, up = adapters[layer]
        clock.tick(hidden, qkv_fetch.corner)
        ready[layer, 0] = qkv_fetch.pieces()
        if not last:
            following = request(layer + 1, 0, 1)
        qkv, starts = ready[layer, 0]
        offs = table(member, *starts)
        bias = query_value_bias[layer].reshape(1, 2 * model)
        clock.tick(out_fetch.block)
        parts, inner, normed = project(
            offs, clock.tied(hidden), gain[:1], shift[:1], bias, down, up, (qkv, 0), groups
        )
        clock.tick(*parts)
        out_fetch.far()
        if not last:
            clock.tick(out_fetch.side, *parts)
            if layer + 2 == layers:
                wide.gather()
                next_down = wide
            else:
                next_down = request(layer + 1, 2)
        parts = plan.swap(parts)
        clock.tick(out_fetch.side)
        if not last:
            down_fetch.near()
        parts[0] = clock.tied(parts[0])
        mixed_parts, mixed, lse = attend(offs, parts)
        clock.tick(mixed)
        mixed_parts = plan.swap(mixed_parts)
        clock.tick(mixed, out_fetch.corner)
        ready[layer, 1] = out_fetch.pieces()
        out_up, starts = ready[layer, 1]
        if not last:
            clock.tick(down_fetch.side)
            mixed_parts[0] = clock.tied(mixed_parts[0])
        offs = table(member, *starts)
        middle, second = mix(
            offs,
            hidden,
            output_projection_bias[layer, :1],
            gain[1:],
            shift[1:],
            mixed_parts,
            (out_up, 0),
        )
        if not last:
            down_fetch.far()
            clock.tick(down_fetch.side)
            next_qkv, next_out = following.split(3 * model)
            next_qkv.near()
            clock.tick(next_qkv.block)
        acted, slope = feed_up(
            offs, clock.tied(second), feed_up_bias[layer : layer + 1], (out_up, model)
        )
        clock.tick(acted)
        if last:
            sent = clock.tied(*plan.gather_start(after(cotangent, second)))
            grad = plan.gather_finish(sent)
        else:
            next_out.near()
            clock.tick(acted, down_fetch.corner)
        ready[layer, 2] = down_fetch.pieces()
        saved.append((hidden, normed, inner, parts, mixed, lse, middle, acted, slope))
        down_w, starts = ready[layer, 2]
        if not last:
            clock.tick(next_out.block)
            hidden, after_low = feed_down(
                table(member, *starts),
                clock.tied(acted),
                middle,
                output_projection_bias[layer, 1:],
                (down_w, 0),
            )
            clock.tick(hidden)
            next_qkv.far()
            outputs.append(plan.scatter_start(after_low))
            qkv_fetch, out_fetch, down_fetch = next_qkv, next_out, next_down
    sums = [None] * layers
    waiting = outputs.pop()
    for layer in reversed(range(layers)):
        hidden, normed, inner, parts, mixed, lse, middle, acted, slope = saved[layer]
        gain = layer_norm_gain[layer]
        down, up = adapters[layer]
        (qkv, starts), (out_up, starts_up) = ready[layer, 0], ready[layer, 1]
        down_w, starts_down = ready[layer, 2]
        offs = table(member, *starts)
        if layer + 1 < layers:
            later_qkv, later_starts = ready[layer + 1, 0]
            mid, d_mixed = between_back(
                table(member, *later_starts, *starts_up, *starts_down, *starts_up),
                len(starts_down),
                mid,
                saved[layer + 1][0],
                layer_norm_gain[layer + 1, :1],
                d_inner,
                adapters[layer + 1][0],
                grads,
                (later_qkv, 0),
                middle,
                slope,
                gain[1:],
                (out_up, model),
                (down_w, 0),
                (out_up, 0),
            )
        else:
            mid, d_mixed = feed_back(
                table(member, *starts_up, *starts_down, *starts_up),
                grad,
                middle,
                slope,
                gain[1:],
                (out_up, model),
                (down_w, 0),
                (out_up, 0),
                groups,
            )
        d_mixed = plan.swap(d_mixed)
        if layer + 1 == layers:
            _, after_low = feed_down(
                table(member, *starts_down),
                after(acted, mid),
                middle,
                output_projection_bias[layer, 1:],
                (down_w, 0),
            )
            outputs_late = [plan.scatter_start(after_low)]
            d_mixed[0] = after(d_mixed[0], after_low)
        grads = list(attend_back(offs, parts, d_mixed, mixed, lse))
        if waiting:
            grads[1], *arrived = lax.optimization_barrier((grads[1], *waiting))
            outputs.append(arrived)
        if outputs_late:
            waiting = outputs_late.pop()
        else:
            waiting = []
        grads = plan.swap(grads)
        grad_a, grad_b, d_inner = adapt_back(normed, inner, up, grads, offs, rank)
        sums[layer] = jnp.concatenate([grad_a, grad_b])
        if layer:
            d_inner = after(d_inner, grad_a)
    total = jnp.stack(sums)
    flat = plan.sp_size * plan.dp_size
    bits = [1 << bit for bit in range(flat.bit_length() - 1)]
    steps = [1] + [bit for bit in bits if bit >= plan.dp_size]
    steps += [bit for bit in bits if 1 < bit < plan.dp_size]
    for step in steps[:1]:
        total = add_from(total, step, flat)
    sent = []
    for half in range(2):
        if half + 1 < len(steps):
            total = add_from(total, steps[half + 1], flat)
        which = (plan.doc & 1) ^ half
        back = project_back(
            table(member, *starts, which),
            mid,
            hidden,
            gain[:1],
            d_inner,
            down,
            grads,
            (qkv, 0),
            half=True,
        )
        total, back = lax.optimization_barrier((total, back))
        sent.append(lax.ppermute(back, ("sp", "dp"), plan.back[half]))
        d_inner = after(d_inner, back)
    for step in steps[3:]:
        total = add_from(total, step, flat)
    grad_tokens = plan.scatter_finish(sent).astype(full)
    total = total.reshape(layers, 2, 8, model)[:, :, : 2 * rank]
    total = total.reshape(layers, 2, 2, rank, model)
    outputs = [plan.scatter_finish(got).astype(full) for got in outputs]
    return (jnp.stack(outputs), grad_tokens, total[:, 0].swapaxes(-1, -2), total[:, 1])


def solution(mesh):
    in_specs = (
        P("dp", "sp", None),
        P("dp", "sp", None),
        P(),
        P(),
        P(None, ("sp", "dp"), None),
        P(),
        P(None, ("sp", "dp"), None),
        P(),
        P(None, ("sp", "dp"), None),
        P(),
        P(None, ("sp", "dp"), None),
        P(),
        P(),
    )
    out_specs = (P(None, "dp", "sp", None), P("dp", "sp", None), P(), P())
    return jax.shard_map(
        on_device, mesh=mesh, in_specs=in_specs, out_specs=out_specs, check_vma=False
    )
```

```python
import functools
import jax
import jax.numpy as jnp
from jax import lax
from jax.experimental import pallas as pl
from jax.experimental.pallas import tpu as pltpu
from jax.sharding import PartitionSpec as P

HEAD = 64
LANES = 128
adapter_scale = 8.0
VMEM_BYTES = 58 * 1024 * 1024
BACK_VMEM_BYTES = 50 * 1024 * 1024
low = jnp.bfloat16
full = jnp.float32


def dot(left, right):
    return jnp.dot(left, right, preferred_element_type=full)


def dot_nt(left, right):
    return lax.dot_general(left, right, (((1,), (1,)), ((), ())), preferred_element_type=full)


def dot_tn(left, right):
    return lax.dot_general(left, right, (((0,), (0,)), ((), ())), preferred_element_type=full)


def normalise(value):
    center = value - jnp.mean(value, axis=-1, keepdims=True)
    scale = lax.rsqrt(jnp.mean(center * center, axis=-1, keepdims=True) + 1e-05)
    return center * scale, scale


def norm_back(unit, scale, gain, grad):
    grad = grad * gain
    inner = jnp.mean(grad * unit, axis=-1, keepdims=True)
    return scale * (grad - jnp.mean(grad, axis=-1, keepdims=True) - unit * inner)


def vmem():
    return pl.BlockSpec(memory_space=pltpu.VMEM)


def hbm():
    return pl.BlockSpec(memory_space=pl.ANY)


def smem():
    return pl.BlockSpec(memory_space=pltpu.SMEM)


def brief():
    return pl.CostEstimate(flops=1000, bytes_accessed=1000, transcendentals=0)


def params(name):
    back = name.endswith("_back")
    return pltpu.CompilerParams(vmem_limit_bytes=BACK_VMEM_BYTES if back else VMEM_BYTES)


class Copies:
    def __init__(self, sems):
        self.sems, self.used, self.open = sems, 0, []

    def start(self, source, target):
        copy = pltpu.make_async_copy(source, target, self.sems.at[self.used])
        self.used += 1
        copy.start()
        return copy

    def send(self, source, target):
        self.open.append(self.start(source, target))

    def finish(self):
        for copy in self.open:
            copy.wait()

    def rows(self, pieces, column, offsets, first, target, parts=1):
        width = target.shape[1] // parts
        result = []
        for part in range(parts):
            cols = pl.ds(part * width, width)
            source = pl.ds(column + part * width, width)
            row = []
            for index, piece in enumerate(pieces):
                start = pl.multiple_of(offsets[first + index], 64)
                rows = pl.ds(start, piece.shape[0])
                row.append(self.start(piece.at[:, source], target.at[rows, cols]))
            result.append(row)
        return result


def wait_all(copies):
    while copies:
        copies.pop(0).wait()


def call(kernel, name, outs, scalars, small, large, scratch, sems):
    return pl.pallas_call(
        kernel,
        out_shape=outs,
        in_specs=[smem()] * len(scalars) + [vmem()] * len(small) + [hbm()] * len(large),
        out_specs=[hbm()] * len(outs),
        scratch_shapes=[pltpu.VMEM(shape, kind) for shape, kind in scratch]
        + [pltpu.SemaphoreType.DMA((sems,))],
        compiler_params=params(name),
        cost_estimate=brief(),
        name=name,
    )(*scalars, *small, *large)


def sized(kind, *shape):
    return jax.ShapeDtypeStruct(shape, kind)


def project_kernel(count, column, groups, offs, gain, shift, bias, down, up, h_hbm, *rest):
    pieces, rest = rest[:count], rest[count:]
    outs, (u_hbm, a_hbm), rest = rest[:groups], rest[groups : groups + 2], rest[groups + 2 :]
    h_ref, weight, result, a_ref, u_ref, sems = rest
    move = Copies(sems)
    h_copy = move.start(h_hbm, h_ref)
    parts = 3 * groups
    loads = move.rows(pieces, column, offs, 1, weight, parts)
    member = offs[0]
    model = h_ref.shape[1]
    width = model // groups
    h_copy.wait()
    unit, _ = normalise(h_ref[...].astype(full))
    a = (unit * gain[...] + shift[...]).astype(low)
    a_ref[...] = a
    move.send(a_ref, a_hbm)
    u = dot(a, down[...]).astype(low)
    u_ref[...] = u
    move.send(u_ref, u_hbm)
    for part in range(parts):
        kind, group = part // groups, part % groups
        wait_all(loads[part])
        cols = pl.ds(part * width, width)
        value = dot(a, weight[:, cols])
        if kind != 1:
            at = pl.ds((kind // 2) * model + group * width, width)
            value = value + bias[:, at] + dot(u, up[:, at])
        result[:, cols] = value.astype(low)
        if group + 1 == groups:
            for step in range(groups):
                source = pl.multiple_of(kind * model + (member ^ step) * width, width)
                move.send(result.at[:, pl.ds(source, width)], outs[step].at[:, pl.ds(kind * width, width)])
    move.finish()


def project(offs, hidden, gain, shift, bias, down, up, pieces, groups):
    pieces, column = pieces
    tokens, model = hidden.shape
    outs = [sized(low, tokens, 3 * model // groups)] * groups
    outs += [sized(low, tokens, LANES), sized(low, tokens, model)]
    count = len(pieces)
    result = call(
        functools.partial(project_kernel, count, column, groups),
        "project",
        outs,
        [offs],
        [gain, shift, bias, down, up],
        [hidden, *pieces],
        [
            ((tokens, model), hidden.dtype),
            ((model, 3 * model), low),
            ((tokens, 3 * model), low),
            ((tokens, model), low),
            ((tokens, LANES), low),
        ],
        1 + count * 3 * groups + 2 + 3 * groups,
    )
    return result[:groups], result[groups], result[groups + 1]


def mix_kernel(count, column, groups, offs, bias, gain, shift, h_hbm, *rest):
    mixed, pieces, rest = rest[:groups], rest[groups : groups + count], rest[groups + count :]
    m_hbm, c_hbm, h_ref, o_ref, weight, m_ref, c_ref, sems = rest
    move = Copies(sems)
    width = mixed[0].shape[1]
    loads = []
    for step in range(groups):
        at = pl.multiple_of((offs[0] ^ step) * width, width)
        loads.append(move.start(mixed[step], o_ref.at[:, pl.ds(at, width)]))
    loads += move.rows(pieces, column, offs, 1, weight)[0]
    loads.append(move.start(h_hbm, h_ref))
    wait_all(loads)
    step = h_ref.shape[0] // 2
    for start in (0, step):
        rows = pl.ds(start, step)
        total = h_ref[rows, :].astype(full) + (dot(o_ref[rows, :], weight[...]) + bias[...])
        m_ref[rows, :] = total
        move.send(m_ref.at[rows, :], m_hbm.at[rows, :])
        unit, _ = normalise(total)
        c_ref[rows, :] = (unit * gain[...] + shift[...]).astype(low)
        move.send(c_ref.at[rows, :], c_hbm.at[rows, :])
    move.finish()


def mix(offs, hidden, bias, gain, shift, mixed, pieces):
    pieces, column = pieces
    groups, count = len(mixed), len(pieces)
    tokens, model = hidden.shape
    return call(
        functools.partial(mix_kernel, count, column, groups),
        "mix",
        [sized(full, tokens, model), sized(low, tokens, model)],
        [offs],
        [bias, gain, shift],
        [hidden, *mixed, *pieces],
        [
            ((tokens, model), hidden.dtype),
            ((tokens, model), low),
            ((model, model), low),
            ((tokens, model), full),
            ((tokens, model), low),
        ],
        1 + groups + count + 4,
    )


SOME = 128
ROOT = 0.7978845608028654
CUBE = 0.044715


def feed_up_kernel(count, column, parts, offs, up_bias, c_hbm, *rest):
    pieces, (acted_hbm, slope_hbm, c_ref, up, acted, slope, sems) = rest[:count], rest[count:]
    move = Copies(sems)
    c_copy = move.start(c_hbm, c_ref)
    loads = move.rows(pieces, column, offs, 1, up, parts)
    width = up.shape[1] // parts
    c_copy.wait()
    tokens = c_ref.shape[0]
    some = min(tokens, SOME)
    for part in range(parts):
        cols = pl.ds(part * width, width)
        wait_all(loads[part])
        for start in range(0, tokens, some):
            rows = pl.ds(start, some)
            z = dot(c_ref[rows, :], up[:, cols]) + up_bias[:, cols]
            square = z * z
            t = jnp.tanh(z * (ROOT + (ROOT * CUBE) * square))
            half = 0.5 + 0.5 * t
            acted[rows, cols] = (z * half).astype(low)
            slope[rows, cols] = (
                half + z * (1.0 - t * t) * (0.5 * ROOT + (1.5 * ROOT * CUBE) * square)
            ).astype(low)
        move.send(acted.at[:, cols], acted_hbm.at[:, cols])
        move.send(slope.at[:, cols], slope_hbm.at[:, cols])
    move.finish()


def feed_up(offs, second, up_bias, pieces):
    pieces, column = pieces
    tokens, model = second.shape
    hidden = up_bias.shape[1]
    count, parts = len(pieces), 4
    return call(
        functools.partial(feed_up_kernel, count, column, parts),
        "feed_up",
        [sized(low, tokens, hidden)] * 2,
        [offs],
        [up_bias],
        [second, *pieces],
        [
            ((tokens, model), low),
            ((model, hidden), low),
            ((tokens, hidden), low),
            ((tokens, hidden), low),
        ],
        1 + count * parts + 2 * parts,
    )


def chunks(pieces, offs, first, entries, most=1024):
    if entries > len(pieces):
        rows = pieces[0].shape[0] // 4
        stripe = 128
        per = most // stripe
        for block in range(4):
            for start in range(0, rows // stripe, per):
                sources = [(0, (4 * (start + i) + block) * stripe, stripe) for i in range(per)]
                yield sources, pl.multiple_of(offs[first + block] + start * stripe, 256), most
        return
    for index, piece in enumerate(pieces):
        for start in range(0, piece.shape[0], most):
            rows = min(most, piece.shape[0] - start)
            yield [(index, start, rows)], pl.multiple_of(offs[first + index] + start, 256), rows


def load_chunk(move, pieces, sources, column, target, at):
    copies = []
    for index, start, rows in sources:
        source = pieces[index].at[pl.ds(start, rows), pl.ds(column, target.shape[1])]
        copies.append(move.start(source, target.at[pl.ds(at, rows), :]))
        at += rows
    return copies


def feed_down_kernel(count, column, entries, offs, bias, y_hbm, m_hbm, *rest):
    pieces, (h_hbm, low_hbm, y_ref, total, h_low, down, sems) = rest[:count], rest[count:]
    move = Copies(sems)
    m_copy = move.start(m_hbm, total)
    parts = []
    at = 0
    for sources, row, rows in chunks(pieces, offs, 1, entries):
        copies = [move.start(y_hbm.at[:, pl.ds(row, rows)], y_ref.at[:, pl.ds(at, rows)])]
        copies += load_chunk(move, pieces, sources, column, down, at)
        parts.append((at, rows, copies))
        at += rows
    m_copy.wait()
    total[...] += bias[...]
    for at, rows, copies in parts:
        wait_all(copies)
        total[...] += dot(y_ref[:, pl.ds(at, rows)], down[pl.ds(at, rows), :])
    move.send(total, h_hbm)
    h_low[...] = total[...].astype(low)
    move.send(h_low, low_hbm)
    move.finish()


def feed_down(offs, acted, middle, bias, pieces):
    pieces, column = pieces
    tokens, hidden = acted.shape
    model = middle.shape[1]
    count = len(pieces)
    return call(
        functools.partial(feed_down_kernel, count, column, offs.shape[0] - 1),
        "feed_down",
        [sized(full, tokens, model), sized(low, tokens, model)],
        [offs],
        [bias],
        [acted, middle, *pieces],
        [
            ((tokens, hidden), low),
            ((tokens, model), full),
            ((tokens, model), low),
            ((hidden, model), low),
        ],
        64,
    )


def feed_back_kernel(entries, ups, downs, outs_count, columns, groups, offs, gain, g_hbm, m_hbm, slope_hbm, *rest):
    up_pieces, rest = rest[:ups], rest[ups:]
    down_pieces, rest = rest[:downs], rest[downs:]
    out_pieces, rest = rest[:outs_count], rest[outs_count:]
    mid_hbm, rest = rest[0], rest[1:]
    outs, rest = rest[:groups], rest[groups:]
    g_ref, m_ref, slope, up, down, out, d_pre, d_second, mixed, sems = rest
    move = Copies(sems)
    g_copy = move.start(g_hbm, g_ref)
    parts = []
    at = 0
    for sources, row, rows in chunks(down_pieces, offs, 1 + ups, entries):
        cols, where = pl.ds(row, rows), pl.ds(at, rows)
        copies = load_chunk(move, down_pieces, sources, columns[1], down, at)
        copies.append(move.start(slope_hbm.at[:, cols], slope.at[:, where]))
        parts.append((where, cols, copies))
        at += rows
    up_loads = move.rows(up_pieces, columns[0], offs, 1, up)[0]
    m_copy = move.start(m_hbm, m_ref)
    out_loads = move.rows(out_pieces, columns[2], offs, 1 + ups + entries, out)[0]
    model = up.shape[0]
    g_copy.wait()
    g = g_ref[...].astype(low)
    for where, cols, copies in parts:
        wait_all(copies)
        d_acted = dot_nt(g, down[where, :])
        d_pre[:, cols] = (d_acted * slope[:, where].astype(full)).astype(low)
    wait_all(up_loads)
    step = 256
    for start in range(0, model, step):
        cols = pl.ds(start, step)
        d_second[:, cols] = dot_nt(d_pre[...], up[cols, :])
    m_copy.wait()
    unit, scale = normalise(m_ref[...])
    grad = g_ref[...].astype(full) + norm_back(unit, scale, gain[...], d_second[...])
    m_ref[...] = grad
    move.send(m_ref, mid_hbm)
    grad = grad.astype(low)
    wait_all(out_loads)
    width = model // groups
    for group in range(groups):
        cols = pl.ds(group * width, width)
        mixed[:, cols] = dot_nt(grad, out[cols, :]).astype(low)
    for step in range(groups):
        at = pl.multiple_of((offs[0] ^ step) * width, width)
        move.send(mixed.at[:, pl.ds(at, width)], outs[step])
    move.finish()


def feed_back(offs, grad, middle, slope, gain, up_pieces, down_pieces, out_pieces, groups):
    (up_pieces, up_column), (down_pieces, down_column) = up_pieces, down_pieces
    out_pieces, out_column = out_pieces
    columns = (up_column, down_column, out_column)
    tokens, model = middle.shape
    hidden = slope.shape[1]
    ups, downs, outs_count = len(up_pieces), len(down_pieces), len(out_pieces)
    result = call(
        functools.partial(feed_back_kernel, offs.shape[0] - 1 - ups - outs_count, ups, downs, outs_count, columns, groups),
        "feed_back",
        [sized(full, tokens, model)] + [sized(low, tokens, model // groups)] * groups,
        [offs],
        [gain],
        [grad, middle, slope, *up_pieces, *down_pieces, *out_pieces],
        [
            ((tokens, model), grad.dtype),
            ((tokens, model), full),
            ((tokens, hidden), low),
            ((model, hidden), low),
            ((hidden, model), low),
            ((model, model), low),
            ((tokens, hidden), low),
            ((tokens, model), full),
            ((tokens, model), low),
        ],
        96,
    )
    return result[0], result[1:]


def adapt_back_kernel(groups, rank, offs, up, a_hbm, u_hbm, *rest):
    grads, rest = rest[:groups], rest[groups:]
    grad_a_hbm, grad_b_hbm, d_inner_hbm, a_ref, u_ref, d_pair, d_inner, grad_a, grad_b, sems = rest
    move = Copies(sems)
    model = a_ref.shape[1]
    width = model // groups
    loads = [move.start(u_hbm, u_ref)]
    for place, kind in enumerate((0, 2)):
        for step in range(groups):
            at = pl.multiple_of(place * model + (offs[0] ^ step) * width, width)
            source = grads[step].at[:, pl.ds(kind * width, width)]
            loads.append(move.start(source, d_pair.at[:, pl.ds(at, width)]))
    a_copy = move.start(a_hbm, a_ref)
    wait_all(loads)
    d_inner[...] = dot_nt(d_pair[...], up[...]).astype(low)
    move.send(d_inner, d_inner_hbm)
    u = u_ref[...]
    lane = lax.broadcasted_iota(jnp.int32, (1, LANES), 1)
    u_query = jnp.where(lane < rank, u, 0).astype(low)
    u_value = jnp.where(lane >= rank, u, 0).astype(low)
    by_rank = dot_tn(u_query, d_pair[:, pl.ds(0, model)]) + dot_tn(u_value, d_pair[:, pl.ds(model, model)])
    grad_b[...] = adapter_scale * by_rank[:8]
    move.send(grad_b, grad_b_hbm)
    a_copy.wait()
    grad_a[...] = dot_tn(d_inner[...], a_ref[...])[:8]
    move.send(grad_a, grad_a_hbm)
    move.finish()


def adapt_back(normed, inner, up, grads, offs, rank):
    groups = len(grads)
    tokens, model = normed.shape
    return call(
        functools.partial(adapt_back_kernel, groups, rank),
        "adapt_back",
        [sized(full, 8, model), sized(full, 8, model), sized(low, tokens, LANES)],
        [offs],
        [up],
        [normed, inner, *grads],
        [
            ((tokens, model), low),
            ((tokens, LANES), low),
            ((tokens, 2 * model), low),
            ((tokens, LANES), low),
            ((8, model), full),
            ((8, model), full),
        ],
        2 + 2 * groups + 3,
    )


def project_back_kernel(count, column, groups, half, offs, gain, down, inner_hbm, mid_hbm, h_hbm, *rest):
    grads, pieces, rest = rest[:groups], rest[groups : groups + count], rest[groups + count :]
    outs, rest = rest[:1], rest[1:]
    d_inner, mid_ref, h_ref, weight, d_all, d_normed, g_low, sems = rest
    move = Copies(sems)
    tokens, model = h_ref.shape
    width = model // groups
    at = pl.multiple_of(offs[1 + count] * tokens, tokens) if half else 0
    mine = pl.ds(at, tokens)
    loads = [move.start(inner_hbm.at[mine, :], d_inner)]
    for kind in range(3):
        for step in range(groups):
            to = pl.multiple_of(kind * model + (offs[0] ^ step) * width, width)
            source = grads[step].at[mine, pl.ds(kind * width, width)]
            loads.append(move.start(source, d_all.at[:, pl.ds(to, width)]))
    weights = move.rows(pieces, column, offs, 1, weight)[0]
    later = [move.start(h_hbm.at[mine, :], h_ref), move.start(mid_hbm.at[mine, :], mid_ref)]
    wait_all(loads)
    wait_all(weights)
    step = 256
    for start in range(0, model, step):
        cols = pl.ds(start, step)
        d_normed[:, cols] = dot_nt(d_all[...], weight[cols, :])
    wait_all(later)
    unit, scale = normalise(h_ref[...].astype(full))
    through = d_normed[...] + dot_nt(d_inner[...], down[...])
    grad = mid_ref[...] + norm_back(unit, scale, gain[...], through)
    g_low[...] = grad.astype(low)
    if half:
        move.send(g_low, outs[0])
    else:
        mid_ref[...] = grad
        move.send(mid_ref, outs[0])
    move.finish()


def project_back(offs, mid, hidden, gain, d_inner, down, grads, pieces, half=False):
    pieces, column = pieces
    groups, count = len(grads), len(pieces)
    tokens, model = hidden.shape
    if half:
        tokens = tokens // 2
    return call(
        functools.partial(project_back_kernel, count, column, groups, half),
        "project_back",
        [sized(low, tokens, model)] if half else [sized(full, tokens, model)],
        [offs],
        [gain, down],
        [d_inner, mid, hidden, *grads, *pieces],
        [
            ((tokens, LANES), low),
            ((tokens, model), full),
            ((tokens, model), hidden.dtype),
            ((model, 3 * model), low),
            ((tokens, 3 * model), low),
            ((tokens, model), full),
            ((tokens, model), low),
        ],
        1 + 3 * groups + count + 2 + 2,
    )[0]


def between_back_kernel(
    qkvs, ups, downs, outs_count, entries, columns, groups, offs, gain, earlier_gain, down_map,
    inner_hbm, mid_hbm, h_hbm, m_hbm, slope_hbm, *rest
):
    grads, rest = rest[:groups], rest[groups:]
    qkv_pieces, rest = rest[:qkvs], rest[qkvs:]
    up_pieces, rest = rest[:ups], rest[ups:]
    down_pieces, rest = rest[:downs], rest[downs:]
    out_pieces, rest = rest[:outs_count], rest[outs_count:]
    mid_out, rest = rest[0], rest[1:]
    outs, rest = rest[:groups], rest[groups:]
    d_inner, g_ref, h_ref, m_ref, qkv, d_all, slope, up, down, out, d_pre, d_second, mixed, sems = rest
    move = Copies(sems)
    tokens, model = h_ref.shape
    width = model // groups
    loads = [move.start(inner_hbm, d_inner)]
    for kind in range(3):
        for step in range(groups):
            to = pl.multiple_of(kind * model + (offs[0] ^ step) * width, width)
            source = grads[step].at[:, pl.ds(kind * width, width)]
            loads.append(move.start(source, d_all.at[:, pl.ds(to, width)]))
    loads += move.rows(qkv_pieces, columns[3], offs, 1, qkv)[0]
    later = [move.start(h_hbm, h_ref), move.start(mid_hbm, g_ref)]
    parts = []
    at = 0
    first = 1 + qkvs
    for sources, row, rows in chunks(down_pieces, offs, first + ups, entries):
        cols, where = pl.ds(row, rows), pl.ds(at, rows)
        copies = load_chunk(move, down_pieces, sources, columns[1], down, at)
        copies.append(move.start(slope_hbm.at[:, cols], slope.at[:, where]))
        parts.append((where, cols, copies))
        at += rows
    up_loads = move.rows(up_pieces, columns[0], offs, first, up)[0]
    m_copy = move.start(m_hbm, m_ref)
    out_loads = move.rows(out_pieces, columns[2], offs, first + ups + entries, out)[0]
    wait_all(loads)
    step = 256
    for start in range(0, model, step):
        cols = pl.ds(start, step)
        d_second[:, cols] = dot_nt(d_all[...], qkv[cols, :])
    wait_all(later)
    unit, scale = normalise(h_ref[...])
    through = d_second[...] + dot_nt(d_inner[...], down_map[...])
    g_ref[...] = g_ref[...] + norm_back(unit, scale, gain[...], through)
    g = g_ref[...].astype(low)
    for where, cols, copies in parts:
        wait_all(copies)
        d_acted = dot_nt(g, down[where, :])
        d_pre[:, cols] = (d_acted * slope[:, where].astype(full)).astype(low)
    wait_all(up_loads)
    for start in range(0, model, step):
        cols = pl.ds(start, step)
        d_second[:, cols] = dot_nt(d_pre[...], up[cols, :])
    m_copy.wait()
    unit, scale = normalise(m_ref[...])
    grad = g_ref[...] + norm_back(unit, scale, earlier_gain[...], d_second[...])
    m_ref[...] = grad
    move.send(m_ref, mid_out)
    grad = grad.astype(low)
    wait_all(out_loads)
    for group in range(groups):
        cols = pl.ds(group * width, width)
        mixed[:, cols] = dot_nt(grad, out[cols, :]).astype(low)
    for step in range(groups):
        at = pl.multiple_of((offs[0] ^ step) * width, width)
        move.send(mixed.at[:, pl.ds(at, width)], outs[step])
    move.finish()


def between_back(
    offs, entries, mid, hidden, gain, d_inner, down_map, grads, qkv_pieces,
    middle, slope, earlier_gain, up_pieces, down_pieces, out_pieces
):
    (qkv_pieces, qkv_column), (up_pieces, up_column) = qkv_pieces, up_pieces
    (down_pieces, down_column), (out_pieces, out_column) = down_pieces, out_pieces
    columns = (up_column, down_column, out_column, qkv_column)
    tokens, model = middle.shape
    hidden_width, groups = slope.shape[1], len(grads)
    counts = [len(p) for p in (qkv_pieces, up_pieces, down_pieces, out_pieces)]
    result = call(
        functools.partial(between_back_kernel, *counts, entries, columns, groups),
        "between_back",
        [sized(full, tokens, model)] + [sized(low, tokens, model // groups)] * groups,
        [offs],
        [gain, earlier_gain, down_map],
        [d_inner, mid, hidden, middle, slope, *grads]
        + [*qkv_pieces, *up_pieces, *down_pieces, *out_pieces],
        [
            ((tokens, LANES), low),
            ((tokens, model), full),
            ((tokens, model), full),
            ((tokens, model), full),
            ((model, 3 * model), low),
            ((tokens, 3 * model), low),
            ((tokens, hidden_width), low),
            ((model, hidden_width), low),
            ((hidden_width, model), low),
            ((model, model), low),
            ((tokens, hidden_width), low),
            ((tokens, model), full),
            ((tokens, model), low),
        ],
        128,
    )
    return result[0], result[1:]


BLOCK = 256


def causal_corner(block):
    keys = lax.broadcasted_iota(jnp.int32, (block, block), 0)
    return keys <= lax.broadcasted_iota(jnp.int32, (block, block), 1)


def head_masks():
    lane = lax.broadcasted_iota(jnp.int32, (1, LANES), 1)
    return [(lane < HEAD).astype(low), (lane >= HEAD).astype(low)]


def attend_kernel(groups, offs, *rest):
    pieces, rest = rest[:groups], rest[groups:]
    outs, (o_hbm, lse_hbm), rest = rest[:groups], rest[groups : groups + 2], rest[groups + 2 :]
    qkv, v_turned, o_turned, o_ref, lse, sems = rest
    move = Copies(sems)
    member = offs[0]
    count, width3 = pieces[0].shape
    width = width3 // 3
    length = count * groups
    pairs = width // LANES
    block = min(BLOCK, length)
    places = [
        pl.ds(pl.multiple_of((member ^ step) * count, count), count) for step in range(groups)
    ]
    loads = []
    for pair in range(pairs):
        row = []
        for kind in (2, 1, 0):
            cols = pl.ds(kind * width + pair * LANES, LANES)
            for step in range(groups):
                row.append(move.start(pieces[step].at[:, cols], qkv.at[places[step], cols]))
        loads.append(row)
    keep = head_masks()
    causal = causal_corner(block)
    if lse.shape[0] > 2 * pairs:
        lse[...] = jnp.zeros_like(lse)
    for pair in range(pairs):
        at = pair * LANES
        here = pl.ds(at, LANES)
        wait_all(loads[pair])
        v_turned[...] = qkv[:, pl.ds(2 * width + at, LANES)].T
        for start in range(0, length, block):
            rows = pl.ds(start, block)
            upto = start + block
            q = qkv[rows, here]
            k = qkv[pl.ds(0, upto), pl.ds(width + at, LANES)]
            scores = [dot_nt(k, q * (keep[head] * 0.125)) for head in range(2)]
            for head in range(2):
                where = pl.ds(head * HEAD, HEAD)
                value = scores[head]
                corner = jnp.where(causal, value[start:], -1e30)
                value = jnp.concatenate([value[:start], corner], axis=0) if start else corner
                top = jnp.max(value, axis=0, keepdims=True)
                weights = jnp.exp(value - top)
                total = jnp.sum(weights, axis=0, keepdims=True)
                mixed = dot(v_turned[where, pl.ds(0, upto)], weights.astype(low))
                o_turned[where, rows] = (mixed * (1.0 / total)).astype(low)
                lse[pl.ds(2 * pair + head, 1), rows] = top + jnp.log(total)
        o_ref[:, here] = o_turned[...].T
        move.send(o_ref.at[:, here], o_hbm.at[:, here])
        for step in range(groups):
            move.send(o_ref.at[places[step], here], outs[step].at[:, here])
    move.send(lse, lse_hbm)
    move.finish()


def attend(offs, pieces):
    groups = len(pieces)
    count, width3 = pieces[0].shape
    width, length = width3 // 3, count * groups
    heads = max(8, width // HEAD)
    pairs = width // LANES
    result = call(
        functools.partial(attend_kernel, groups),
        "attend",
        [sized(low, count, width)] * groups + [sized(low, length, width), sized(full, heads, length)],
        [offs],
        [],
        pieces,
        [
            ((length, width3), low),
            ((LANES, length), low),
            ((LANES, length), low),
            ((length, width), low),
            ((heads, length), full),
        ],
        pairs * (4 * groups + 1) + 1,
    )
    return result[:groups], result[groups], result[groups + 1]


def attend_back_kernel(groups, offs, o_hbm, lse_hbm, *rest):
    pieces, grads, rest = rest[:groups], rest[groups : 2 * groups], rest[2 * groups :]
    outs, rest = rest[:groups], rest[groups:]
    qkv, d_out, o_ref, lse, k_turned, q_turned, result, inner, sum_k, sum_v, sems = rest
    move = Copies(sems)
    member = offs[0]
    count, width3 = pieces[0].shape
    width = width3 // 3
    length = count * groups
    pairs = width // LANES
    block = min(BLOCK, length)
    places = [
        pl.ds(pl.multiple_of((member ^ step) * count, count), count) for step in range(groups)
    ]
    first = [move.start(grads[step], d_out.at[places[step], :]) for step in range(groups)]
    first.append(move.start(o_hbm, o_ref))
    loads = []
    for kind in (1, 0, 2):
        cols = pl.ds(kind * width, width)
        loads.append(
            [move.start(pieces[i].at[:, cols], qkv.at[places[i], cols]) for i in range(groups)]
        )
    lse_copy = move.start(lse_hbm, lse)
    keep = head_masks()
    causal = causal_corner(block)
    heads = lse.shape[0]
    of_head = (
        lax.broadcasted_iota(jnp.int32, (heads, width), 1) // HEAD
        == lax.broadcasted_iota(jnp.int32, (heads, width), 0)
    ).astype(low)
    wait_all(first)
    product = d_out[...].astype(full) * o_ref[...].astype(full)
    high = product.astype(low)
    rest_of = (product - high.astype(full)).astype(low)
    inner[...] = dot_nt(of_head, high) + dot_nt(of_head, rest_of)
    wait_all(loads[0])
    k_turned[...] = qkv[:, pl.ds(width, width)].T
    wait_all(loads[1])
    wait_all(loads[2])
    lse_copy.wait()

    def pair_step(pair):
        at = pair * LANES
        for start in reversed(range(0, length, block)):
            rows = pl.ds(start, block)
            upto = start + block
            past = pl.ds(0, upto)
            q = qkv[rows, pl.ds(at, LANES)]
            d = d_out[rows, pl.ds(at, LANES)]
            k = qkv[past, pl.ds(width + at, LANES)]
            v = qkv[past, pl.ds(2 * width + at, LANES)]
            q_heads = [q * (keep[head] * 0.125) for head in range(2)]
            d_heads = [d * keep[head] for head in range(2)]
            scores = [dot_nt(k, q_heads[head]) for head in range(2)]
            d_probs = [dot_nt(v, d_heads[head]) for head in range(2)]
            more_k = more_v = None
            for head in range(2):
                line = pl.ds(2 * pair + head, 1)
                probs = jnp.exp(scores[head] - lse[line, rows])
                corner = jnp.where(causal, probs[start:], 0.0)
                probs = jnp.concatenate([probs[:start], corner], axis=0) if start else corner
                d_scores = (probs * (d_probs[head] - inner[line, rows])).astype(low)
                part_v = dot(probs.astype(low), d_heads[head])
                part_k = dot(d_scores, q_heads[head])
                more_v = part_v if more_v is None else more_v + part_v
                more_k = part_k if more_k is None else more_k + part_k
                where = pl.ds(at + head * HEAD, HEAD)
                q_turned[where, rows] = (0.125 * dot(k_turned[where, past], d_scores)).astype(low)
            if upto == length:
                sum_v[...] = more_v
                sum_k[...] = more_k
            else:
                sum_v[past, :] += more_v
                sum_k[past, :] += more_k
        result[:, pl.ds(width + at, LANES)] = sum_k[...].astype(low)
        result[:, pl.ds(2 * width + at, LANES)] = sum_v[...].astype(low)

    for pair in range(pairs):
        pair_step(pair)
    result[:, pl.ds(0, width)] = q_turned[...].T
    for step in range(groups):
        move.send(result.at[places[step], :], outs[step])
    move.finish()


def attend_back(offs, pieces, grads, mixed, lse):
    groups = len(pieces)
    count, width3 = pieces[0].shape
    width, length = width3 // 3, count * groups
    heads = lse.shape[0]
    return call(
        functools.partial(attend_back_kernel, groups),
        "attend_back",
        [sized(low, count, width3)] * groups,
        [offs],
        [],
        [mixed, lse, *pieces, *grads],
        [
            ((length, width3), low),
            ((length, width), low),
            ((length, width), low),
            ((heads, length), full),
            ((width, length), low),
            ((width, length), low),
            ((length, width3), low),
            ((heads, length), full),
            ((length, LANES), full),
            ((length, LANES), full),
        ],
        5 * groups + 2,
    )


def reshard_perms(sp_size, dp_size):
    quarter = sp_size // 4
    perms = []
    for part in range(2):
        perm = []
        for s in range(sp_size):
            for d in range(dp_size):
                doc = 2 * (d & 1) + ((s & 1) ^ part)
                member = s >> 1
                target_sp = doc * quarter + (member >> 1)
                target_dp = 2 * (d >> 1) + (member & 1)
                perm.append((s * dp_size + d, target_sp * dp_size + target_dp))
        perms.append(perm)
    return perms


def member_perm(sp_size, dp_size, step):
    quarter = sp_size // 4
    perm = []
    for s in range(sp_size):
        for d in range(dp_size):
            doc, high = s // quarter, s % quarter
            member = (2 * high + (d & 1)) ^ step
            target_sp = doc * quarter + (member >> 1)
            target_dp = 2 * (d >> 1) + (member & 1)
            perm.append((s * dp_size + d, target_sp * dp_size + target_dp))
    return perm


class Plan:
    def __init__(self, sp_size, dp_size):
        self.sp_size, self.dp_size = sp_size, dp_size
        self.members = sp_size // 2
        self.perms = reshard_perms(sp_size, dp_size)
        self.back = [[(b, a) for a, b in perm] for perm in self.perms]
        self.s = lax.axis_index("sp")
        self.d = lax.axis_index("dp")
        quarter = sp_size // 4
        self.doc = self.s // quarter
        self.member = 2 * (self.s % quarter) + (self.d & 1)

    def gather_start(self, blocks):
        got = []
        for part in range(2):
            block = lax.dynamic_index_in_dim(blocks, (self.s & 1) ^ part, 0, keepdims=False)
            got.append(lax.ppermute(block, ("sp", "dp"), self.perms[part]))
        return got

    def gather_finish(self, got):
        flip = (self.doc & 1) == 1
        first = jnp.where(flip, got[1], got[0])
        second = jnp.where(flip, got[0], got[1])
        return jnp.concatenate([first, second], axis=0)

    def gather_doc(self, blocks):
        return self.gather_finish(self.gather_start(blocks))

    def scatter_start(self, rows):
        half = rows.shape[0] // 2
        blocks = rows.reshape(2, half, rows.shape[1])
        got = []
        for part in range(2):
            block = lax.dynamic_index_in_dim(blocks, (self.doc & 1) ^ part, 0, keepdims=False)
            got.append(lax.ppermute(block, ("sp", "dp"), self.back[part]))
        return got

    def scatter_finish(self, got):
        flip = (self.s & 1) == 1
        first = jnp.where(flip, got[1], got[0])
        second = jnp.where(flip, got[0], got[1])
        return jnp.stack([first, second])

    def scatter_doc(self, rows):
        return self.scatter_finish(self.scatter_start(rows))

    def swap(self, parts):
        out = [parts[0]]
        for step in range(1, self.members):
            perm = member_perm(self.sp_size, self.dp_size, step)
            out.append(lax.ppermute(parts[step], ("sp", "dp"), perm))
        return out


def add_from(value, step, total):
    return value + lax.ppermute(value, ("sp", "dp"), [(i, i ^ step) for i in range(total)])


def after(value, *earlier):
    return lax.optimization_barrier((value, *earlier))[0]


class Clock:
    def __init__(self):
        self.event = ()

    def tick(self, *values):
        self.event = values

    def tied(self, *values):
        if not self.event:
            return values if len(values) > 1 else values[0]
        got = lax.optimization_barrier((*values, *self.event))[: len(values)]
        return got if len(values) > 1 else got[0]


class Fetch:
    def __init__(self, plan, clock, shard):
        self.plan, self.clock = plan, clock
        self.whole = plan.sp_size != 4
        shard = clock.tied(shard)
        if self.whole:
            self.block = lax.all_gather(shard, ("sp", "dp"), axis=0, tiled=True)
            self.side = self.corner = self.block
            return
        self.block = lax.all_gather(shard, "dp", axis=0, tiled=True)
        sp_size, dp_size = plan.sp_size, plan.dp_size
        self.over_core = [(i, i ^ 1) for i in range(dp_size)]
        places = [(s, d) for s in range(sp_size) for d in range(dp_size)]
        self.first_way = [(s * dp_size + d, (s ^ (1 << (d & 1))) * dp_size + d) for s, d in places]
        self.second_way = [(s * dp_size + d, (s ^ (2 >> (d & 1))) * dp_size + d) for s, d in places]

    def split(self, columns):
        both = []
        for cols in (slice(None, columns), slice(columns, None)):
            part = object.__new__(Fetch)
            part.__dict__.update(self.__dict__)
            part.block = self.block[:, cols]
            if self.whole:
                part.side = part.corner = part.block
            both.append(part)
        return both

    def near(self):
        if not self.whole:
            block = self.clock.tied(self.block)
            self.side = lax.ppermute(block, ("sp", "dp"), self.first_way)

    def far(self):
        if self.whole:
            return
        rows = self.block.shape[0]
        self.side = self.clock.tied(self.side)
        half = lax.dynamic_slice_in_dim(self.side, (self.plan.d & 1) * (rows // 2), rows // 2, axis=0)
        self.corner = lax.ppermute(half, ("sp", "dp"), self.second_way)
        self.other_side = lax.ppermute(self.side, "dp", self.over_core)

    def pieces(self):
        plan = self.plan
        if self.whole:
            return [self.block], [0]
        corner = self.clock.tied(self.corner)
        other_corner = lax.ppermute(corner, "dp", self.over_core)
        rows = self.block.shape[0]
        s, core = plan.s, plan.d & 1
        half = rows // 2
        starts = [
            s * rows,
            (s ^ (1 << core)) * rows,
            (s ^ (2 >> core)) * rows,
            (s ^ 3) * rows + core * half,
            (s ^ 3) * rows + (1 - core) * half,
        ]
        return [self.block, self.side, self.other_side, corner, other_corner], starts


class Wide:
    def __init__(self, plan, clock, shard):
        self.plan, self.clock = plan, clock
        self.whole = plan.sp_size != 4
        shard = clock.tied(shard)
        self.parts = [shard]
        if not self.whole:
            for step in range(1, 4):
                way = [(i, i ^ step) for i in range(4)]
                self.parts.append(lax.ppermute(shard, "sp", way))

    def gather(self):
        parts = self.clock.tied(*self.parts) if len(self.parts) > 1 else self.parts
        axes = ("sp", "dp") if self.whole else "dp"
        self.block = lax.all_gather(jnp.concatenate(parts), axes, axis=0, tiled=True)

    def pieces(self):
        if self.whole:
            return [self.block], [0]
        rows = self.block.shape[0] // 4
        return [self.block], [(self.plan.s ^ step) * rows for step in range(4)]


def on_device(
    tokens,
    cotangent,
    layer_norm_gain,
    layer_norm_bias,
    query_key_value_weight,
    query_value_bias,
    attention_out_weight,
    output_projection_bias,
    feed_up_weight,
    feed_up_bias,
    feed_down_weight,
    adapter_down_maps,
    adapter_up_weights,
):
    layers = query_key_value_weight.shape[0]
    model = tokens.shape[2]
    rank = adapter_down_maps.shape[3]
    plan = Plan(lax.axis_size("sp"), lax.axis_size("dp"))
    clock = Clock()
    groups = plan.members
    member = plan.member.astype(jnp.int32)

    def table(*entries):
        return jnp.stack([jnp.asarray(entry, jnp.int32) for entry in entries])

    adapters = []
    for layer in range(layers):
        down = jnp.concatenate([adapter_down_maps[layer, 0], adapter_down_maps[layer, 1]], axis=1)
        down = jnp.pad(down, ((0, 0), (0, LANES - 2 * rank)))
        up = adapter_up_weights[layer] * jnp.asarray(adapter_scale, low)
        up = jnp.concatenate(
            [
                jnp.pad(up[0], ((0, LANES - rank), (0, 0))),
                jnp.pad(up[1], ((rank, LANES - 2 * rank), (0, 0))),
            ],
            axis=1,
        )
        adapters.append((down, up))

    def request(layer, *kinds):
        shards = []
        for kind in kinds:
            if kind == 0:
                shards.append(query_key_value_weight[layer])
            elif kind == 1:
                shards += [attention_out_weight[layer], feed_up_weight[layer]]
            else:
                shards.append(feed_down_weight[layer])
        shard = jnp.concatenate(shards, axis=1) if len(shards) > 1 else shards[0]
        return Fetch(plan, clock, shard)

    saved, outputs = [], []
    ready = {}
    qkv_fetch = request(0, 0)
    wide = Wide(plan, clock, feed_down_weight[layers - 1])
    sent = plan.gather_start(tokens)
    clock.tick(*wide.parts, *sent)
    hidden = plan.gather_finish(clock.tied(*sent))
    clock.tick(hidden)
    out_fetch = request(0, 1)
    down_fetch = request(0, 2)
    clock.tick(*wide.parts)
    qkv_fetch.near()
    clock.tick(hidden)
    qkv_fetch.far()
    clock.tick(qkv_fetch.side)
    out_fetch.near()
    for layer in range(layers):
        last = layer + 1 == layers
        gain, shift = layer_norm_gain[layer], layer_norm_bias[layer]
        down, up = adapters[layer]
        clock.tick(hidden, qkv_fetch.corner)
        ready[layer, 0] = qkv_fetch.pieces()
        if not last:
            following = request(layer + 1, 0, 1)
        qkv, starts = ready[layer, 0]
        offs = table(member, *starts)
        bias = query_value_bias[layer].reshape(1, 2 * model)
        clock.tick(out_fetch.block)
        parts, inner, normed = project(
            offs, clock.tied(hidden), gain[:1], shift[:1], bias, down, up, (qkv, 0), groups
        )
        clock.tick(*parts)
        out_fetch.far()
        if not last:
            clock.tick(out_fetch.side, *parts)
            if layer + 2 == layers:
                wide.gather()
                next_down = wide
            else:
                next_down = request(layer + 1, 2)
        parts = plan.swap(parts)
        clock.tick(out_fetch.side)
        if not last:
            down_fetch.near()
        parts[0] = clock.tied(parts[0])
        mixed_parts, mixed, lse = attend(offs, parts)
        clock.tick(mixed)
        mixed_parts = plan.swap(mixed_parts)
        clock.tick(mixed, out_fetch.corner)
        ready[layer, 1] = out_fetch.pieces()
        out_up, starts = ready[layer, 1]
        if not last:
            clock.tick(down_fetch.side)
            mixed_parts[0] = clock.tied(mixed_parts[0])
        offs = table(member, *starts)
        middle, second = mix(
            offs,
            hidden,
            output_projection_bias[layer, :1],
            gain[1:],
            shift[1:],
            mixed_parts,
            (out_up, 0),
        )
        if not last:
            down_fetch.far()
            clock.tick(down_fetch.side)
            next_qkv, next_out = following.split(3 * model)
            next_qkv.near()
            clock.tick(next_qkv.block)
        acted, slope = feed_up(
            offs, clock.tied(second), feed_up_bias[layer : layer + 1], (out_up, model)
        )
        clock.tick(acted)
        if last:
            sent = clock.tied(*plan.gather_start(after(cotangent, second)))
            grad = plan.gather_finish(sent)
        else:
            next_out.near()
            clock.tick(acted, down_fetch.corner)
        ready[layer, 2] = down_fetch.pieces()
        saved.append((hidden, normed, inner, parts, mixed, lse, middle, acted, slope))
        down_w, starts = ready[layer, 2]
        if not last:
            clock.tick(next_out.block)
            hidden, after_low = feed_down(
                table(member, *starts),
                clock.tied(acted),
                middle,
                output_projection_bias[layer, 1:],
                (down_w, 0),
            )
            clock.tick(hidden)
            next_qkv.far()
            outputs.append(plan.scatter_start(after_low))
            qkv_fetch, out_fetch, down_fetch = next_qkv, next_out, next_down
    sums = [None] * layers
    waiting = outputs.pop()
    for layer in reversed(range(layers)):
        hidden, normed, inner, parts, mixed, lse, middle, acted, slope = saved[layer]
        gain = layer_norm_gain[layer]
        down, up = adapters[layer]
        (qkv, starts), (out_up, starts_up) = ready[layer, 0], ready[layer, 1]
        down_w, starts_down = ready[layer, 2]
        offs = table(member, *starts)
        if layer + 1 < layers:
            later_qkv, later_starts = ready[layer + 1, 0]
            mid, d_mixed = between_back(
                table(member, *later_starts, *starts_up, *starts_down, *starts_up),
                len(starts_down),
                mid,
                saved[layer + 1][0],
                layer_norm_gain[layer + 1, :1],
                d_inner,
                adapters[layer + 1][0],
                grads,
                (later_qkv, 0),
                middle,
                slope,
                gain[1:],
                (out_up, model),
                (down_w, 0),
                (out_up, 0),
            )
        else:
            mid, d_mixed = feed_back(
                table(member, *starts_up, *starts_down, *starts_up),
                grad,
                middle,
                slope,
                gain[1:],
                (out_up, model),
                (down_w, 0),
                (out_up, 0),
                groups,
            )
        d_mixed = plan.swap(d_mixed)
        if layer + 1 == layers:
            _, after_low = feed_down(
                table(member, *starts_down),
                after(acted, mid),
                middle,
                output_projection_bias[layer, 1:],
                (down_w, 0),
            )
            outputs_late = [plan.scatter_start(after_low)]
            d_mixed[0] = after(d_mixed[0], after_low)
        grads = list(attend_back(offs, parts, d_mixed, mixed, lse))
        if waiting:
            grads[1], *arrived = lax.optimization_barrier((grads[1], *waiting))
            outputs.append(arrived)
        if outputs_late:
            waiting = outputs_late.pop()
        else:
            waiting = []
        grads = plan.swap(grads)
        grad_a, grad_b, d_inner = adapt_back(normed, inner, up, grads, offs, rank)
        sums[layer] = jnp.concatenate([grad_a, grad_b])
        if layer:
            d_inner = after(d_inner, grad_a)
    total = jnp.stack(sums)
    flat = plan.sp_size * plan.dp_size
    bits = [1 << bit for bit in range(flat.bit_length() - 1)]
    steps = [1] + [bit for bit in bits if bit >= plan.dp_size]
    steps += [bit for bit in bits if 1 < bit < plan.dp_size]
    for step in steps[:1]:
        total = add_from(total, step, flat)
    sent = []
    for half in range(2):
        if half + 1 < len(steps):
            total = add_from(total, steps[half + 1], flat)
        which = (plan.doc & 1) ^ half
        back = project_back(
            table(member, *starts, which),
            mid,
            hidden,
            gain[:1],
            d_inner,
            down,
            grads,
            (qkv, 0),
            half=True,
        )
        total, back = lax.optimization_barrier((total, back))
        sent.append(lax.ppermute(back, ("sp", "dp"), plan.back[half]))
        d_inner = after(d_inner, back)
    for step in steps[3:]:
        total = add_from(total, step, flat)
    grad_tokens = plan.scatter_finish(sent).astype(full)
    total = total.reshape(layers, 2, 8, model)[:, :, : 2 * rank]
    total = total.reshape(layers, 2, 2, rank, model)
    outputs = [plan.scatter_finish(got).astype(full) for got in outputs]
    return (jnp.stack(outputs), grad_tokens, total[:, 0].swapaxes(-1, -2), total[:, 1])


def solution(mesh):
    in_specs = (
        P("dp", "sp", None),
        P("dp", "sp", None),
        P(),
        P(),
        P(None, ("sp", "dp"), None),
        P(),
        P(None, ("sp", "dp"), None),
        P(),
        P(None, ("sp", "dp"), None),
        P(),
        P(None, ("sp", "dp"), None),
        P(),
        P(),
    )
    out_specs = (P(None, "dp", "sp", None), P("dp", "sp", None), P(), P())
    return jax.shard_map(
        on_device, mesh=mesh, in_specs=in_specs, out_specs=out_specs, check_vma=False
    )
```
